512 devices in a mesh: grp: 4 (over x), comp: 128 (over y, z, core).
Axes of the slice: x: 4, y: 8, z: 8, core: 2. Of those that a mesh axis runs over, the one named last changes fastest.
Arguments:
- spectra: float32 [600, 196608], P('grp', 'comp'), may hold values from 0.05 to 2
- wind_speed: float32 [196608], P('comp'), may hold values from 4 to 24
- wind_dir: float32 [196608], P('comp'), may hold values from -3.140625 to 3.140625
- sea_cell: int32 [196608], P('comp'), may hold values from 0 to 2047, as said below
Outputs:
- spectra_grid: float32 [600, 1024, 256], P('grp', 'comp')
The draws below stay inside these ranges and needn't reach their ends.
Inputs may be any that keep to these rules, and one draw needn't show every extreme that they name: `sea_cell`: each aligned block of 1536 entries names 1536 different cells of one tile of 8 x 256 cells (row * 256 + column).
All inputs are finite; a program needn't handle non-finite values.
Results may differ from the reference program's by a relative error of at most 0.0003.
Values sent between devices are 32-bit elements; how exact they have to be, the bound alone decides.
No kernel may reach another device: no remote copies, remote signals or barrier semaphores. Data moves between devices by JAX's collectives and lax.ppermute only.
A program may use at most 64 MiB of HBM per device.

```python
import math
import jax
import jax.numpy as jnp
from jax import lax

DIRS = 24
FREQ = 25
TROWS = 8
NY = 256
ADV_STEPS = 2
SEA = 1536
SEND = 12
NPTS = 196608
NX = 1024


def draw_sea_cell(key, part):
    key = jax.random.fold_in(key, 11)
    tile_count = NPTS // SEA
    subkeys = jax.random.split(key, tile_count)

    def one_tile(subkey):
        return jax.random.permutation(subkey, TROWS * NY)[:SEA]
    tile_cells = jax.vmap(one_tile)(subkeys)
    return tile_cells.reshape(-1).astype(jnp.int32)


def block_levels(own_key, extent, cuts, least, high):
    factor_of = 1.0
    for position, shards_of in cuts:
        heights = jax.random.uniform(jax.random.fold_in(jax.random.fold_in(own_key, 6), position), (shards_of,), jnp.float32, least / len(cuts), high / len(cuts))
        factor_of = factor_of * jnp.repeat(jnp.exp(heights), extent[position] // shards_of).reshape((-1,) + (1,) * (len(extent) - 1 - position))
    return factor_of


def setup_inputs(seed: int = 0) -> dict:
    splits = jax.random.split(jax.random.key(seed), 5)
    return {
        "spectra": jnp.clip(jnp.exp(math.log(2.0) - 3.6888794 * jax.random.uniform(splits[0], (DIRS * FREQ, NPTS), jnp.float32) ** block_levels(splits[0], (DIRS * FREQ, NPTS), ((0, 4), (1, 128)), -0.2, 0.2)), 0.05, 2.0),
        "wind_speed": jnp.clip(4.0 + 20.0 * jax.random.uniform(splits[1], (NPTS,), jnp.float32) ** block_levels(splits[1], (NPTS,), ((0, 128),), -0.2, 0.2), 4.0, 24.0),
        "wind_dir": jnp.clip(jax.random.uniform(splits[2], (NPTS,), jnp.float32, -3.140625, 3.140625), -3.140625, 3.140625),
        "sea_cell": draw_sea_cell(jax.random.fold_in(splits[4], 71), 0),
    }


GRAV = 9.81
LOW_FREQ = 0.0418
FREQ_STEP = 1.1


def spectral_tables(first_dir, dir_count, total_dirs, freq_count):
    component = jnp.arange(dir_count * freq_count, dtype=jnp.int32)
    direction = (component // freq_count + first_dir).astype(jnp.float32)
    frequency = LOW_FREQ * jnp.power(jnp.float32(FREQ_STEP), (component % freq_count).astype(jnp.float32))
    angles = 2.0 * math.pi * (direction + 0.5) / total_dirs
    angular = 2.0 * math.pi * frequency
    weight = (2.0 * math.pi / total_dirs) * 0.1 * frequency
    return angles, angular, weight


def source_terms(spectra, energy, inverse, angles, angular, wind_speed, wind_dir):
    mean_freq = energy / inverse
    wavenumber = mean_freq * mean_freq / GRAV
    steepness = energy * wavenumber * wavenumber
    steep_ratio = steepness / (steepness + 0.02)
    forcing = 28.0 * 0.035 * wind_speed * jnp.cos(angles - wind_dir) * angular / GRAV
    rate_in = 0.1 * jnp.maximum(forcing - 1.0, 0.0)
    relative = angular / mean_freq
    rate_out = 0.4 * relative * relative * steep_ratio
    return spectra * jnp.exp(rate_in - rate_out)


def courant(angles, angular):
    reach = 0.45 * (2.0 * math.pi * LOW_FREQ) / angular
    return reach * jnp.cos(angles), reach * jnp.sin(angles)


def koren_slope(slope_back, slope_ahead):
    middle = (slope_back + 2.0 * slope_ahead) / 3.0
    rising = jnp.maximum(0.0, jnp.minimum(jnp.minimum(2.0 * slope_ahead, middle), 2.0 * slope_back))
    falling = jnp.minimum(0.0, jnp.maximum(jnp.maximum(2.0 * slope_ahead, middle), 2.0 * slope_back))
    return jnp.where(slope_back >= 0.0, rising, falling)


def face_flux(back_one, centre, ahead_one, ahead_two, number):
    forward = number >= 0.0
    upstream = jnp.where(forward, centre, ahead_one)
    slope_back = jnp.where(forward, centre - back_one, ahead_one - ahead_two)
    slope_ahead = jnp.where(forward, ahead_one - centre, centre - ahead_one)
    return number * (upstream + 0.5 * (1.0 - jnp.abs(number)) * koren_slope(slope_back, slope_ahead))


def advect(padded, courant_x, courant_y):
    count = padded.shape[-2] - 4
    flux_rows = face_flux(padded[..., 0:count + 1, :], padded[..., 1:count + 2, :],
                          padded[..., 2:count + 3, :], padded[..., 3:count + 4, :], courant_x)
    centre = padded[..., 2:count + 2, :]
    flux_cols = face_flux(jnp.roll(centre, 1, -1), centre, jnp.roll(centre, -1, -1),
                          jnp.roll(centre, -2, -1), courant_y)
    return centre - (flux_rows[..., 1:, :] - flux_rows[..., :-1, :]) - (flux_cols - jnp.roll(flux_cols, 1, -1))


def reference(spectra, wind_speed, wind_dir, sea_cell):
    angles, angular, weight = spectral_tables(0, DIRS, DIRS, FREQ)
    energy = jnp.sum(weight[:, None] * spectra, axis=0)
    inverse = jnp.sum((weight / angular)[:, None] * spectra, axis=0)
    sourced = source_terms(spectra, energy, inverse, angles[:, None], angular[:, None],
                           wind_speed[None, :], wind_dir[None, :])
    slot_index = jnp.arange(NPTS, dtype=jnp.int32)
    tile_index = slot_index // SEA
    within = slot_index % SEA
    sender = within // SEND
    place_index = within % SEND
    point_index = sender * SEA + tile_index * SEND + place_index
    cell_index = tile_index * (TROWS * NY) + sea_cell.astype(jnp.int32)
    grid_flat = jnp.zeros((DIRS * FREQ, NX * NY), jnp.float32).at[:, cell_index].set(sourced[:, point_index])
    sea_mask = jnp.zeros((NX * NY,), jnp.float32).at[cell_index].set(1.0).reshape(NX, NY)
    courant_x, courant_y = courant(angles, angular)

    def advance(packed):
        wave_field, number_x, number_y = packed
        wave_field = wave_field.reshape(NX, NY)
        for substep in range(ADV_STEPS):
            wave_field = advect(jnp.pad(wave_field, ((2, 2), (0, 0))), number_x, number_y) * sea_mask
        return wave_field

    return lax.map(advance, (grid_flat, courant_x, courant_y))
```

```python
import functools
import math

import jax
import jax.numpy as jnp
import numpy as np
from jax import lax
from jax.experimental import pallas as pl
from jax.experimental.pallas import tpu as pltpu
from jax.sharding import PartitionSpec as P

DIRS = 24
FREQ = 25
TROWS = 8
NY = 256
SEA = 1536
SEND = 12
GROUPS = 4
TILES = 128
LOCAL = DIRS * FREQ // GROUPS
ROWS = 152
MASK_ROW = LOCAL
MAIN = 128
EXTRA = ROWS - MAIN
PER_TILE = 5
SLOTS = 15
GRAV = 9.81
LOW_FREQ = 0.0418
FREQ_STEP = 1.1

VMEM = pl.BlockSpec(memory_space=pltpu.VMEM)
SMEM = pl.BlockSpec(memory_space=pltpu.SMEM)
BIG = pltpu.CompilerParams(vmem_limit_bytes=48 * 1024 * 1024)

W_E, W_I, C_COS, C_SIN, C_OUT, U_X, K_X, U_Y, K_Y = range(9)


def coefficient_table():
    table = np.zeros((GROUPS, ROWS, 128), np.float64)
    for group in range(GROUPS):
        for row in range(LOCAL):
            d, j = row // FREQ + group * (DIRS // GROUPS), row % FREQ
            angle = 2.0 * math.pi * (d + 0.5) / DIRS
            freq = LOW_FREQ * FREQ_STEP**j
            s = 2.0 * math.pi * freq
            w = 2.0 * math.pi / DIRS * 0.1 * freq
            reach = 0.45 * (2.0 * math.pi * LOW_FREQ) / s
            ux, uy = abs(reach * math.cos(angle)), abs(reach * math.sin(angle))
            push = 0.1 * 28.0 * 0.035 * s / GRAV
            table[group, row, :9] = (
                w, w / s, push * math.cos(angle), push * math.sin(angle), 0.4 * s * s,
                ux, ux * (1.0 - ux), uy, uy * (1.0 - uy),
            )
    return table.astype(np.float32)


def pack_kernel(x_ref, wind_ref, out_ref, z_ref, b_ref):
    b_ref[0 : LOCAL - MAIN, :] = x_ref[MAIN:LOCAL, :]
    b_ref[LOCAL - MAIN : EXTRA, :] = wind_ref[...]
    b_ref[EXTRA:128, :] = jnp.zeros((128 - EXTRA, SEA), jnp.float32)
    for block in range(SEA // 128):
        cols = slice(block * 128, block * 128 + 128)
        z_ref[0, cols, :] = x_ref[0:MAIN, cols].T
        z_ref[1, cols, :] = b_ref[:, cols].T
    for k in range(SEND):
        out_ref[pl.ds(k, TILES, stride=SLOTS), :] = z_ref[0, pl.ds(k, TILES, stride=SEND), :]
    for tile in range(SLOTS - SEND):
        total = None
        for k in range(tile * PER_TILE, min(SEND, (tile + 1) * PER_TILE)):
            piece = z_ref[1, pl.ds(k, TILES, stride=SEND), :]
            shift = (k % PER_TILE) * EXTRA
            piece = pltpu.roll(piece, shift, 1) if shift else piece
            total = piece if total is None else total + piece
        out_ref[pl.ds(SEND + tile, TILES, stride=SLOTS), :] = total


def moments_kernel(r_ref, tab_ref, y_ref, wind_ref, e_ref):
    extra = None
    we = jnp.broadcast_to(tab_ref[:, W_E : W_E + 1], (ROWS, 128))
    wi = jnp.broadcast_to(tab_ref[:, W_I : W_I + 1], (ROWS, 128))
    for k in range(SEND):
        if k % PER_TILE == 0:
            extra = r_ref[pl.ds(SEND + k // PER_TILE, TILES, stride=SLOTS), :].T
        part = extra[(k % PER_TILE) * EXTRA : (k % PER_TILE + 1) * EXTRA, :]
        main = r_ref[pl.ds(k, TILES, stride=SLOTS), :].T
        y_ref[k, 0:MAIN, :] = main
        y_ref[k, MAIN:ROWS, :] = part
        wind_ref[k : k + 1, :] = part[LOCAL - MAIN : LOCAL - MAIN + 1, :]
        wind_ref[SEND + k : SEND + k + 1, :] = part[LOCAL - MAIN + 1 : EXTRA, :]
        y = y_ref[k]
        energy = jnp.sum(y * we, axis=0, keepdims=True)
        inverse = jnp.sum(y * wi, axis=0, keepdims=True)
        for g in range(GROUPS):
            e_ref[g, k : k + 1, :] = energy
            e_ref[g, SEND + k : SEND + k + 1, :] = inverse


def onehot_kernel(cell_ref, out_ref):
    lane = lax.broadcasted_iota(jnp.int32, (128, 128), 1)
    for k in range(SEND):
        cell = jnp.broadcast_to(cell_ref[k : k + 1, :], (128, 128)).T
        for tile in range(TROWS * NY // 128):
            hit = cell == lane + tile * 128
            out_ref[k * 128 : (k + 1) * 128, tile * 128 : (tile + 1) * 128] = jnp.where(
                hit, 1.0, 0.0
            ).astype(jnp.bfloat16)


def place_kernel(y_ref, wind_ref, e_ref, tab_ref, hot_ref, low_ref, mid_ref, up_ref, s_ref):
    moments = e_ref[0] + e_ref[1] + e_ref[2] + e_ref[3]
    energy, inverse = moments[0:SEND], moments[SEND : 2 * SEND]
    mean = energy / inverse
    wavenumber = mean * mean / GRAV
    steepness = energy * wavenumber * wavenumber
    ratio = steepness / (steepness + 0.02)
    decay = ratio / (mean * mean)
    speed, heading = wind_ref[0:SEND, :], wind_ref[SEND : 2 * SEND, :]
    along = speed * jnp.cos(heading)
    across = speed * jnp.sin(heading)
    ccos = jnp.broadcast_to(tab_ref[:, C_COS : C_COS + 1], (ROWS, 128))
    csin = jnp.broadcast_to(tab_ref[:, C_SIN : C_SIN + 1], (ROWS, 128))
    cout = jnp.broadcast_to(tab_ref[:, C_OUT : C_OUT + 1], (ROWS, 128))
    row = lax.broadcasted_iota(jnp.int32, (ROWS, 128), 0)
    for k in range(SEND):
        grow = ccos * along[k : k + 1] + csin * across[k : k + 1]
        rate = jnp.maximum(grow - 0.1, 0.0) - cout * decay[k : k + 1]
        value = y_ref[k] * jnp.exp(rate)
        value = jnp.where(row < LOCAL, value, jnp.where(row == MASK_ROW, 1.0, 0.0))
        s_ref[:, k * 128 : (k + 1) * 128] = value
    value = s_ref[...]
    high = value.astype(jnp.bfloat16)
    rest = (value - high.astype(jnp.float32)).astype(jnp.bfloat16)
    for e in range(TROWS):
        hot = hot_ref[:, e * NY : (e + 1) * NY]
        out = jnp.dot(high, hot, preferred_element_type=jnp.float32)
        out = out + jnp.dot(rest, hot, preferred_element_type=jnp.float32)
        if e < 2:
            low_ref[e] = out
        elif e < 4:
            mid_ref[e - 2] = out
        else:
            up_ref[e - 4] = out


def limited(a, b):
    m = (a + (b + b)) * (1.0 / 6.0)
    rising = jnp.maximum(jnp.minimum(m, jnp.minimum(a, b)), 0.0)
    falling = jnp.minimum(jnp.maximum(m, jnp.maximum(a, b)), 0.0)
    return rising + falling


def advance(q, mask, coef, forward):
    ux, kx, uy, ky = coef
    step, back = (NY - 1, 1) if forward else (1, NY - 1)
    diff = [q[i + 1] - q[i] for i in range(len(q) - 1)]
    flux = [None] + [
        ux * q[i] + kx * limited(diff[i - 1], diff[i]) for i in range(1, len(q) - 1)
    ]
    new = []
    for i in range(2, len(q) - 1):
        ahead = pltpu.roll(q[i], step, 1) - q[i]
        behind = pltpu.roll(ahead, back, 1)
        side = uy * q[i] + ky * limited(behind, ahead)
        div = (flux[i] - flux[i - 1]) + (side - pltpu.roll(side, back, 1))
        new.append((q[i] - div) * mask[i - 2])
    return new


def advect_kernel(flag_ref, tab_ref, below_ref, low_ref, mid_ref, up_ref, above_ref, out_ref,
                  mask_ref, coef_ref, turn_ref):
    cells = [(below_ref, i) for i in range(4)] + [(low_ref, i) for i in range(2)]
    cells += [(mid_ref, i) for i in range(2)] + [(up_ref, i) for i in range(4)]
    cells += [(above_ref, i) for i in range(2)]
    for i in range(2, 13):
        ref, at = cells[i]
        mask_ref[i - 2] = jnp.broadcast_to(ref[at, MASK_ROW : MASK_ROW + 1, :], (8, NY))
    for n, column in enumerate((U_X, K_X, U_Y, K_Y)):
        coef_ref[n] = jnp.broadcast_to(tab_ref[:, column : column + 1], (ROWS, NY))
    mirrored = flag_ref[0]

    def tile(start, count, forward):
        rows = pl.ds(start, 8)
        q = [ref[at, rows, :] for ref, at in cells]
        coef = [coef_ref[n, rows, :] for n in range(4)]
        q = advance(q, [mask_ref[i] for i in range(11)], coef, forward)
        q = advance(q, [mask_ref[i] for i in range(2, 10)], coef, forward)
        for e in range(TROWS):
            r = e + (TROWS - 1 - 2 * e) * mirrored
            for half in range(2):
                turn_ref[half, pl.ds(r, 8, stride=TROWS), :] = q[e][:, half * 128 : half * 128 + 128]
        for i in range(count):
            for half in range(2):
                out_ref[start + i, :, half * 128 : half * 128 + 128] = turn_ref[
                    half, i * TROWS : (i + 1) * TROWS, :
                ]

    def sweep(forward):
        def body(i, carry):
            tile(pl.multiple_of(i * 8, 8), 8, forward)
            return carry

        lax.fori_loop(0, LOCAL // 8, body, 0)
        tile(LOCAL // 8 * 8, LOCAL % 8, forward)

    @pl.when(flag_ref[1] == 0)
    def _():
        sweep(True)

    @pl.when(flag_ref[1] == 1)
    def _():
        sweep(False)


def call(kernel, shapes, scratch, ins, *args):
    return pl.pallas_call(
        kernel,
        out_shape=shapes,
        in_specs=ins,
        out_specs=jax.tree.map(lambda _: VMEM, shapes),
        scratch_shapes=scratch,
        compiler_params=BIG,
    )(*args)


def f32(*shape):
    return jax.ShapeDtypeStruct(shape, jnp.float32)


def local(spectra, wind_speed, wind_dir, sea_cell):
    group = lax.axis_index("grp")
    table = lax.dynamic_index_in_dim(jnp.asarray(coefficient_table()), group, 0, keepdims=False)
    mirror_x = ((group == 1) | (group == 2)).astype(jnp.int32)
    mirror_y = (group >= 2).astype(jnp.int32)
    flags = jnp.stack([mirror_x, mirror_y])
    wind = jnp.stack([wind_speed, wind_dir])
    packed = call(
        pack_kernel,
        f32(TILES * SLOTS, 128),
        [pltpu.VMEM((2, SEA, 128), jnp.float32), pltpu.VMEM((128, SEA), jnp.float32)],
        [VMEM] * 2,
        spectra,
        wind,
    )
    received = lax.all_to_all(
        packed.reshape(TILES, 1, SLOTS * 128), "comp", split_axis=0, concat_axis=0, tiled=True
    ).reshape(TILES * SLOTS, 128)
    cells = sea_cell.reshape(TILES, SEND).T
    cells = cells ^ (mirror_x * (NY * (TROWS - 1)))
    hot = call(
        onehot_kernel,
        jax.ShapeDtypeStruct((SEA, TROWS * NY), jnp.bfloat16),
        [],
        [VMEM],
        cells,
    )
    points, wind_here, partial = call(
        moments_kernel,
        (f32(SEND, ROWS, 128), f32(2 * SEND, 128), f32(GROUPS, 2 * SEND, 128)),
        [],
        [VMEM] * 2,
        received,
        table,
    )
    partial = lax.all_to_all(partial, "grp", split_axis=0, concat_axis=0, tiled=True)
    low, mid, up = call(
        place_kernel,
        (f32(2, ROWS, NY), f32(2, ROWS, NY), f32(4, ROWS, NY)),
        [pltpu.VMEM((ROWS, SEA), jnp.float32)],
        [VMEM] * 5,
        points,
        wind_here,
        partial,
        table,
        hot,
    )
    ahead, back = [], []
    for g in range(GROUPS):
        for i in range(TILES - 1):
            rise, fall = (g * TILES + i, g * TILES + i + 1), (g * TILES + i + 1, g * TILES + i)
            ahead.append(fall if g in (1, 2) else rise)
            back.append(rise if g in (1, 2) else fall)
    below = lax.ppermute(up, ("grp", "comp"), ahead)
    above = lax.ppermute(low, ("grp", "comp"), back)
    return call(
        advect_kernel,
        f32(LOCAL, TROWS, NY),
        [
            pltpu.VMEM((11, 8, NY), jnp.float32),
            pltpu.VMEM((4, ROWS, NY), jnp.float32),
            pltpu.VMEM((2, 8 * TROWS, 128), jnp.float32),
        ],
        [SMEM] + [VMEM] * 6,
        flags,
        table,
        below,
        low,
        mid,
        up,
        above,
    )


def solution(mesh):
    in_specs = (P("grp", "comp"), P("comp"), P("comp"), P("comp"))
    out_specs = P("grp", "comp", None)
    return jax.shard_map(local, mesh=mesh, in_specs=in_specs, out_specs=out_specs, check_vma=False)
```

```python
import functools
import math

import jax
import jax.numpy as jnp
import numpy as np
from jax import lax
from jax.experimental import pallas as pl
from jax.experimental.pallas import tpu as pltpu
from jax.sharding import PartitionSpec as P

DIRS = 24
FREQ = 25
TROWS = 8
NY = 256
SEA = 1536
SEND = 12
GROUPS = 4
TILES = 128
LOCAL = DIRS * FREQ // GROUPS
ROWS = 152
DEPTH = 160
MASK_ROW = LOCAL
MAIN = 128
EXTRA = ROWS - MAIN
PER_TILE = 5
SLOTS = 15
GRAV = 9.81
LOW_FREQ = 0.0418
FREQ_STEP = 1.1

VMEM = pl.BlockSpec(memory_space=pltpu.VMEM)
SMEM = pl.BlockSpec(memory_space=pltpu.SMEM)

W_E, W_I, C_COS, C_SIN, C_OUT, U_X, K_X, U_Y, K_Y = range(9)


def coefficient_table():
    table = np.zeros((GROUPS, ROWS, 128), np.float64)
    for group in range(GROUPS):
        for row in range(LOCAL):
            d, j = row // FREQ + group * (DIRS // GROUPS), row % FREQ
            angle = 2.0 * math.pi * (d + 0.5) / DIRS
            freq = LOW_FREQ * FREQ_STEP**j
            s = 2.0 * math.pi * freq
            w = 2.0 * math.pi / DIRS * 0.1 * freq
            reach = 0.45 * (2.0 * math.pi * LOW_FREQ) / s
            ux, uy = abs(reach * math.cos(angle)), abs(reach * math.sin(angle))
            push = 0.1 * 28.0 * 0.035 * s / GRAV
            table[group, row, :9] = (
                w, w / s, push * math.cos(angle), push * math.sin(angle), 0.4 * s * s,
                ux, ux * (1.0 - ux), uy, uy * (1.0 - uy),
            )
    return table.astype(np.float32)


def pack_kernel(x_ref, speed_ref, heading_ref, out_ref, z_ref, b_ref):
    b_ref[0 : LOCAL - MAIN, :] = x_ref[MAIN:LOCAL, :]
    for block in range(SEA // 128):
        cols = slice(block * 128, block * 128 + 128)
        b_ref[LOCAL - MAIN : LOCAL - MAIN + 1, cols] = speed_ref[block : block + 1, :]
        b_ref[LOCAL - MAIN + 1 : EXTRA, cols] = heading_ref[block : block + 1, :]
    b_ref[EXTRA:128, :] = jnp.zeros((128 - EXTRA, SEA), jnp.float32)
    for block in range(SEA // 128):
        cols = slice(block * 128, block * 128 + 128)
        z_ref[0, cols, :] = x_ref[0:MAIN, cols].T
        z_ref[1, cols, :] = b_ref[:, cols].T
    for k in range(SEND):
        out_ref[pl.ds(k, TILES, stride=SLOTS), :] = z_ref[0, pl.ds(k, TILES, stride=SEND), :]
    for tile in range(SLOTS - SEND):
        total = None
        for k in range(tile * PER_TILE, min(SEND, (tile + 1) * PER_TILE)):
            piece = z_ref[1, pl.ds(k, TILES, stride=SEND), :]
            shift = (k % PER_TILE) * EXTRA
            piece = pltpu.roll(piece, shift, 1) if shift else piece
            total = piece if total is None else total + piece
        out_ref[pl.ds(SEND + tile, TILES, stride=SLOTS), :] = total


def moments_kernel(r_ref, tab_ref, y_ref, wind_ref, e_ref):
    extra = None
    we = jnp.broadcast_to(tab_ref[:, W_E : W_E + 1], (ROWS, 128))
    wi = jnp.broadcast_to(tab_ref[:, W_I : W_I + 1], (ROWS, 128))
    for k in range(SEND):
        if k % PER_TILE == 0:
            extra = r_ref[pl.ds(SEND + k // PER_TILE, TILES, stride=SLOTS), :].T
        part = extra[(k % PER_TILE) * EXTRA : (k % PER_TILE + 1) * EXTRA, :]
        main = r_ref[pl.ds(k, TILES, stride=SLOTS), :].T
        y_ref[k, 0:MAIN, :] = main
        y_ref[k, MAIN:ROWS, :] = part
        wind_ref[k : k + 1, :] = part[LOCAL - MAIN : LOCAL - MAIN + 1, :]
        wind_ref[SEND + k : SEND + k + 1, :] = part[LOCAL - MAIN + 1 : EXTRA, :]
        y = y_ref[k]
        energy = jnp.sum(y * we, axis=0, keepdims=True)
        inverse = jnp.sum(y * wi, axis=0, keepdims=True)
        for g in range(GROUPS):
            e_ref[g, k : k + 1, :] = energy
            e_ref[g, SEND + k : SEND + k + 1, :] = inverse


def onehot_kernel(cell_ref, out_ref):
    lane = lax.broadcasted_iota(jnp.int32, (128, 128), 1)
    for k in range(SEND):
        cell = jnp.broadcast_to(cell_ref[k : k + 1, :], (128, 128)).T
        for tile in range(TROWS * NY // 128):
            hit = cell == lane + tile * 128
            lanes = slice(tile % 8 * 128, tile % 8 * 128 + 128)
            out_ref[tile // 8, k * 128 : (k + 1) * 128, lanes] = jnp.where(hit, 1.0, 0.0).astype(
                jnp.bfloat16
            )


def place_kernel(y_ref, wind_ref, e_ref, tab_ref, hot_ref, low_ref, mid_ref, up_ref, s_ref,
                 held_ref, sem):
    copies = [pltpu.make_async_copy(hot_ref.at[h], held_ref.at[h], sem.at[h]) for h in range(2)]
    copies[1].start()
    copies[0].start()
    moments = e_ref[0] + e_ref[1] + e_ref[2] + e_ref[3]
    energy, inverse = moments[0:SEND], moments[SEND : 2 * SEND]
    mean = energy / inverse
    wavenumber = mean * mean / GRAV
    steepness = energy * wavenumber * wavenumber
    ratio = steepness / (steepness + 0.02)
    decay = ratio / (mean * mean)
    speed, heading = wind_ref[0:SEND, :], wind_ref[SEND : 2 * SEND, :]
    along = speed * jnp.cos(heading)
    across = speed * jnp.sin(heading)
    ccos = jnp.broadcast_to(tab_ref[:, C_COS : C_COS + 1], (ROWS, 128))
    csin = jnp.broadcast_to(tab_ref[:, C_SIN : C_SIN + 1], (ROWS, 128))
    cout = jnp.broadcast_to(tab_ref[:, C_OUT : C_OUT + 1], (ROWS, 128))
    row = lax.broadcasted_iota(jnp.int32, (ROWS, 128), 0)
    s_ref[ROWS:DEPTH, :] = jnp.zeros((DEPTH - ROWS, SEA), jnp.float32)
    for k in range(SEND):
        grow = ccos * along[k : k + 1] + csin * across[k : k + 1]
        rate = jnp.maximum(grow - 0.1, 0.0) - cout * decay[k : k + 1]
        value = y_ref[k] * jnp.exp(rate)
        value = jnp.where(row < LOCAL, value, jnp.where(row == MASK_ROW, 1.0, 0.0))
        s_ref[0:ROWS, k * 128 : (k + 1) * 128] = value
    value = s_ref[...]
    high = value.astype(jnp.bfloat16)
    rest = (value - high.astype(jnp.float32)).astype(jnp.bfloat16)
    both = jnp.concatenate([high, rest], axis=0)
    for half in (1, 0):
        copies[half].wait()
        for i in range(4):
            hot = held_ref[half, :, i * NY : (i + 1) * NY]
            out = jnp.dot(both, hot, preferred_element_type=jnp.float32)
            out = out[0:ROWS] + out[DEPTH : DEPTH + ROWS]
            if half == 1:
                up_ref[i] = out
            elif i < 2:
                low_ref[i] = out
            else:
                mid_ref[i - 2] = out


def limited(a, b):
    m = (a + (b + b)) * (1.0 / 6.0)
    rising = jnp.maximum(jnp.minimum(m, jnp.minimum(a, b)), 0.0)
    falling = jnp.minimum(jnp.maximum(m, jnp.maximum(a, b)), 0.0)
    return rising + falling


def advance(q, mask, coef, forward):
    ux, kx, uy, ky = coef
    step, back = (NY - 1, 1) if forward else (1, NY - 1)
    diff = [q[i + 1] - q[i] for i in range(len(q) - 1)]
    flux = [None] + [
        ux * q[i] + kx * limited(diff[i - 1], diff[i]) for i in range(1, len(q) - 1)
    ]
    new = []
    for i in range(2, len(q) - 1):
        ahead = pltpu.roll(q[i], step, 1) - q[i]
        behind = pltpu.roll(ahead, back, 1)
        side = uy * q[i] + ky * limited(behind, ahead)
        div = (flux[i] - flux[i - 1]) + (side - pltpu.roll(side, back, 1))
        new.append((q[i] - div) * mask[i - 2])
    return new


def advect_kernel(flag_ref, tab_ref, below_ref, low_ref, mid_ref, up_ref, above_ref, out_ref,
                  mask_ref, coef_ref, turn_ref):
    cells = [(below_ref, i) for i in range(4)] + [(low_ref, i) for i in range(2)]
    cells += [(mid_ref, i) for i in range(2)] + [(up_ref, i) for i in range(4)]
    cells += [(above_ref, i) for i in range(2)]
    for i in range(2, 13):
        ref, at = cells[i]
        mask_ref[i - 2] = jnp.broadcast_to(ref[at, MASK_ROW : MASK_ROW + 1, :], (8, NY))
    for n, column in enumerate((U_X, K_X, U_Y, K_Y)):
        coef_ref[n] = jnp.broadcast_to(tab_ref[:, column : column + 1], (ROWS, NY))
    mirrored = flag_ref[0]

    def tile(start, count, forward):
        rows = pl.ds(start, 8)
        q = [ref[at, rows, :] for ref, at in cells]
        coef = [coef_ref[n, rows, :] for n in range(4)]
        q = advance(q, [mask_ref[i] for i in range(11)], coef, forward)
        q = advance(q, [mask_ref[i] for i in range(2, 10)], coef, forward)
        for e in range(TROWS):
            r = e + (TROWS - 1 - 2 * e) * mirrored
            for half in range(2):
                turn_ref[half, pl.ds(r, 8, stride=TROWS), :] = q[e][:, half * 128 : half * 128 + 128]
        for i in range(count):
            for half in range(2):
                out_ref[start + i, :, half * 128 : half * 128 + 128] = turn_ref[
                    half, i * TROWS : (i + 1) * TROWS, :
                ]

    def sweep(forward):
        def body(i, carry):
            tile(pl.multiple_of(i * 8, 8), 8, forward)
            return carry

        lax.fori_loop(0, LOCAL // 8, body, 0)
        tile(LOCAL // 8 * 8, LOCAL % 8, forward)

    @pl.when(flag_ref[1] == 0)
    def _():
        sweep(True)

    @pl.when(flag_ref[1] == 1)
    def _():
        sweep(False)


def call(kernel, shapes, scratch, ins, *args, limit=20):
    return pl.pallas_call(
        kernel,
        out_shape=shapes,
        in_specs=ins,
        out_specs=jax.tree.map(lambda _: VMEM, shapes),
        scratch_shapes=scratch,
        compiler_params=pltpu.CompilerParams(vmem_limit_bytes=limit * 1024 * 1024),
    )(*args)


def f32(*shape):
    return jax.ShapeDtypeStruct(shape, jnp.float32)


def local(spectra, wind_speed, wind_dir, sea_cell):
    group = lax.axis_index("grp")
    table = lax.dynamic_index_in_dim(jnp.asarray(coefficient_table()), group, 0, keepdims=False)
    mirror_x = ((group == 1) | (group == 2)).astype(jnp.int32)
    mirror_y = (group >= 2).astype(jnp.int32)
    flags = jnp.stack([mirror_x, mirror_y])
    packed = call(
        pack_kernel,
        f32(TILES * SLOTS, 128),
        [pltpu.VMEM((2, SEA, 128), jnp.float32), pltpu.VMEM((128, SEA), jnp.float32)],
        [VMEM] * 3,
        spectra,
        wind_speed.reshape(SEA // 128, 128),
        wind_dir.reshape(SEA // 128, 128),
    )
    received = lax.all_to_all(
        packed.reshape(TILES, 1, SLOTS * 128), "comp", split_axis=0, concat_axis=0, tiled=True
    ).reshape(TILES * SLOTS, 128)
    cells = sea_cell.reshape(TILES, SEND).T
    cells = cells ^ (mirror_x * (NY * (TROWS - 1)))
    hot = call(
        onehot_kernel,
        jax.ShapeDtypeStruct((2, SEA, 4 * NY), jnp.bfloat16),
        [],
        [VMEM],
        cells,
    )
    received, hot = lax.optimization_barrier((received, hot))
    points, wind_here, partial = call(
        moments_kernel,
        (f32(SEND, ROWS, 128), f32(2 * SEND, 128), f32(GROUPS, 2 * SEND, 128)),
        [],
        [VMEM] * 2,
        received,
        table,
    )
    partial = lax.all_to_all(partial, "grp", split_axis=0, concat_axis=0, tiled=True)
    low, mid, up = call(
        place_kernel,
        (f32(2, ROWS, NY), f32(2, ROWS, NY), f32(4, ROWS, NY)),
        [
            pltpu.VMEM((DEPTH, SEA), jnp.float32),
            pltpu.VMEM((2, SEA, 4 * NY), jnp.bfloat16),
            pltpu.SemaphoreType.DMA((2,)),
        ],
        [VMEM] * 4 + [pl.BlockSpec(memory_space=pltpu.HBM)],
        points,
        wind_here,
        partial,
        table,
        hot,
        limit=50,
    )
    ahead, back = [], []
    for g in range(GROUPS):
        for i in range(TILES - 1):
            rise, fall = (g * TILES + i, g * TILES + i + 1), (g * TILES + i + 1, g * TILES + i)
            ahead.append(fall if g in (1, 2) else rise)
            back.append(rise if g in (1, 2) else fall)
    below = lax.ppermute(up, ("grp", "comp"), ahead)
    above = lax.ppermute(low, ("grp", "comp"), back)
    return call(
        advect_kernel,
        f32(LOCAL, TROWS, NY),
        [
            pltpu.VMEM((11, 8, NY), jnp.float32),
            pltpu.VMEM((4, ROWS, NY), jnp.float32),
            pltpu.VMEM((2, 8 * TROWS, 128), jnp.float32),
        ],
        [SMEM] + [VMEM] * 6,
        flags,
        table,
        below,
        low,
        mid,
        up,
        above,
    )


def solution(mesh):
    in_specs = (P("grp", "comp"), P("comp"), P("comp"), P("comp"))
    out_specs = P("grp", "comp", None)
    return jax.shard_map(local, mesh=mesh, in_specs=in_specs, out_specs=out_specs, check_vma=False)
```

```python
import functools
import math

import jax
import jax.numpy as jnp
import numpy as np
from jax import lax
from jax.experimental import pallas as pl
from jax.experimental.pallas import tpu as pltpu
from jax.sharding import PartitionSpec as P

DIRS = 24
FREQ = 25
TROWS = 8
NY = 256
SEA = 1536
SEND = 12
GROUPS = 4
TILES = 128
LOCAL = DIRS * FREQ // GROUPS
ROWS = 152
DEPTH = 160
MAIN = 128
EXTRA = ROWS - MAIN
PER_TILE = 5
SLOTS = 15
GRAV = 9.81
LOW_FREQ = 0.0418
FREQ_STEP = 1.1

VMEM = pl.BlockSpec(memory_space=pltpu.VMEM)
SMEM = pl.BlockSpec(memory_space=pltpu.SMEM)

W_E, W_I, C_COS, C_SIN, C_OUT = range(5)
PHASES = 32
PACKS = 4
SHORT = PHASES // PACKS
LINES = (PHASES + SHORT) * 8
CHUNK = 4


def coefficient_tables():
    table = np.zeros((GROUPS, ROWS, 128), np.float64)
    courant = np.zeros((GROUPS, 8, 256), np.float64)
    for group in range(GROUPS):
        for row in range(LOCAL):
            d, j = row // FREQ + group * (DIRS // GROUPS), row % FREQ
            angle = 2.0 * math.pi * (d + 0.5) / DIRS
            freq = LOW_FREQ * FREQ_STEP**j
            s = 2.0 * math.pi * freq
            w = 2.0 * math.pi / DIRS * 0.1 * freq
            reach = 0.45 * (2.0 * math.pi * LOW_FREQ) / s
            ux, uy = abs(reach * math.cos(angle)), abs(reach * math.sin(angle))
            push = 0.1 * 28.0 * 0.035 * s / GRAV
            table[group, row, :5] = (
                w, w / s, push * math.cos(angle), push * math.sin(angle), 0.4 * s * s
            )
            if row < MAIN:
                lanes = [row]
            else:
                lanes = [128 + pack * 32 + row - MAIN for pack in range(PACKS)]
            for lane in lanes:
                courant[group, :4, lane] = (ux, ux * (1.0 - ux), uy, uy * (1.0 - uy))
    return table.astype(np.float32), courant.astype(np.float32)


def pack_kernel(x_ref, speed_ref, heading_ref, out_ref, z_ref, b_ref):
    b_ref[0 : LOCAL - MAIN, :] = x_ref[MAIN:LOCAL, :]
    for block in range(SEA // 128):
        cols = slice(block * 128, block * 128 + 128)
        b_ref[LOCAL - MAIN : LOCAL - MAIN + 1, cols] = speed_ref[block : block + 1, :]
        b_ref[LOCAL - MAIN + 1 : EXTRA, cols] = heading_ref[block : block + 1, :]
    b_ref[EXTRA:128, :] = jnp.zeros((128 - EXTRA, SEA), jnp.float32)
    for block in range(SEA // 128):
        cols = slice(block * 128, block * 128 + 128)
        z_ref[0, cols, :] = x_ref[0:MAIN, cols].T
        z_ref[1, cols, :] = b_ref[:, cols].T
    for k in range(SEND):
        out_ref[pl.ds(k, TILES, stride=SLOTS), :] = z_ref[0, pl.ds(k, TILES, stride=SEND), :]
    for tile in range(SLOTS - SEND):
        total = None
        for k in range(tile * PER_TILE, min(SEND, (tile + 1) * PER_TILE)):
            piece = z_ref[1, pl.ds(k, TILES, stride=SEND), :]
            shift = (k % PER_TILE) * EXTRA
            piece = pltpu.roll(piece, shift, 1) if shift else piece
            total = piece if total is None else total + piece
        out_ref[pl.ds(SEND + tile, TILES, stride=SLOTS), :] = total


def moments_kernel(r_ref, tab_ref, y_ref, wind_ref, e_ref):
    extra = None
    we = jnp.broadcast_to(tab_ref[:, W_E : W_E + 1], (ROWS, 128))
    wi = jnp.broadcast_to(tab_ref[:, W_I : W_I + 1], (ROWS, 128))
    for k in range(SEND):
        if k % PER_TILE == 0:
            extra = r_ref[pl.ds(SEND + k // PER_TILE, TILES, stride=SLOTS), :].T
        part = extra[(k % PER_TILE) * EXTRA : (k % PER_TILE + 1) * EXTRA, :]
        main = r_ref[pl.ds(k, TILES, stride=SLOTS), :].T
        y_ref[k, 0:MAIN, :] = main
        y_ref[k, MAIN:ROWS, :] = part
        wind_ref[k : k + 1, :] = part[LOCAL - MAIN : LOCAL - MAIN + 1, :]
        wind_ref[SEND + k : SEND + k + 1, :] = part[LOCAL - MAIN + 1 : EXTRA, :]
        y = y_ref[k]
        energy = jnp.sum(y * we, axis=0, keepdims=True)
        inverse = jnp.sum(y * wi, axis=0, keepdims=True)
        for g in range(GROUPS):
            e_ref[g, k : k + 1, :] = energy
            e_ref[g, SEND + k : SEND + k + 1, :] = inverse


def onehot_kernel(cell_ref, out_ref):
    row = lax.broadcasted_iota(jnp.int32, (16, 128), 0)
    base = row % 8 * 32 + row // 8
    spots = [cell_ref[k : k + 1, :] - base for k in range(SEND)]

    def body(e, carry):
        for phase in range(0, PHASES, 2):
            pack, short = phase // SHORT, phase % SHORT
            line = ((e // 4 * PACKS + pack) * 4 + e % 4) * SHORT * 8 + short * 8
            for k in range(SEND):
                hit = spots[k] == e * NY + phase
                out_ref[pl.ds(pl.multiple_of(line, 16), 16), k * 128 : (k + 1) * 128] = jnp.where(
                    hit, 1.0, 0.0
                ).astype(jnp.bfloat16)
        return carry

    lax.fori_loop(0, TROWS, body, 0)


def place_kernel(y_ref, wind_ref, e_ref, tab_ref, hot_ref, low_ref, mid_ref, up_ref, s_ref,
                 held_ref, side_ref, sem):
    half = TROWS * NY // 2
    copies = [
        pltpu.make_async_copy(hot_ref.at[pl.ds(h * half, half)], held_ref.at[h], sem.at[h])
        for h in range(2)
    ]
    copies[1].start()
    copies[0].start()
    moments = e_ref[0] + e_ref[1] + e_ref[2] + e_ref[3]
    energy, inverse = moments[0:SEND], moments[SEND : 2 * SEND]
    mean = energy / inverse
    wavenumber = mean * mean / GRAV
    steepness = energy * wavenumber * wavenumber
    ratio = steepness / (steepness + 0.02)
    decay = ratio / (mean * mean)
    speed, heading = wind_ref[0:SEND, :], wind_ref[SEND : 2 * SEND, :]
    along = speed * jnp.cos(heading)
    across = speed * jnp.sin(heading)
    ccos = jnp.broadcast_to(tab_ref[:, C_COS : C_COS + 1], (ROWS, 128))
    csin = jnp.broadcast_to(tab_ref[:, C_SIN : C_SIN + 1], (ROWS, 128))
    cout = jnp.broadcast_to(tab_ref[:, C_OUT : C_OUT + 1], (ROWS, 128))
    row = lax.broadcasted_iota(jnp.int32, (ROWS, 128), 0)
    s_ref[ROWS:DEPTH, :] = jnp.zeros((DEPTH - ROWS, SEA), jnp.float32)
    for k in range(SEND):
        grow = ccos * along[k : k + 1] + csin * across[k : k + 1]
        rate = jnp.maximum(grow - 0.1, 0.0) - cout * decay[k : k + 1]
        value = y_ref[k] * jnp.exp(rate)
        value = jnp.where(row < LOCAL, value, 0.0)
        s_ref[0:ROWS, k * 128 : (k + 1) * 128] = value
    value = s_ref[...]
    high = value.astype(jnp.bfloat16)
    rest = (value - high.astype(jnp.float32)).astype(jnp.bfloat16)
    main = jnp.concatenate([high[0:MAIN], rest[0:MAIN]], axis=0)
    side_ref[...] = jnp.zeros(side_ref.shape, jnp.bfloat16)
    for pack in range(PACKS):
        side_ref[pack, pack * 32 : pack * 32 + 32, :] = high[MAIN:DEPTH]
        side_ref[pack, 128 + pack * 32 : 128 + pack * 32 + 32, :] = rest[MAIN:DEPTH]
    turned = (((1,), (1,)), ((), ()))
    block = SHORT * 8
    for h in (1, 0):
        copies[h].wait()
        refs = [(up_ref, i) for i in range(4)]
        if h == 0:
            refs = [(low_ref, 0), (low_ref, 1), (mid_ref, 0), (mid_ref, 1)]
        out = lax.dot_general(held_ref[h], main, turned, preferred_element_type=jnp.float32)
        out = out[:, 0:128] + out[:, 128:256]
        for pack in range(PACKS):
            for i, (ref, at) in enumerate(refs):
                line = (pack * 4 + i) * block
                ref[at, pack * block : (pack + 1) * block, :] = out[line : line + block]
        total = None
        for pack in range(PACKS):
            hot = held_ref[h, pack * 4 * block : (pack + 1) * 4 * block, :]
            out = lax.dot_general(hot, side_ref[pack], turned, preferred_element_type=jnp.float32)
            total = out if total is None else total + out
        total = total[:, 0:128] + total[:, 128:256]
        for i, (ref, at) in enumerate(refs):
            ref[at, PHASES * 8 : LINES, :] = total[i * block : (i + 1) * block]


def limited(a, b):
    m = (a + (b + b)) * (1.0 / 6.0)
    least = jnp.minimum(jnp.maximum(a, b), 0.0)
    most = jnp.maximum(jnp.minimum(a, b), 0.0)
    return jnp.minimum(jnp.maximum(m, least), most)


def next_main(x):
    return pltpu.roll(x, 7, 0)


def last_main(x):
    return pltpu.roll(x, 1, 0)


def next_side(x):
    lane = lax.broadcasted_iota(jnp.int32, (8, 128), 1)
    x = pltpu.roll(x, 96, 1)
    return jnp.where(lane >= 96, pltpu.roll(x, 7, 0), x)


def last_side(x):
    lane = lax.broadcasted_iota(jnp.int32, (8, 128), 1)
    x = pltpu.roll(x, 32, 1)
    return jnp.where(lane < 32, pltpu.roll(x, 1, 0), x)


def substep(rows, seas, put, keep_ref, coef, base, phases, after, before):
    ux, kx, uy, ky = coef
    count = len(rows) - 3

    def load(spot, phase):
        ref, at = spot
        return ref[at, pl.ds(pl.multiple_of(base + phase * 8, 8), 8), :]

    for i in range(count):
        spot = rows[i + 2]
        end = load(spot, phases - 1)
        ahead = load(spot, 0) - before(end)
        prior = before(end - load(spot, phases - 2))
        keep_ref[i, 0] = ahead
        keep_ref[i, 1] = uy * before(end) + ky * limited(prior, ahead)

    def body(chunk, carry):
        first = chunk * CHUNK
        following = jnp.where(first + CHUNK == phases, 0, first + CHUNK)
        wraps = first + CHUNK == phases
        q = [load(rows[1], first + j) for j in range(CHUNK)]
        diff = [q[j] - load(rows[0], first + j) for j in range(CHUNK)]
        flux = None
        for i in range(-1, count):
            up = [load(rows[i + 3], first + j) for j in range(CHUNK)]
            slope = [up[j] - q[j] for j in range(CHUNK)]
            gone = [ux * q[j] + kx * limited(diff[j], slope[j]) for j in range(CHUNK)]
            if i >= 0:
                behind, past = keep_ref[i, 0], keep_ref[i, 1]
                edge = load(rows[i + 2], following)
                edge = jnp.where(wraps, after(edge), edge)
                for j in range(CHUNK):
                    ahead = (q[j + 1] if j + 1 < CHUNK else edge) - q[j]
                    side = uy * q[j] + ky * limited(behind, ahead)
                    new = q[j] - ((gone[j] - flux[j]) + (side - past))
                    sea = q[j] if seas is None else load(seas[i], first + j)
                    put(i, first + j, jnp.where(sea > 0.0, new, 0.0))
                    behind, past = ahead, side
                keep_ref[i, 0] = behind
                keep_ref[i, 1] = past
            q, diff, flux = up, slope, gone
        return carry

    lax.fori_loop(0, phases // CHUNK, body, 0)


def advect_kernel(flag_ref, tab_ref, below_ref, low_ref, mid_ref, up_ref, above_ref, out_ref,
                  once_ref, twice_ref, keep_ref, turn_ref, rest_ref):
    cells = [(below_ref, i) for i in range(4)] + [(low_ref, i) for i in range(2)]
    cells += [(mid_ref, i) for i in range(2)] + [(up_ref, i) for i in range(4)]
    cells += [(above_ref, i) for i in range(2)]
    rows_back = flag_ref[0]
    cols_back = flag_ref[1]
    halves = (
        (0, PHASES, 0, next_main, last_main),
        (PHASES * 8, SHORT, 128, next_side, last_side),
    )
    for base, phases, lanes, after, before in halves:
        coef = [
            jnp.broadcast_to(tab_ref[n : n + 1, lanes : lanes + 128], (8, 128)) for n in range(4)
        ]

        def put_once(i, phase, value):
            once_ref[i, pl.ds(pl.multiple_of(base + phase * 8, 8), 8), :] = value

        def put_twice(i, phase, value):
            if base == 0:
                phase = phase + (PHASES - 1 - 2 * phase) * cols_back
            line = i * LINES + base + phase * 8
            twice_ref[pl.ds(pl.multiple_of(line, 8), 8), :] = value

        substep(cells, None, put_once, keep_ref, coef, base, phases, after, before)
        once = [(once_ref, i) for i in range(11)]
        substep(once, cells[4:12], put_twice, keep_ref, coef, base, phases, after, before)

    for e in range(TROWS):
        r = e + (TROWS - 1 - 2 * e) * rows_back
        for half in range(2):
            parts = []
            for s in range(half * 4, half * 4 + 4):
                start = e * LINES + s + (7 - 2 * s) * cols_back
                parts.append(twice_ref[pl.ds(start, PHASES, stride=8), :])
            block = jnp.concatenate(parts, axis=0).T
            turn_ref[half, pl.ds(r, MAIN, stride=TROWS), :] = block
        line = e * LINES + PHASES * 8
        block = jnp.concatenate(
            [twice_ref[line : line + SHORT * 8, :], jnp.zeros((128 - SHORT * 8, 128), jnp.float32)],
            axis=0,
        ).T
        for pack in range(PACKS):
            rest_ref[pack, pl.ds(r, 32, stride=TROWS), :] = block[pack * 32 : pack * 32 + 32]
    spot = lax.broadcasted_iota(jnp.int32, (PACKS * 128, NY), 0)
    col = lax.broadcasted_iota(jnp.int32, (PACKS * 128, NY), 1)
    col = col + (NY - 1 - 2 * col) * cols_back
    pack, inner = spot // 128, spot % 128
    wanted = inner % 8 * 32 + pack * SHORT + inner // 8
    order = jnp.where((wanted == col) & (inner < SHORT * 8), 1.0, 0.0).astype(jnp.bfloat16)
    value = jnp.concatenate([rest_ref[pack] for pack in range(PACKS)], axis=1)
    high = value.astype(jnp.bfloat16)
    rest = (value - high.astype(jnp.float32)).astype(jnp.bfloat16)
    value = jnp.dot(high, order, preferred_element_type=jnp.float32)
    value = value + jnp.dot(rest, order, preferred_element_type=jnp.float32)
    for i in range(LOCAL - MAIN):
        out_ref[MAIN + i] = value[i * TROWS : (i + 1) * TROWS, :]
    for i in range(MAIN):
        for half in range(2):
            out_ref[i, :, half * 128 : half * 128 + 128] = turn_ref[
                half, i * TROWS : (i + 1) * TROWS, :
            ]


def call(kernel, shapes, scratch, ins, *args, limit=20):
    return pl.pallas_call(
        kernel,
        out_shape=shapes,
        in_specs=ins,
        out_specs=jax.tree.map(lambda _: VMEM, shapes),
        scratch_shapes=scratch,
        compiler_params=pltpu.CompilerParams(vmem_limit_bytes=limit * 1024 * 1024),
    )(*args)


def f32(*shape):
    return jax.ShapeDtypeStruct(shape, jnp.float32)


def local(spectra, wind_speed, wind_dir, sea_cell):
    group = lax.axis_index("grp")
    table, courant = (
        lax.dynamic_index_in_dim(jnp.asarray(t), group, 0, keepdims=False)
        for t in coefficient_tables()
    )
    mirror_x = ((group == 1) | (group == 2)).astype(jnp.int32)
    mirror_y = (group >= 2).astype(jnp.int32)
    flags = jnp.stack([mirror_x, mirror_y])
    packed = call(
        pack_kernel,
        f32(TILES * SLOTS, 128),
        [pltpu.VMEM((2, SEA, 128), jnp.float32), pltpu.VMEM((128, SEA), jnp.float32)],
        [VMEM] * 3,
        spectra,
        wind_speed.reshape(SEA // 128, 128),
        wind_dir.reshape(SEA // 128, 128),
    )
    received = lax.all_to_all(
        packed.reshape(TILES, 1, SLOTS * 128), "comp", split_axis=0, concat_axis=0, tiled=True
    ).reshape(TILES * SLOTS, 128)
    cells = sea_cell.reshape(TILES, SEND).T
    cells = cells ^ (mirror_x * (NY * (TROWS - 1)) + mirror_y * (NY - 1))
    hot = call(
        onehot_kernel,
        jax.ShapeDtypeStruct((TROWS * NY, SEA), jnp.bfloat16),
        [],
        [VMEM],
        cells,
    )
    received, hot = lax.optimization_barrier((received, hot))
    points, wind_here, partial = call(
        moments_kernel,
        (f32(SEND, ROWS, 128), f32(2 * SEND, 128), f32(GROUPS, 2 * SEND, 128)),
        [],
        [VMEM] * 2,
        received,
        table,
    )
    partial = lax.all_to_all(partial, "grp", split_axis=0, concat_axis=0, tiled=True)
    low, mid, up = call(
        place_kernel,
        (f32(2, LINES, 128), f32(2, LINES, 128), f32(4, LINES, 128)),
        [
            pltpu.VMEM((DEPTH, SEA), jnp.float32),
            pltpu.VMEM((2, TROWS * NY // 2, SEA), jnp.bfloat16),
            pltpu.VMEM((PACKS, 256, SEA), jnp.bfloat16),
            pltpu.SemaphoreType.DMA((2,)),
        ],
        [VMEM] * 4 + [pl.BlockSpec(memory_space=pltpu.HBM)],
        points,
        wind_here,
        partial,
        table,
        hot,
        limit=50,
    )
    ahead, back = [], []
    for g in range(GROUPS):
        for i in range(TILES - 1):
            rise, fall = (g * TILES + i, g * TILES + i + 1), (g * TILES + i + 1, g * TILES + i)
            ahead.append(fall if g in (1, 2) else rise)
            back.append(rise if g in (1, 2) else fall)
    below = lax.ppermute(up, ("grp", "comp"), ahead)
    above = lax.ppermute(low, ("grp", "comp"), back)
    return call(
        advect_kernel,
        f32(LOCAL, TROWS, NY),
        [
            pltpu.VMEM((11, LINES, 128), jnp.float32),
            pltpu.VMEM((TROWS * LINES, 128), jnp.float32),
            pltpu.VMEM((11, 2, 8, 128), jnp.float32),
            pltpu.VMEM((2, MAIN * TROWS, 128), jnp.float32),
            pltpu.VMEM((PACKS, 32 * TROWS, 128), jnp.float32),
        ],
        [SMEM] + [VMEM] * 6,
        flags,
        courant,
        below,
        low,
        mid,
        up,
        above,
    )


def solution(mesh):
    in_specs = (P("grp", "comp"), P("comp"), P("comp"), P("comp"))
    out_specs = P("grp", "comp", None)
    return jax.shard_map(local, mesh=mesh, in_specs=in_specs, out_specs=out_specs, check_vma=False)
```

```python
import functools
import math

import jax
import jax.numpy as jnp
import numpy as np
from jax import lax
from jax.experimental import pallas as pl
from jax.experimental.pallas import tpu as pltpu
from jax.sharding import PartitionSpec as P

DIRS = 24
FREQ = 25
TROWS = 8
NY = 256
SEA = 1536
SEND = 12
GROUPS = 4
TILES = 128
LOCAL = DIRS * FREQ // GROUPS
ROWS = 152
DEPTH = 160
MAIN = 128
EXTRA = ROWS - MAIN
PER_TILE = 5
SLOTS = 15
GRAV = 9.81
LOW_FREQ = 0.0418
FREQ_STEP = 1.1

VMEM = pl.BlockSpec(memory_space=pltpu.VMEM)
SMEM = pl.BlockSpec(memory_space=pltpu.SMEM)

W_E, W_I, C_COS, C_SIN, C_OUT = range(5)
PHASES = 32
PACKS = 4
SHORT = PHASES // PACKS
LINES = (PHASES + SHORT) * 8
CHUNK = 4
PARTS = 4
HALF = TROWS * NY // 2


def coefficient_tables():
    table = np.zeros((GROUPS, ROWS, 128), np.float64)
    courant = np.zeros((GROUPS, 8, 256), np.float64)
    for group in range(GROUPS):
        for row in range(LOCAL):
            d, j = row // FREQ + group * (DIRS // GROUPS), row % FREQ
            angle = 2.0 * math.pi * (d + 0.5) / DIRS
            freq = LOW_FREQ * FREQ_STEP**j
            s = 2.0 * math.pi * freq
            w = 2.0 * math.pi / DIRS * 0.1 * freq
            reach = 0.45 * (2.0 * math.pi * LOW_FREQ) / s
            ux, uy = abs(reach * math.cos(angle)), abs(reach * math.sin(angle))
            push = 0.1 * 28.0 * 0.035 * s / GRAV
            table[group, row, :5] = (
                w, w / s, push * math.cos(angle), push * math.sin(angle), 0.4 * s * s
            )
            if row < MAIN:
                lanes = [row]
            else:
                lanes = [128 + pack * 32 + row - MAIN for pack in range(PACKS)]
            for lane in lanes:
                courant[group, :4, lane] = (ux, ux * (1.0 - ux), uy, uy * (1.0 - uy))
    return table.astype(np.float32), courant.astype(np.float32)


def pack_kernel(x_hbm, speed_hbm, heading_hbm, out_hbm, x_ref, wind_ref, z_ref, b_ref, m_ref,
                sem_in, sem_wind, sem_out):
    width = SEA // PARTS
    tiles = TILES // PARTS
    ins = [
        pltpu.make_async_copy(x_hbm.at[:, pl.ds(c * width, width)], x_ref.at[c], sem_in.at[c])
        for c in range(PARTS)
    ]
    winds = [
        pltpu.make_async_copy(ref, wind_ref.at[i], sem_wind.at[i])
        for i, ref in enumerate((speed_hbm, heading_hbm))
    ]
    outs = [
        pltpu.make_async_copy(
            m_ref.at[pl.ds(c * tiles * SLOTS, tiles * SLOTS)],
            out_hbm.at[pl.ds(c * tiles * SLOTS, tiles * SLOTS)],
            sem_out.at[c],
        )
        for c in range(PARTS)
    ]
    ins[0].start()
    winds[0].start()
    winds[1].start()
    for c in range(1, PARTS):
        ins[c].start()
    b_ref[EXTRA:128, :] = jnp.zeros((128 - EXTRA, width), jnp.float32)
    for c in range(PARTS):
        ins[c].wait()
        if c == 0:
            winds[0].wait()
            winds[1].wait()
        b_ref[0 : LOCAL - MAIN, :] = x_ref[c, MAIN:LOCAL, :]
        for block in range(width // 128):
            cols = slice(block * 128, block * 128 + 128)
            at = c * (width // 128) + block
            for i in range(2):
                row = LOCAL - MAIN + i
                b_ref[row : row + 1, cols] = wind_ref[i, at : at + 1, :]
            z_ref[0, cols, :] = x_ref[c, 0:MAIN, cols].T
            z_ref[1, cols, :] = b_ref[:, cols].T
        first = c * tiles * SLOTS
        for k in range(SEND):
            m_ref[pl.ds(first + k, tiles, stride=SLOTS), :] = z_ref[
                0, pl.ds(k, tiles, stride=SEND), :
            ]
        for tile in range(SLOTS - SEND):
            total = None
            for k in range(tile * PER_TILE, min(SEND, (tile + 1) * PER_TILE)):
                piece = z_ref[1, pl.ds(k, tiles, stride=SEND), :]
                shift = (k % PER_TILE) * EXTRA
                piece = pltpu.roll(piece, shift, 1) if shift else piece
                total = piece if total is None else total + piece
            m_ref[pl.ds(first + SEND + tile, tiles, stride=SLOTS), :] = total
        outs[c].start()
    for c in range(PARTS):
        outs[c].wait()


def moments_kernel(r_ref, tab_ref, y_ref, wind_ref, e_ref):
    extra = None
    we = jnp.broadcast_to(tab_ref[:, W_E : W_E + 1], (ROWS, 128))
    wi = jnp.broadcast_to(tab_ref[:, W_I : W_I + 1], (ROWS, 128))
    for k in range(SEND):
        if k % PER_TILE == 0:
            extra = r_ref[pl.ds(SEND + k // PER_TILE, TILES, stride=SLOTS), :].T
        part = extra[(k % PER_TILE) * EXTRA : (k % PER_TILE + 1) * EXTRA, :]
        main = r_ref[pl.ds(k, TILES, stride=SLOTS), :].T
        y_ref[k, 0:MAIN, :] = main
        y_ref[k, MAIN:ROWS, :] = part
        wind_ref[k : k + 1, :] = part[LOCAL - MAIN : LOCAL - MAIN + 1, :]
        wind_ref[SEND + k : SEND + k + 1, :] = part[LOCAL - MAIN + 1 : EXTRA, :]
        y = y_ref[k]
        energy = jnp.sum(y * we, axis=0, keepdims=True)
        inverse = jnp.sum(y * wi, axis=0, keepdims=True)
        for g in range(GROUPS):
            e_ref[g, k : k + 1, :] = energy
            e_ref[g, SEND + k : SEND + k + 1, :] = inverse


def onehot_kernel(cell_ref, out_ref):
    row = lax.broadcasted_iota(jnp.int32, (16, 128), 0)
    base = row % 8 * 32 + row // 8
    spots = [cell_ref[k : k + 1, :] - base for k in range(SEND)]

    def body(e, carry):
        for phase in range(0, PHASES, 2):
            pack, short = phase // SHORT, phase % SHORT
            line = ((e // 4 * PACKS + pack) * 4 + e % 4) * SHORT * 8 + short * 8
            for k in range(SEND):
                hit = spots[k] == e * NY + phase
                out_ref[pl.ds(pl.multiple_of(line, 16), 16), k * 128 : (k + 1) * 128] = jnp.where(
                    hit, 1.0, 0.0
                ).astype(jnp.bfloat16)
        return carry

    lax.fori_loop(0, TROWS, body, 0)


def spread(held_ref, main, side, refs):
    turned = (((1,), (1,)), ((), ()))
    block = SHORT * 8
    out = lax.dot_general(held_ref[...], main, turned, preferred_element_type=jnp.float32)
    out = out[:, 0:128] + out[:, 128:256]
    rest = lax.dot_general(held_ref[...], side, turned, preferred_element_type=jnp.float32)
    rest = rest[:, 0:128] + rest[:, 128:256]
    lane = lax.broadcasted_iota(jnp.int32, (block, 128), 1)
    for i, (ref, at) in enumerate(refs):
        total = None
        for pack in range(PACKS):
            line = (pack * 4 + i) * block
            ref[at, pack * block : (pack + 1) * block, :] = out[line : line + block]
            part = rest[line : line + block]
            total = part if total is None else jnp.where(lane < pack * 32, total, part)
        ref[at, PHASES * 8 : LINES, :] = total


def place_kernel(y_ref, wind_ref, e_ref, tab_ref, hot_ref, up_ref, main_ref, side_ref, kept_ref,
                 s_ref, held_ref, sem):
    copies = [
        pltpu.make_async_copy(hot_ref.at[pl.ds(h * HALF, HALF)], ref, sem.at[h])
        for h, ref in enumerate((kept_ref, held_ref))
    ]
    copies[1].start()
    copies[0].start()
    moments = e_ref[0] + e_ref[1] + e_ref[2] + e_ref[3]
    energy, inverse = moments[0:SEND], moments[SEND : 2 * SEND]
    mean = energy / inverse
    wavenumber = mean * mean / GRAV
    steepness = energy * wavenumber * wavenumber
    ratio = steepness / (steepness + 0.02)
    decay = ratio / (mean * mean)
    speed, heading = wind_ref[0:SEND, :], wind_ref[SEND : 2 * SEND, :]
    along = speed * jnp.cos(heading)
    across = speed * jnp.sin(heading)
    ccos = jnp.broadcast_to(tab_ref[:, C_COS : C_COS + 1], (ROWS, 128))
    csin = jnp.broadcast_to(tab_ref[:, C_SIN : C_SIN + 1], (ROWS, 128))
    cout = jnp.broadcast_to(tab_ref[:, C_OUT : C_OUT + 1], (ROWS, 128))
    row = lax.broadcasted_iota(jnp.int32, (ROWS, 128), 0)
    s_ref[ROWS:DEPTH, :] = jnp.zeros((DEPTH - ROWS, SEA), jnp.float32)
    for k in range(SEND):
        grow = ccos * along[k : k + 1] + csin * across[k : k + 1]
        rate = jnp.maximum(grow - 0.1, 0.0) - cout * decay[k : k + 1]
        value = y_ref[k] * jnp.exp(rate)
        value = jnp.where(row < LOCAL, value, 0.0)
        s_ref[0:ROWS, k * 128 : (k + 1) * 128] = value
    value = s_ref[...]
    high = value.astype(jnp.bfloat16)
    rest = (value - high.astype(jnp.float32)).astype(jnp.bfloat16)
    main_ref[0:MAIN, :] = high[0:MAIN]
    main_ref[MAIN:256, :] = rest[0:MAIN]
    for pack in range(PACKS):
        side_ref[pack * 32 : pack * 32 + 32, :] = high[MAIN:DEPTH]
        side_ref[128 + pack * 32 : 128 + pack * 32 + 32, :] = rest[MAIN:DEPTH]
    copies[1].wait()
    spread(held_ref, main_ref[...], side_ref[...], [(up_ref, i) for i in range(4)])
    copies[0].wait()


def place_rest_kernel(main_ref, side_ref, kept_ref, low_ref, mid_ref):
    refs = [(low_ref, 0), (low_ref, 1), (mid_ref, 0), (mid_ref, 1)]
    spread(kept_ref, main_ref[...], side_ref[...], refs)


def limited(a, b):
    m = (a + (b + b)) * (1.0 / 6.0)
    least = jnp.minimum(jnp.maximum(a, b), 0.0)
    most = jnp.maximum(jnp.minimum(a, b), 0.0)
    return jnp.minimum(jnp.maximum(m, least), most)


def next_main(x):
    return pltpu.roll(x, 7, 0)


def last_main(x):
    return pltpu.roll(x, 1, 0)


def next_side(x):
    lane = lax.broadcasted_iota(jnp.int32, (8, 128), 1)
    x = pltpu.roll(x, 96, 1)
    return jnp.where(lane >= 96, pltpu.roll(x, 7, 0), x)


def last_side(x):
    lane = lax.broadcasted_iota(jnp.int32, (8, 128), 1)
    x = pltpu.roll(x, 32, 1)
    return jnp.where(lane < 32, pltpu.roll(x, 1, 0), x)


def substep(rows, seas, put, keep_ref, coef, base, phases, after, before):
    ux, kx, uy, ky = coef
    count = len(rows) - 3

    def load(spot, phase):
        ref, at = spot
        return ref[at, pl.ds(pl.multiple_of(base + phase * 8, 8), 8), :]

    for i in range(count):
        spot = rows[i + 2]
        end = load(spot, phases - 1)
        ahead = load(spot, 0) - before(end)
        prior = before(end - load(spot, phases - 2))
        keep_ref[i, 0] = ahead
        keep_ref[i, 1] = uy * before(end) + ky * limited(prior, ahead)

    def body(chunk, carry):
        first = chunk * CHUNK
        following = jnp.where(first + CHUNK == phases, 0, first + CHUNK)
        wraps = first + CHUNK == phases
        q = [load(rows[1], first + j) for j in range(CHUNK)]
        diff = [q[j] - load(rows[0], first + j) for j in range(CHUNK)]
        flux = None
        for i in range(-1, count):
            up = [load(rows[i + 3], first + j) for j in range(CHUNK)]
            slope = [up[j] - q[j] for j in range(CHUNK)]
            gone = [ux * q[j] + kx * limited(diff[j], slope[j]) for j in range(CHUNK)]
            if i >= 0:
                behind, past = keep_ref[i, 0], keep_ref[i, 1]
                edge = load(rows[i + 2], following)
                edge = jnp.where(wraps, after(edge), edge)
                for j in range(CHUNK):
                    ahead = (q[j + 1] if j + 1 < CHUNK else edge) - q[j]
                    side = uy * q[j] + ky * limited(behind, ahead)
                    new = q[j] - ((gone[j] - flux[j]) + (side - past))
                    sea = q[j] if seas is None else load(seas[i], first + j)
                    put(i, first + j, jnp.where(sea > 0.0, new, 0.0))
                    behind, past = ahead, side
                keep_ref[i, 0] = behind
                keep_ref[i, 1] = past
            q, diff, flux = up, slope, gone
        return carry

    lax.fori_loop(0, phases // CHUNK, body, 0)


def halves(tab_ref):
    for base, phases, lanes, after, before in (
        (0, PHASES, 0, next_main, last_main),
        (PHASES * 8, SHORT, 128, next_side, last_side),
    ):
        coef = [
            jnp.broadcast_to(tab_ref[n : n + 1, lanes : lanes + 128], (8, 128)) for n in range(4)
        ]
        yield coef, base, phases, after, before


def writer(ref, base, offset):
    def put(i, phase, value):
        ref[i + offset, pl.ds(pl.multiple_of(base + phase * 8, 8), 8), :] = value

    return put


def last_writer(ref, base, offset, cols_back):
    def put(i, phase, value):
        if base == 0:
            phase = phase + (PHASES - 1 - 2 * phase) * cols_back
        line = (i + offset) * LINES + base + phase * 8
        ref[pl.ds(pl.multiple_of(line, 8), 8), :] = value

    return put


def inner_kernel(flag_ref, tab_ref, low_ref, mid_ref, up_ref, once_ref, twice_ref, keep_ref):
    cells = [(low_ref, 0), (low_ref, 1), (mid_ref, 0), (mid_ref, 1)]
    cells += [(up_ref, i) for i in range(4)]
    once = [(once_ref, i) for i in range(5)]
    for half in halves(tab_ref):
        base = half[1]
        substep(cells, None, writer(once_ref, base, 0), keep_ref, *half)
        put = last_writer(twice_ref, base, 0, flag_ref[1])
        substep(once, cells[4:6], put, keep_ref, *half)


def outer_kernel(flag_ref, tab_ref, below_ref, low_ref, mid_ref, up_ref, above_ref, inner_ref,
                 inner_twice_ref, out_ref, once_ref, twice_ref, keep_ref, turn_ref, rest_ref):
    cells = [(below_ref, i) for i in range(4)] + [(low_ref, i) for i in range(2)]
    cells += [(mid_ref, i) for i in range(2)] + [(up_ref, i) for i in range(4)]
    cells += [(above_ref, i) for i in range(2)]
    once = [(once_ref, i) for i in range(4)] + [(inner_ref, i) for i in range(5)]
    once += [(once_ref, i) for i in range(4, 6)]
    rows_back = flag_ref[0]
    cols_back = flag_ref[1]
    for half in halves(tab_ref):
        base = half[1]
        substep(cells[0:7], None, writer(once_ref, base, 0), keep_ref, *half)
        substep(cells[9:14], None, writer(once_ref, base, 4), keep_ref, *half)
        put = last_writer(twice_ref, base, 0, cols_back)
        substep(once[0:7], cells[4:8], put, keep_ref, *half)
        put = last_writer(twice_ref, base, 4, cols_back)
        substep(once[6:11], cells[10:12], put, keep_ref, *half)

    where = [(twice_ref, i) for i in range(4)] + [(inner_twice_ref, i) for i in range(2)]
    where += [(twice_ref, i) for i in range(4, 6)]
    for e, (ref, at) in enumerate(where):
        r = e + (TROWS - 1 - 2 * e) * rows_back
        for half in range(2):
            parts = []
            for s in range(half * 4, half * 4 + 4):
                start = at * LINES + s + (7 - 2 * s) * cols_back
                parts.append(ref[pl.ds(start, PHASES, stride=8), :])
            block = jnp.concatenate(parts, axis=0).T
            turn_ref[half, pl.ds(r, MAIN, stride=TROWS), :] = block
        line = at * LINES + PHASES * 8
        block = jnp.concatenate(
            [ref[line : line + SHORT * 8, :], jnp.zeros((128 - SHORT * 8, 128), jnp.float32)],
            axis=0,
        ).T
        for pack in range(PACKS):
            rest_ref[pack, pl.ds(r, 32, stride=TROWS), :] = block[pack * 32 : pack * 32 + 32]
    spot = lax.broadcasted_iota(jnp.int32, (PACKS * 128, NY), 0)
    col = lax.broadcasted_iota(jnp.int32, (PACKS * 128, NY), 1)
    col = col + (NY - 1 - 2 * col) * cols_back
    pack, inner = spot // 128, spot % 128
    wanted = inner % 8 * 32 + pack * SHORT + inner // 8
    order = jnp.where((wanted == col) & (inner < SHORT * 8), 1.0, 0.0).astype(jnp.bfloat16)
    value = jnp.concatenate([rest_ref[pack] for pack in range(PACKS)], axis=1)
    high = value.astype(jnp.bfloat16)
    rest = (value - high.astype(jnp.float32)).astype(jnp.bfloat16)
    value = jnp.dot(high, order, preferred_element_type=jnp.float32)
    value = value + jnp.dot(rest, order, preferred_element_type=jnp.float32)
    for i in range(LOCAL - MAIN):
        out_ref[MAIN + i] = value[i * TROWS : (i + 1) * TROWS, :]
    for i in range(MAIN):
        for half in range(2):
            out_ref[i, :, half * 128 : half * 128 + 128] = turn_ref[
                half, i * TROWS : (i + 1) * TROWS, :
            ]


def call(kernel, shapes, scratch, ins, *args, limit=20, us=0, outs=None):
    cost = pl.CostEstimate(flops=us * 10**9, bytes_accessed=us * 3 * 10**6, transcendentals=0)
    return pl.pallas_call(
        kernel,
        out_shape=shapes,
        in_specs=ins,
        out_specs=outs or jax.tree.map(lambda _: VMEM, shapes),
        scratch_shapes=scratch,
        cost_estimate=cost if us else None,
        compiler_params=pltpu.CompilerParams(vmem_limit_bytes=limit * 1024 * 1024),
    )(*args)


def f32(*shape):
    return jax.ShapeDtypeStruct(shape, jnp.float32)


def local(spectra, wind_speed, wind_dir, sea_cell):
    group = lax.axis_index("grp")
    table, courant = (
        lax.dynamic_index_in_dim(jnp.asarray(t), group, 0, keepdims=False)
        for t in coefficient_tables()
    )
    mirror_x = ((group == 1) | (group == 2)).astype(jnp.int32)
    mirror_y = (group >= 2).astype(jnp.int32)
    flags = jnp.stack([mirror_x, mirror_y])
    hbm = pl.BlockSpec(memory_space=pltpu.HBM)
    packed = call(
        pack_kernel,
        f32(TILES * SLOTS, 128),
        [
            pltpu.VMEM((PARTS, LOCAL, SEA // PARTS), jnp.float32),
            pltpu.VMEM((2, SEA // 128, 128), jnp.float32),
            pltpu.VMEM((2, SEA // PARTS, 128), jnp.float32),
            pltpu.VMEM((128, SEA // PARTS), jnp.float32),
            pltpu.VMEM((TILES * SLOTS, 128), jnp.float32),
            pltpu.SemaphoreType.DMA((PARTS,)),
            pltpu.SemaphoreType.DMA((2,)),
            pltpu.SemaphoreType.DMA((PARTS,)),
        ],
        [hbm] * 3,
        spectra,
        wind_speed.reshape(SEA // 128, 128),
        wind_dir.reshape(SEA // 128, 128),
        limit=57,
        outs=hbm,
    )
    received = lax.all_to_all(
        packed.reshape(TILES, 1, SLOTS * 128), "comp", split_axis=0, concat_axis=0, tiled=True
    ).reshape(TILES * SLOTS, 128)
    cells = sea_cell.reshape(TILES, SEND).T
    cells = cells ^ (mirror_x * (NY * (TROWS - 1)) + mirror_y * (NY - 1))
    hot = call(
        onehot_kernel,
        jax.ShapeDtypeStruct((TROWS * NY, SEA), jnp.bfloat16),
        [],
        [VMEM],
        cells,
    )
    received, hot = lax.optimization_barrier((received, hot))
    points, wind_here, partial = call(
        moments_kernel,
        (f32(SEND, ROWS, 128), f32(2 * SEND, 128), f32(GROUPS, 2 * SEND, 128)),
        [],
        [VMEM] * 2,
        received,
        table,
    )
    partial = lax.all_to_all(partial, "grp", split_axis=0, concat_axis=0, tiled=True)
    bf16 = functools.partial(jax.ShapeDtypeStruct, dtype=jnp.bfloat16)
    up, main, side, kept = call(
        place_kernel,
        (f32(4, LINES, 128), bf16((256, SEA)), bf16((256, SEA)), bf16((HALF, SEA))),
        [
            pltpu.VMEM((DEPTH, SEA), jnp.float32),
            pltpu.VMEM((HALF, SEA), jnp.bfloat16),
            pltpu.SemaphoreType.DMA((2,)),
        ],
        [VMEM] * 4 + [hbm],
        points,
        wind_here,
        partial,
        table,
        hot,
        limit=44,
    )
    low, mid = call(
        place_rest_kernel,
        (f32(2, LINES, 128), f32(2, LINES, 128)),
        [],
        [VMEM] * 3,
        main,
        side,
        kept,
        us=2,
    )
    ahead, back = [], []
    for g in range(GROUPS):
        for i in range(TILES - 1):
            rise, fall = (g * TILES + i, g * TILES + i + 1), (g * TILES + i + 1, g * TILES + i)
            ahead.append(fall if g in (1, 2) else rise)
            back.append(rise if g in (1, 2) else fall)
    below = lax.ppermute(up, ("grp", "comp"), ahead)
    above = lax.ppermute(low, ("grp", "comp"), back)
    once, twice = call(
        inner_kernel,
        (f32(5, LINES, 128), f32(2 * LINES, 128)),
        [pltpu.VMEM((5, 2, 8, 128), jnp.float32)],
        [SMEM] + [VMEM] * 4,
        flags,
        courant,
        low,
        mid,
        up,
        us=3,
    )
    return call(
        outer_kernel,
        f32(LOCAL, TROWS, NY),
        [
            pltpu.VMEM((6, LINES, 128), jnp.float32),
            pltpu.VMEM((6 * LINES, 128), jnp.float32),
            pltpu.VMEM((4, 2, 8, 128), jnp.float32),
            pltpu.VMEM((2, MAIN * TROWS, 128), jnp.float32),
            pltpu.VMEM((PACKS, 32 * TROWS, 128), jnp.float32),
        ],
        [SMEM] + [VMEM] * 8,
        flags,
        courant,
        below,
        low,
        mid,
        up,
        above,
        once,
        twice,
    )


def solution(mesh):
    in_specs = (P("grp", "comp"), P("comp"), P("comp"), P("comp"))
    out_specs = P("grp", "comp", None)
    return jax.shard_map(local, mesh=mesh, in_specs=in_specs, out_specs=out_specs, check_vma=False)
```

```python
import functools
import math

import jax
import jax.numpy as jnp
import numpy as np
from jax import lax
from jax.experimental import pallas as pl
from jax.experimental.pallas import tpu as pltpu
from jax.sharding import PartitionSpec as P

DIRS = 24
FREQ = 25
TROWS = 8
NY = 256
SEA = 1536
SEND = 12
GROUPS = 4
TILES = 128
LOCAL = DIRS * FREQ // GROUPS
ROWS = 152
DEPTH = 160
MAIN = 128
EXTRA = ROWS - MAIN
PER_TILE = 5
SLOTS = 15
GRAV = 9.81
LOW_FREQ = 0.0418
FREQ_STEP = 1.1

VMEM = pl.BlockSpec(memory_space=pltpu.VMEM)
SMEM = pl.BlockSpec(memory_space=pltpu.SMEM)

W_E, W_I, C_COS, C_SIN, C_OUT = range(5)
PHASES = 32
PACKS = 4
SHORT = PHASES // PACKS
LINES = (PHASES + SHORT) * 8
CHUNK = 4
PAD = 8
PARTS = 4
HALF = TROWS * NY // 2


def coefficient_tables():
    table = np.zeros((GROUPS, ROWS, 128), np.float64)
    courant = np.zeros((GROUPS, 8, 256), np.float64)
    for group in range(GROUPS):
        for row in range(LOCAL):
            d, j = row // FREQ + group * (DIRS // GROUPS), row % FREQ
            angle = 2.0 * math.pi * (d + 0.5) / DIRS
            freq = LOW_FREQ * FREQ_STEP**j
            s = 2.0 * math.pi * freq
            w = 2.0 * math.pi / DIRS * 0.1 * freq
            reach = 0.45 * (2.0 * math.pi * LOW_FREQ) / s
            ux, uy = abs(reach * math.cos(angle)), abs(reach * math.sin(angle))
            push = 0.1 * 28.0 * 0.035 * s / GRAV
            table[group, row, :5] = (
                w, w / s, push * math.cos(angle), push * math.sin(angle), 0.4 * s * s
            )
            if row < MAIN:
                lanes = [row]
            else:
                lanes = [128 + pack * 32 + row - MAIN for pack in range(PACKS)]
            for lane in lanes:
                courant[group, :4, lane] = (ux, ux * (1.0 - ux), uy, uy * (1.0 - uy))
    return table.astype(np.float32), courant.astype(np.float32)


def pack_kernel(x_hbm, speed_hbm, heading_hbm, out_hbm, x_ref, wind_ref, z_ref, b_ref, m_ref,
                sem_in, sem_wind, sem_out):
    width = SEA // PARTS
    tiles = TILES // PARTS
    ins = [
        pltpu.make_async_copy(x_hbm.at[:, pl.ds(c * width, width)], x_ref.at[c], sem_in.at[c])
        for c in range(PARTS)
    ]
    winds = [
        pltpu.make_async_copy(ref, wind_ref.at[i], sem_wind.at[i])
        for i, ref in enumerate((speed_hbm, heading_hbm))
    ]
    outs = [
        pltpu.make_async_copy(
            m_ref.at[pl.ds(c * tiles * SLOTS, tiles * SLOTS)],
            out_hbm.at[pl.ds(c * tiles * SLOTS, tiles * SLOTS)],
            sem_out.at[c],
        )
        for c in range(PARTS)
    ]
    ins[0].start()
    winds[0].start()
    winds[1].start()
    for c in range(1, PARTS):
        ins[c].start()
    b_ref[EXTRA:128, :] = jnp.zeros((128 - EXTRA, width), jnp.float32)
    for c in range(PARTS):
        ins[c].wait()
        if c == 0:
            winds[0].wait()
            winds[1].wait()
        b_ref[0 : LOCAL - MAIN, :] = x_ref[c, MAIN:LOCAL, :]
        for block in range(width // 128):
            cols = slice(block * 128, block * 128 + 128)
            at = c * (width // 128) + block
            for i in range(2):
                row = LOCAL - MAIN + i
                b_ref[row : row + 1, cols] = wind_ref[i, at : at + 1, :]
            z_ref[0, cols, :] = x_ref[c, 0:MAIN, cols].T
            z_ref[1, cols, :] = b_ref[:, cols].T
        first = c * tiles * SLOTS
        for k in range(SEND):
            m_ref[pl.ds(first + k, tiles, stride=SLOTS), :] = z_ref[
                0, pl.ds(k, tiles, stride=SEND), :
            ]
        for tile in range(SLOTS - SEND):
            total = None
            for k in range(tile * PER_TILE, min(SEND, (tile + 1) * PER_TILE)):
                piece = z_ref[1, pl.ds(k, tiles, stride=SEND), :]
                shift = (k % PER_TILE) * EXTRA
                piece = pltpu.roll(piece, shift, 1) if shift else piece
                total = piece if total is None else total + piece
            m_ref[pl.ds(first + SEND + tile, tiles, stride=SLOTS), :] = total
        outs[c].start()
    for c in range(PARTS):
        outs[c].wait()


def moments_kernel(r_ref, tab_ref, y_ref, wind_ref, e_ref):
    extra = None
    we = jnp.broadcast_to(tab_ref[:, W_E : W_E + 1], (ROWS, 128))
    wi = jnp.broadcast_to(tab_ref[:, W_I : W_I + 1], (ROWS, 128))
    for k in range(SEND):
        if k % PER_TILE == 0:
            extra = r_ref[pl.ds(SEND + k // PER_TILE, TILES, stride=SLOTS), :].T
        part = extra[(k % PER_TILE) * EXTRA : (k % PER_TILE + 1) * EXTRA, :]
        main = r_ref[pl.ds(k, TILES, stride=SLOTS), :].T
        y_ref[k, 0:MAIN, :] = main
        y_ref[k, MAIN:ROWS, :] = part
        wind_ref[k : k + 1, :] = part[LOCAL - MAIN : LOCAL - MAIN + 1, :]
        wind_ref[SEND + k : SEND + k + 1, :] = part[LOCAL - MAIN + 1 : EXTRA, :]
        y = y_ref[k]
        energy = jnp.sum(y * we, axis=0, keepdims=True)
        inverse = jnp.sum(y * wi, axis=0, keepdims=True)
        for g in range(GROUPS):
            e_ref[g, k : k + 1, :] = energy
            e_ref[g, SEND + k : SEND + k + 1, :] = inverse


def onehot_kernel(cell_ref, out_ref):
    row = lax.broadcasted_iota(jnp.int32, (16, 128), 0)
    base = row % 8 * 32 + row // 8
    spots = [cell_ref[k : k + 1, :] - base for k in range(SEND)]

    def body(e, carry):
        for phase in range(0, PHASES, 2):
            pack, short = phase // SHORT, phase % SHORT
            line = ((e // 4 * PACKS + pack) * 4 + e % 4) * SHORT * 8 + short * 8
            for k in range(SEND):
                hit = spots[k] == e * NY + phase
                out_ref[pl.ds(pl.multiple_of(line, 16), 16), k * 128 : (k + 1) * 128] = jnp.where(
                    hit, 1.0, 0.0
                ).astype(jnp.bfloat16)
        return carry

    lax.fori_loop(0, TROWS, body, 0)


def spread(held_ref, main, side, ref):
    turned = (((1,), (1,)), ((), ()))
    block = SHORT * 8
    out = lax.dot_general(held_ref[...], main, turned, preferred_element_type=jnp.float32)
    out = out[:, 0:128] + out[:, 128:256]
    rest = lax.dot_general(held_ref[...], side, turned, preferred_element_type=jnp.float32)
    rest = rest[:, 0:128] + rest[:, 128:256]
    lane = lax.broadcasted_iota(jnp.int32, (block, 128), 1)
    for i in range(4):
        total = None
        for pack in range(PACKS):
            line = (pack * 4 + i) * block
            ref[i, pack * block : (pack + 1) * block, :] = out[line : line + block]
            part = rest[line : line + block]
            total = part if total is None else jnp.where(lane < pack * 32, total, part)
        ref[i, PHASES * 8 : LINES, :] = total


def place_kernel(y_ref, wind_ref, e_ref, tab_ref, hot_ref, first_ref, main_ref, side_ref,
                 kept_ref, s_ref, held_ref, sem):
    copies = [
        pltpu.make_async_copy(hot_ref.at[pl.ds(h * HALF, HALF)], ref, sem.at[h])
        for h, ref in enumerate((held_ref, kept_ref))
    ]
    copies[0].start()
    copies[1].start()
    moments = e_ref[0] + e_ref[1] + e_ref[2] + e_ref[3]
    energy, inverse = moments[0:SEND], moments[SEND : 2 * SEND]
    mean = energy / inverse
    wavenumber = mean * mean / GRAV
    steepness = energy * wavenumber * wavenumber
    ratio = steepness / (steepness + 0.02)
    decay = ratio / (mean * mean)
    speed, heading = wind_ref[0:SEND, :], wind_ref[SEND : 2 * SEND, :]
    along = speed * jnp.cos(heading)
    across = speed * jnp.sin(heading)
    ccos = jnp.broadcast_to(tab_ref[:, C_COS : C_COS + 1], (ROWS, 128))
    csin = jnp.broadcast_to(tab_ref[:, C_SIN : C_SIN + 1], (ROWS, 128))
    cout = jnp.broadcast_to(tab_ref[:, C_OUT : C_OUT + 1], (ROWS, 128))
    row = lax.broadcasted_iota(jnp.int32, (ROWS, 128), 0)
    s_ref[ROWS:DEPTH, :] = jnp.zeros((DEPTH - ROWS, SEA), jnp.float32)
    for k in range(SEND):
        grow = ccos * along[k : k + 1] + csin * across[k : k + 1]
        rate = jnp.maximum(grow - 0.1, 0.0) - cout * decay[k : k + 1]
        value = y_ref[k] * jnp.exp(rate)
        value = jnp.where(row < LOCAL, value, 0.0)
        s_ref[0:ROWS, k * 128 : (k + 1) * 128] = value
    value = s_ref[...]
    high = value.astype(jnp.bfloat16)
    rest = (value - high.astype(jnp.float32)).astype(jnp.bfloat16)
    main_ref[0:MAIN, :] = high[0:MAIN]
    main_ref[MAIN:256, :] = rest[0:MAIN]
    for pack in range(PACKS):
        side_ref[pack * 32 : pack * 32 + 32, :] = high[MAIN:DEPTH]
        side_ref[128 + pack * 32 : 128 + pack * 32 + 32, :] = rest[MAIN:DEPTH]
    first_ref[:, LINES : LINES + PAD, :] = jnp.zeros((4, PAD, 128), jnp.float32)
    copies[0].wait()
    spread(held_ref, main_ref[...], side_ref[...], first_ref)
    copies[1].wait()


def place_rest_kernel(main_ref, side_ref, kept_ref, second_ref):
    spread(kept_ref, main_ref[...], side_ref[...], second_ref)


def limited(a, b):
    m = (a + (b + b)) * (1.0 / 6.0)
    least = jnp.minimum(jnp.maximum(a, b), 0.0)
    most = jnp.maximum(jnp.minimum(a, b), 0.0)
    return jnp.minimum(jnp.maximum(m, least), most)


def next_main(x):
    return pltpu.roll(x, 7, 0)


def last_main(x):
    return pltpu.roll(x, 1, 0)


def next_side(x):
    lane = lax.broadcasted_iota(jnp.int32, (8, 128), 1)
    x = pltpu.roll(x, 96, 1)
    return jnp.where(lane >= 96, pltpu.roll(x, 7, 0), x)


def last_side(x):
    lane = lax.broadcasted_iota(jnp.int32, (8, 128), 1)
    x = pltpu.roll(x, 32, 1)
    return jnp.where(lane < 32, pltpu.roll(x, 1, 0), x)


def substep(rows, seas, put, keep_ref, coef, base, phases, after, before):
    ux, kx, uy, ky = coef
    count = len(rows) - 3

    def load(spot, phase):
        ref, at = spot
        return ref[at, pl.ds(pl.multiple_of(base + phase * 8, 8), 8), :]

    for i in range(count):
        spot = rows[i + 2]
        end = load(spot, phases - 1)
        ahead = load(spot, 0) - before(end)
        prior = before(end - load(spot, phases - 2))
        keep_ref[i, 0] = ahead
        keep_ref[i, 1] = uy * before(end) + ky * limited(prior, ahead)

    def body(chunk, carry):
        first = chunk * CHUNK
        following = jnp.where(first + CHUNK == phases, 0, first + CHUNK)
        wraps = first + CHUNK == phases
        q = [load(rows[1], first + j) for j in range(CHUNK)]
        diff = [q[j] - load(rows[0], first + j) for j in range(CHUNK)]
        flux = None
        for i in range(-1, count):
            up = [load(rows[i + 3], first + j) for j in range(CHUNK)]
            slope = [up[j] - q[j] for j in range(CHUNK)]
            gone = [ux * q[j] + kx * limited(diff[j], slope[j]) for j in range(CHUNK)]
            if i >= 0:
                behind, past = keep_ref[i, 0], keep_ref[i, 1]
                edge = load(rows[i + 2], following)
                edge = jnp.where(wraps, after(edge), edge)
                for j in range(CHUNK):
                    ahead = (q[j + 1] if j + 1 < CHUNK else edge) - q[j]
                    side = uy * q[j] + ky * limited(behind, ahead)
                    new = q[j] - ((gone[j] - flux[j]) + (side - past))
                    sea = q[j] if seas is None else load(seas[i], first + j)
                    put(i, first + j, jnp.where(sea > 0.0, new, 0.0))
                    behind, past = ahead, side
                keep_ref[i, 0] = behind
                keep_ref[i, 1] = past
            q, diff, flux = up, slope, gone
        return carry

    lax.fori_loop(0, phases // CHUNK, body, 0)


def halves(tab_ref):
    for base, phases, lanes, after, before in (
        (0, PHASES, 0, next_main, last_main),
        (PHASES * 8, SHORT, 128, next_side, last_side),
    ):
        coef = [
            jnp.broadcast_to(tab_ref[n : n + 1, lanes : lanes + 128], (8, 128)) for n in range(4)
        ]
        yield coef, base, phases, after, before


def writer(ref, base, offset):
    def put(i, phase, value):
        ref[i + offset, pl.ds(pl.multiple_of(base + phase * 8, 8), 8), :] = value

    return put


def last_writer(ref, base, offset, cols_back):
    def put(i, phase, value):
        if base == 0:
            phase = phase + (PHASES - 1 - 2 * phase) * cols_back
        line = (i + offset) * LINES + base + phase * 8
        ref[pl.ds(pl.multiple_of(line, 8), 8), :] = value

    return put


def field(flip, first_ref, second_ref):
    parts = (second_ref, first_ref) if flip else (first_ref, second_ref)
    return [(ref, i) for ref in parts for i in range(4)]


def turned_main(ref, at, half, cols_back):
    parts = []
    for s in range(half * 4, half * 4 + 4):
        start = at * LINES + s + (7 - 2 * s) * cols_back
        parts.append(ref[pl.ds(start, PHASES, stride=8), :])
    return jnp.concatenate(parts, axis=0).T


def turned_side(ref, at):
    line = at * LINES + PHASES * 8
    empty = jnp.zeros((128 - SHORT * 8, 128), jnp.float32)
    return jnp.concatenate([ref[line : line + SHORT * 8, :], empty], axis=0).T


def inner_kernel(flag_ref, tab_ref, first_ref, second_ref, once_ref, done_ref, twice_ref, keep_ref):
    once = [(once_ref, i) for i in range(5)]
    for flip in range(2):

        @pl.when(flag_ref[2] == flip)
        def _():
            cells = field(flip, first_ref, second_ref)
            for half in halves(tab_ref):
                base = half[1]
                substep(cells, None, writer(once_ref, base, 0), keep_ref, *half)
                put = last_writer(twice_ref, base, 0, flag_ref[1])
                substep(once, cells[4:6], put, keep_ref, *half)

    for i in range(2):
        done_ref[i, 0] = turned_main(twice_ref, i, 0, flag_ref[1])
        done_ref[i, 1] = turned_main(twice_ref, i, 1, flag_ref[1])
        done_ref[i, 2] = turned_side(twice_ref, i)


def outer_kernel(flag_ref, tab_ref, first_ref, second_ref, got_first_ref, got_second_ref, inner_ref,
                 done_ref, out_hbm, once_ref, twice_ref, keep_ref, turn_ref, rest_ref, last_ref,
                 sem):
    once = [(once_ref, i) for i in range(4)] + [(inner_ref, i) for i in range(5)]
    once += [(once_ref, i) for i in range(4, 6)]
    rows_back = flag_ref[0]
    cols_back = flag_ref[1]
    where = [(0, 0), (1, 1), (2, 2), (3, 3), (4, None), (5, None), (6, 4), (7, 5)]

    def compute(half):
        base = half[1]
        for flip in range(2):

            @pl.when(flag_ref[2] == flip)
            def _():
                below, above = got_first_ref, got_second_ref
                if flip:
                    below, above = above, below
                cells = [(below, i) for i in range(4)] + field(flip, first_ref, second_ref)
                cells += [(above, i) for i in range(2)]
                substep(cells[0:7], None, writer(once_ref, base, 0), keep_ref, *half)
                substep(cells[9:14], None, writer(once_ref, base, 4), keep_ref, *half)
                put = last_writer(twice_ref, base, 0, cols_back)
                substep(once[0:7], cells[4:8], put, keep_ref, *half)
                put = last_writer(twice_ref, base, 4, cols_back)
                substep(once[6:11], cells[10:12], put, keep_ref, *half)

    main, side = halves(tab_ref)
    copies = [
        pltpu.make_async_copy(
            turn_ref.at[half],
            out_hbm.at[pl.ds(0, MAIN), :, pl.ds(half * 128, 128)],
            sem.at[half],
        )
        for half in range(2)
    ]
    count = LOCAL - MAIN
    copies.append(
        pltpu.make_async_copy(
            last_ref.at[pl.ds(0, count)], out_hbm.at[pl.ds(MAIN, count)], sem.at[2]
        )
    )
    compute(main)
    for half in range(2):
        lines = turn_ref.at[half].reshape(MAIN * TROWS, 128)
        for e, at in where:
            r = e + (TROWS - 1 - 2 * e) * rows_back
            block = done_ref[e - 4, half]
            if at is not None:
                block = turned_main(twice_ref, at, half, cols_back)
            lines[pl.ds(r, MAIN, stride=TROWS), :] = block
        copies[half].start()
    compute(side)
    for e, at in where:
        r = e + (TROWS - 1 - 2 * e) * rows_back
        block = done_ref[e - 4, 2] if at is None else turned_side(twice_ref, at)
        for pack in range(PACKS):
            rest_ref[pack, pl.ds(r, 32, stride=TROWS), :] = block[pack * 32 : pack * 32 + 32]
    spot = lax.broadcasted_iota(jnp.int32, (PACKS * 128, NY), 0)
    col = lax.broadcasted_iota(jnp.int32, (PACKS * 128, NY), 1)
    col = col + (NY - 1 - 2 * col) * cols_back
    pack, inner = spot // 128, spot % 128
    wanted = inner % 8 * 32 + pack * SHORT + inner // 8
    order = jnp.where((wanted == col) & (inner < SHORT * 8), 1.0, 0.0).astype(jnp.bfloat16)
    value = jnp.concatenate([rest_ref[pack] for pack in range(PACKS)], axis=1)
    high = value.astype(jnp.bfloat16)
    rest = (value - high.astype(jnp.float32)).astype(jnp.bfloat16)
    value = jnp.dot(high, order, preferred_element_type=jnp.float32)
    value = value + jnp.dot(rest, order, preferred_element_type=jnp.float32)
    for i in range(count):
        last_ref[i] = value[i * TROWS : (i + 1) * TROWS, :]
    copies[2].start()
    for copy in copies:
        copy.wait()


def call(kernel, shapes, scratch, ins, *args, limit=20, us=0, outs=None):
    cost = pl.CostEstimate(flops=us * 10**9, bytes_accessed=us * 3 * 10**6, transcendentals=0)
    return pl.pallas_call(
        kernel,
        out_shape=shapes,
        in_specs=ins,
        out_specs=outs or jax.tree.map(lambda _: VMEM, shapes),
        scratch_shapes=scratch,
        cost_estimate=cost if us else None,
        compiler_params=pltpu.CompilerParams(vmem_limit_bytes=limit * 1024 * 1024),
    )(*args)


def f32(*shape):
    return jax.ShapeDtypeStruct(shape, jnp.float32)


def local(spectra, wind_speed, wind_dir, sea_cell):
    group = lax.axis_index("grp")
    table, courant = (
        lax.dynamic_index_in_dim(jnp.asarray(t), group, 0, keepdims=False)
        for t in coefficient_tables()
    )
    mirror_x = ((group == 1) | (group == 2)).astype(jnp.int32)
    mirror_y = (group >= 2).astype(jnp.int32)
    odd = lax.axis_index("comp") % 2
    flip = (odd ^ mirror_x).astype(jnp.int32)
    flags = jnp.stack([mirror_x, mirror_y, flip])
    hbm = pl.BlockSpec(memory_space=pltpu.HBM)
    packed = call(
        pack_kernel,
        f32(TILES * SLOTS, 128),
        [
            pltpu.VMEM((PARTS, LOCAL, SEA // PARTS), jnp.float32),
            pltpu.VMEM((2, SEA // 128, 128), jnp.float32),
            pltpu.VMEM((2, SEA // PARTS, 128), jnp.float32),
            pltpu.VMEM((128, SEA // PARTS), jnp.float32),
            pltpu.VMEM((TILES * SLOTS, 128), jnp.float32),
            pltpu.SemaphoreType.DMA((PARTS,)),
            pltpu.SemaphoreType.DMA((2,)),
            pltpu.SemaphoreType.DMA((PARTS,)),
        ],
        [hbm] * 3,
        spectra,
        wind_speed.reshape(SEA // 128, 128),
        wind_dir.reshape(SEA // 128, 128),
        limit=57,
        outs=hbm,
    )
    received = lax.all_to_all(
        packed.reshape(TILES, 1, SLOTS * 128), "comp", split_axis=0, concat_axis=0, tiled=True
    ).reshape(TILES * SLOTS, 128)
    cells = sea_cell.reshape(TILES, SEND).T
    cells = cells ^ (mirror_x * (NY * (TROWS - 1)) + mirror_y * (NY - 1)) ^ (flip * (NY * TROWS // 2))
    hot = call(
        onehot_kernel,
        jax.ShapeDtypeStruct((TROWS * NY, SEA), jnp.bfloat16),
        [],
        [VMEM],
        cells,
    )
    received, hot = lax.optimization_barrier((received, hot))
    points, wind_here, partial = call(
        moments_kernel,
        (f32(SEND, ROWS, 128), f32(2 * SEND, 128), f32(GROUPS, 2 * SEND, 128)),
        [],
        [VMEM] * 2,
        received,
        table,
    )
    partial = lax.all_to_all(partial, "grp", split_axis=0, concat_axis=0, tiled=True)
    bf16 = functools.partial(jax.ShapeDtypeStruct, dtype=jnp.bfloat16)
    first, main, side, kept = call(
        place_kernel,
        (f32(4, LINES + PAD, 128), bf16((256, SEA)), bf16((256, SEA)), bf16((HALF, SEA))),
        [
            pltpu.VMEM((DEPTH, SEA), jnp.float32),
            pltpu.VMEM((HALF, SEA), jnp.bfloat16),
            pltpu.SemaphoreType.DMA((2,)),
        ],
        [VMEM] * 4 + [hbm],
        points,
        wind_here,
        partial,
        table,
        hot,
        limit=44,
    )
    second = call(
        place_rest_kernel,
        f32(4, LINES, 128),
        [],
        [VMEM] * 3,
        main,
        side,
        kept,
        us=2,
    )
    across, within = [], []
    for g in range(GROUPS):
        for i in range(TILES - 1):
            low, high = g * TILES + i, g * TILES + i + 1
            (across if i % 2 else within).extend([(low, high), (high, low)])
    got_first = lax.ppermute(first, ("grp", "comp"), across)
    got_second = lax.ppermute(second, ("grp", "comp"), within)
    once, done = call(
        inner_kernel,
        (f32(5, LINES, 128), f32(2, 3, 128, 128)),
        [pltpu.VMEM((2 * LINES, 128), jnp.float32), pltpu.VMEM((5, 2, 8, 128), jnp.float32)],
        [SMEM] + [VMEM] * 3,
        flags,
        courant,
        first,
        second,
        us=3,
    )
    return call(
        outer_kernel,
        f32(LOCAL, TROWS, NY),
        [
            pltpu.VMEM((6, LINES, 128), jnp.float32),
            pltpu.VMEM((6 * LINES, 128), jnp.float32),
            pltpu.VMEM((4, 2, 8, 128), jnp.float32),
            pltpu.VMEM((2, MAIN, TROWS, 128), jnp.float32),
            pltpu.VMEM((PACKS, 32 * TROWS, 128), jnp.float32),
            pltpu.VMEM((32, TROWS, NY), jnp.float32),
            pltpu.SemaphoreType.DMA((3,)),
        ],
        [SMEM] + [VMEM] * 7,
        flags,
        courant,
        first,
        second,
        got_first,
        got_second,
        once,
        done,
        outs=hbm,
    )


def solution(mesh):
    in_specs = (P("grp", "comp"), P("comp"), P("comp"), P("comp"))
    out_specs = P("grp", "comp", None)
    return jax.shard_map(local, mesh=mesh, in_specs=in_specs, out_specs=out_specs, check_vma=False)
```

```python
import functools
import math

import jax
import jax.numpy as jnp
import numpy as np
from jax import lax
from jax.experimental import pallas as pl
from jax.experimental.pallas import tpu as pltpu
from jax.sharding import PartitionSpec as P

DIRS = 24
FREQ = 25
TROWS = 8
NY = 256
SEA = 1536
SEND = 12
GROUPS = 4
TILES = 128
LOCAL = DIRS * FREQ // GROUPS
ROWS = 152
DEPTH = 160
MAIN = 128
EXTRA = ROWS - MAIN
PER_TILE = 5
SLOTS = 15
GRAV = 9.81
LOW_FREQ = 0.0418
FREQ_STEP = 1.1

VMEM = pl.BlockSpec(memory_space=pltpu.VMEM)
SMEM = pl.BlockSpec(memory_space=pltpu.SMEM)

W_E, W_I, C_COS, C_SIN, C_OUT = range(5)
PHASES = 32
PACKS = 4
SHORT = PHASES // PACKS
LINES = (PHASES + SHORT) * 8
CHUNK = 4
PAD = 8
PARTS = 4
HALF = TROWS * NY // 2


def coefficient_tables():
    table = np.zeros((GROUPS, ROWS, 128), np.float64)
    courant = np.zeros((GROUPS, 8, 256), np.float64)
    for group in range(GROUPS):
        for row in range(LOCAL):
            d, j = row // FREQ + group * (DIRS // GROUPS), row % FREQ
            angle = 2.0 * math.pi * (d + 0.5) / DIRS
            freq = LOW_FREQ * FREQ_STEP**j
            s = 2.0 * math.pi * freq
            w = 2.0 * math.pi / DIRS * 0.1 * freq
            reach = 0.45 * (2.0 * math.pi * LOW_FREQ) / s
            ux, uy = abs(reach * math.cos(angle)), abs(reach * math.sin(angle))
            push = 0.1 * 28.0 * 0.035 * s / GRAV
            table[group, row, :5] = (
                w, w / s, push * math.cos(angle), push * math.sin(angle), 0.4 * s * s
            )
            if row < MAIN:
                lanes = [row]
            else:
                lanes = [128 + pack * 32 + row - MAIN for pack in range(PACKS)]
            for lane in lanes:
                courant[group, :4, lane] = (ux, ux * (1.0 - ux), uy, uy * (1.0 - uy))
    return table.astype(np.float32), courant.astype(np.float32)


def pack_kernel(x_hbm, speed_hbm, heading_hbm, out_hbm, x_ref, wind_ref, z_ref, b_ref, m_ref,
                sem_in, sem_wind, sem_out):
    width = SEA // PARTS
    tiles = TILES // PARTS
    ins = [
        pltpu.make_async_copy(x_hbm.at[:, pl.ds(c * width, width)], x_ref.at[c], sem_in.at[c])
        for c in range(PARTS)
    ]
    winds = [
        pltpu.make_async_copy(ref, wind_ref.at[i], sem_wind.at[i])
        for i, ref in enumerate((speed_hbm, heading_hbm))
    ]
    outs = [
        pltpu.make_async_copy(
            m_ref.at[pl.ds(c * tiles * SLOTS, tiles * SLOTS)],
            out_hbm.at[pl.ds(c * tiles * SLOTS, tiles * SLOTS)],
            sem_out.at[c],
        )
        for c in range(PARTS)
    ]
    ins[0].start()
    winds[0].start()
    winds[1].start()
    for c in range(1, PARTS):
        ins[c].start()
    b_ref[EXTRA:128, :] = jnp.zeros((128 - EXTRA, width), jnp.float32)
    for c in range(PARTS):
        ins[c].wait()
        if c == 0:
            winds[0].wait()
            winds[1].wait()
        b_ref[0 : LOCAL - MAIN, :] = x_ref[c, MAIN:LOCAL, :]
        for block in range(width // 128):
            cols = slice(block * 128, block * 128 + 128)
            at = c * (width // 128) + block
            for i in range(2):
                row = LOCAL - MAIN + i
                b_ref[row : row + 1, cols] = wind_ref[i, at : at + 1, :]
            z_ref[0, cols, :] = x_ref[c, 0:MAIN, cols].T
            z_ref[1, cols, :] = b_ref[:, cols].T
        first = c * tiles * SLOTS
        for k in range(SEND):
            m_ref[pl.ds(first + k, tiles, stride=SLOTS), :] = z_ref[
                0, pl.ds(k, tiles, stride=SEND), :
            ]
        for tile in range(SLOTS - SEND):
            total = None
            for k in range(tile * PER_TILE, min(SEND, (tile + 1) * PER_TILE)):
                piece = z_ref[1, pl.ds(k, tiles, stride=SEND), :]
                shift = (k % PER_TILE) * EXTRA
                piece = pltpu.roll(piece, shift, 1) if shift else piece
                total = piece if total is None else total + piece
            m_ref[pl.ds(first + SEND + tile, tiles, stride=SLOTS), :] = total
        outs[c].start()
    for c in range(PARTS):
        outs[c].wait()


def moments_kernel(r_ref, tab_ref, y_ref, wind_ref, e_ref):
    extra = None
    we = jnp.broadcast_to(tab_ref[:, W_E : W_E + 1], (ROWS, 128))
    wi = jnp.broadcast_to(tab_ref[:, W_I : W_I + 1], (ROWS, 128))
    for k in range(SEND):
        if k % PER_TILE == 0:
            extra = r_ref[pl.ds(SEND + k // PER_TILE, TILES, stride=SLOTS), :].T
        part = extra[(k % PER_TILE) * EXTRA : (k % PER_TILE + 1) * EXTRA, :]
        main = r_ref[pl.ds(k, TILES, stride=SLOTS), :].T
        y_ref[k, 0:MAIN, :] = main
        y_ref[k, MAIN:ROWS, :] = part
        wind_ref[k : k + 1, :] = part[LOCAL - MAIN : LOCAL - MAIN + 1, :]
        wind_ref[SEND + k : SEND + k + 1, :] = part[LOCAL - MAIN + 1 : EXTRA, :]
        y = y_ref[k]
        energy = jnp.sum(y * we, axis=0, keepdims=True)
        inverse = jnp.sum(y * wi, axis=0, keepdims=True)
        for g in range(GROUPS):
            e_ref[g, k : k + 1, :] = energy
            e_ref[g, SEND + k : SEND + k + 1, :] = inverse


def onehot_kernel(cell_ref, out_ref):
    row = lax.broadcasted_iota(jnp.int32, (16, 128), 0)
    base = row % 8 * 32 + row // 8
    spots = [cell_ref[k : k + 1, :] - base for k in range(SEND)]

    def body(e, carry):
        for phase in range(0, PHASES, 2):
            pack, short = phase // SHORT, phase % SHORT
            line = ((e // 4 * PACKS + pack) * 4 + e % 4) * SHORT * 8 + short * 8
            for k in range(SEND):
                hit = spots[k] == e * NY + phase
                out_ref[pl.ds(pl.multiple_of(line, 16), 16), k * 128 : (k + 1) * 128] = jnp.where(
                    hit, 1.0, 0.0
                ).astype(jnp.bfloat16)
        return carry

    lax.fori_loop(0, TROWS, body, 0)


def spread(held_ref, main, side, ref):
    turned = (((1,), (1,)), ((), ()))
    block = SHORT * 8
    out = lax.dot_general(held_ref[...], main, turned, preferred_element_type=jnp.float32)
    out = out[:, 0:128] + out[:, 128:256]
    rest = lax.dot_general(held_ref[...], side, turned, preferred_element_type=jnp.float32)
    rest = rest[:, 0:128] + rest[:, 128:256]
    lane = lax.broadcasted_iota(jnp.int32, (block, 128), 1)
    for i in range(4):
        total = None
        for pack in range(PACKS):
            line = (pack * 4 + i) * block
            ref[i, pack * block : (pack + 1) * block, :] = out[line : line + block]
            part = rest[line : line + block]
            total = part if total is None else jnp.where(lane < pack * 32, total, part)
        ref[i, PHASES * 8 : LINES, :] = total


def place_kernel(y_ref, wind_ref, e_ref, tab_ref, hot_ref, first_ref, main_ref, side_ref,
                 kept_ref, s_ref, held_ref, sem):
    copies = [
        pltpu.make_async_copy(hot_ref.at[pl.ds(h * HALF, HALF)], ref, sem.at[h])
        for h, ref in enumerate((held_ref, kept_ref))
    ]
    copies[0].start()
    copies[1].start()
    moments = e_ref[0] + e_ref[1] + e_ref[2] + e_ref[3]
    energy, inverse = moments[0:SEND], moments[SEND : 2 * SEND]
    mean = energy / inverse
    wavenumber = mean * mean / GRAV
    steepness = energy * wavenumber * wavenumber
    ratio = steepness / (steepness + 0.02)
    decay = ratio / (mean * mean)
    speed, heading = wind_ref[0:SEND, :], wind_ref[SEND : 2 * SEND, :]
    along = speed * jnp.cos(heading)
    across = speed * jnp.sin(heading)
    ccos = jnp.broadcast_to(tab_ref[:, C_COS : C_COS + 1], (ROWS, 128))
    csin = jnp.broadcast_to(tab_ref[:, C_SIN : C_SIN + 1], (ROWS, 128))
    cout = jnp.broadcast_to(tab_ref[:, C_OUT : C_OUT + 1], (ROWS, 128))
    row = lax.broadcasted_iota(jnp.int32, (ROWS, 128), 0)
    s_ref[ROWS:DEPTH, :] = jnp.zeros((DEPTH - ROWS, SEA), jnp.float32)
    for k in range(SEND):
        grow = ccos * along[k : k + 1] + csin * across[k : k + 1]
        rate = jnp.maximum(grow - 0.1, 0.0) - cout * decay[k : k + 1]
        value = y_ref[k] * jnp.exp(rate)
        value = jnp.where(row < LOCAL, value, 0.0)
        s_ref[0:ROWS, k * 128 : (k + 1) * 128] = value
    value = s_ref[...]
    high = value.astype(jnp.bfloat16)
    rest = (value - high.astype(jnp.float32)).astype(jnp.bfloat16)
    main_ref[0:MAIN, :] = high[0:MAIN]
    main_ref[MAIN:256, :] = rest[0:MAIN]
    for pack in range(PACKS):
        side_ref[pack * 32 : pack * 32 + 32, :] = high[MAIN:DEPTH]
        side_ref[128 + pack * 32 : 128 + pack * 32 + 32, :] = rest[MAIN:DEPTH]
    first_ref[:, LINES : LINES + PAD, :] = jnp.zeros((4, PAD, 128), jnp.float32)
    copies[0].wait()
    spread(held_ref, main_ref[...], side_ref[...], first_ref)
    copies[1].wait()


def place_rest_kernel(main_ref, side_ref, kept_ref, second_ref):
    spread(kept_ref, main_ref[...], side_ref[...], second_ref)


def limited(a, b):
    m = (a + (b + b)) * (1.0 / 6.0)
    least = jnp.minimum(jnp.maximum(a, b), 0.0)
    most = jnp.maximum(jnp.minimum(a, b), 0.0)
    return jnp.minimum(jnp.maximum(m, least), most)


def next_main(x):
    return pltpu.roll(x, 7, 0)


def last_main(x):
    return pltpu.roll(x, 1, 0)


def next_side(x):
    lane = lax.broadcasted_iota(jnp.int32, (8, 128), 1)
    x = pltpu.roll(x, 96, 1)
    return jnp.where(lane >= 96, pltpu.roll(x, 7, 0), x)


def last_side(x):
    lane = lax.broadcasted_iota(jnp.int32, (8, 128), 1)
    x = pltpu.roll(x, 32, 1)
    return jnp.where(lane < 32, pltpu.roll(x, 1, 0), x)


def substep(rows, seas, put, keep_ref, coef, base, phases, after, before):
    ux, kx, uy, ky = coef
    count = len(rows) - 3

    def load(spot, phase):
        ref, at = spot
        return ref[at, pl.ds(pl.multiple_of(base + phase * 8, 8), 8), :]

    for i in range(count):
        spot = rows[i + 2]
        end = load(spot, phases - 1)
        ahead = load(spot, 0) - before(end)
        prior = before(end - load(spot, phases - 2))
        keep_ref[i, 0] = ahead
        keep_ref[i, 1] = uy * before(end) + ky * limited(prior, ahead)

    def body(chunk, carry):
        first = chunk * CHUNK
        following = jnp.where(first + CHUNK == phases, 0, first + CHUNK)
        wraps = first + CHUNK == phases
        q = [load(rows[1], first + j) for j in range(CHUNK)]
        diff = [q[j] - load(rows[0], first + j) for j in range(CHUNK)]
        flux = None
        for i in range(-1, count):
            up = [load(rows[i + 3], first + j) for j in range(CHUNK)]
            slope = [up[j] - q[j] for j in range(CHUNK)]
            gone = [ux * q[j] + kx * limited(diff[j], slope[j]) for j in range(CHUNK)]
            if i >= 0:
                behind, past = keep_ref[i, 0], keep_ref[i, 1]
                edge = load(rows[i + 2], following)
                edge = jnp.where(wraps, after(edge), edge)
                for j in range(CHUNK):
                    ahead = (q[j + 1] if j + 1 < CHUNK else edge) - q[j]
                    side = uy * q[j] + ky * limited(behind, ahead)
                    new = q[j] - ((gone[j] - flux[j]) + (side - past))
                    sea = q[j] if seas is None else load(seas[i], first + j)
                    put(i, first + j, jnp.where(sea > 0.0, new, 0.0))
                    behind, past = ahead, side
                keep_ref[i, 0] = behind
                keep_ref[i, 1] = past
            q, diff, flux = up, slope, gone
        return carry

    lax.fori_loop(0, phases // CHUNK, body, 0)


def halves(tab_ref):
    for base, phases, lanes, after, before in (
        (0, PHASES, 0, next_main, last_main),
        (PHASES * 8, SHORT, 128, next_side, last_side),
    ):
        coef = [
            jnp.broadcast_to(tab_ref[n : n + 1, lanes : lanes + 128], (8, 128)) for n in range(4)
        ]
        yield coef, base, phases, after, before


def writer(ref, base, offset):
    def put(i, phase, value):
        ref[i + offset, pl.ds(pl.multiple_of(base + phase * 8, 8), 8), :] = value

    return put


def last_writer(ref, base, offset, cols_back):
    def put(i, phase, value):
        if base == 0:
            phase = phase + (PHASES - 1 - 2 * phase) * cols_back
        line = (i + offset) * LINES + base + phase * 8
        ref[pl.ds(pl.multiple_of(line, 8), 8), :] = value

    return put


def field(flip, first_ref, second_ref):
    parts = (second_ref, first_ref) if flip else (first_ref, second_ref)
    return [(ref, i) for ref in parts for i in range(4)]


def turned_main(ref, at, half, cols_back):
    parts = []
    for s in range(half * 4, half * 4 + 4):
        start = at * LINES + s + (7 - 2 * s) * cols_back
        parts.append(ref[pl.ds(start, PHASES, stride=8), :])
    return jnp.concatenate(parts, axis=0).T


def turned_side(ref, at):
    line = at * LINES + PHASES * 8
    empty = jnp.zeros((128 - SHORT * 8, 128), jnp.float32)
    return jnp.concatenate([ref[line : line + SHORT * 8, :], empty], axis=0).T


def inner_kernel(flag_ref, tab_ref, first_ref, second_ref, once_ref, done_ref, twice_ref, keep_ref):
    once = [(once_ref, i) for i in range(5)]
    for flip in range(2):

        @pl.when(flag_ref[2] == flip)
        def _():
            cells = field(flip, first_ref, second_ref)
            for half in halves(tab_ref):
                base = half[1]
                substep(cells, None, writer(once_ref, base, 0), keep_ref, *half)
                put = last_writer(twice_ref, base, 0, flag_ref[1])
                substep(once, cells[4:6], put, keep_ref, *half)

    for i in range(2):
        done_ref[i, 0] = turned_main(twice_ref, i, 0, flag_ref[1])
        done_ref[i, 1] = turned_main(twice_ref, i, 1, flag_ref[1])
        done_ref[i, 2] = turned_side(twice_ref, i)


def edge(lower, cells, got_ref, inner_ref, once_ref, twice_ref, keep_ref, cols_back, half):
    base = half[1]
    once = [(inner_ref, i) for i in range(5)]
    if lower:
        near = [(got_ref, i) for i in range(4)] + cells[0:3]
        seas, fresh = cells[0:4], [(once_ref, i) for i in range(4)]
        once = fresh + once[0:3]
    else:
        near = cells[5:8] + [(got_ref, i) for i in range(2)]
        seas, fresh = cells[6:8], [(once_ref, i) for i in range(2)]
        once = once[2:5] + fresh
    substep(near, None, writer(once_ref, base, 0), keep_ref, *half)
    substep(once, seas, last_writer(twice_ref, base, 0, cols_back), keep_ref, *half)
    return len(seas)


def near_kernel(flag_ref, tab_ref, first_ref, second_ref, got_ref, inner_ref, done_ref, once_ref,
                twice_ref, keep_ref):
    cols_back = flag_ref[1]
    for flip in range(2):

        @pl.when(flag_ref[2] == flip)
        def _():
            cells = field(flip, first_ref, second_ref)
            for half in halves(tab_ref):
                count = edge(flip == 1, cells, got_ref, inner_ref, once_ref, twice_ref, keep_ref,
                             cols_back, half)
            for i in range(count):
                done_ref[i, 0] = turned_main(twice_ref, i, 0, cols_back)
                done_ref[i, 1] = turned_main(twice_ref, i, 1, cols_back)
                done_ref[i, 2] = turned_side(twice_ref, i)


def outer_kernel(flag_ref, tab_ref, first_ref, second_ref, got_ref, inner_ref, done_ref, near_ref,
                 out_hbm, once_ref, twice_ref, keep_ref, turn_ref, rest_ref, last_ref, sem):
    rows_back = flag_ref[0]
    cols_back = flag_ref[1]

    def blocks(flip, part):
        for e in range(TROWS):
            r = e + (TROWS - 1 - 2 * e) * rows_back
            if e in (4, 5):
                yield r, done_ref[e - 4, part]
                continue
            lower, at = e < 4, e if e < 4 else e - 6
            if lower == (flip == 1):
                yield r, near_ref[at, part]
            elif part == 2:
                yield r, turned_side(twice_ref, at)
            else:
                yield r, turned_main(twice_ref, at, part, cols_back)

    def compute(flip, half):
        cells = field(flip, first_ref, second_ref)
        edge(flip == 0, cells, got_ref, inner_ref, once_ref, twice_ref, keep_ref, cols_back, half)

    main, side = halves(tab_ref)
    copies = [
        pltpu.make_async_copy(
            turn_ref.at[half],
            out_hbm.at[pl.ds(0, MAIN), :, pl.ds(half * 128, 128)],
            sem.at[half],
        )
        for half in range(2)
    ]
    count = LOCAL - MAIN
    copies.append(
        pltpu.make_async_copy(
            last_ref.at[pl.ds(0, count)], out_hbm.at[pl.ds(MAIN, count)], sem.at[2]
        )
    )
    for flip in range(2):

        @pl.when(flag_ref[2] == flip)
        def _():
            compute(flip, main)
            for half in range(2):
                lines = turn_ref.at[half].reshape(MAIN * TROWS, 128)
                for r, block in blocks(flip, half):
                    lines[pl.ds(r, MAIN, stride=TROWS), :] = block

    copies[0].start()
    copies[1].start()
    for flip in range(2):

        @pl.when(flag_ref[2] == flip)
        def _():
            compute(flip, side)
            for r, block in blocks(flip, 2):
                for pack in range(PACKS):
                    rest_ref[pack, pl.ds(r, 32, stride=TROWS), :] = block[
                        pack * 32 : pack * 32 + 32
                    ]

    spot = lax.broadcasted_iota(jnp.int32, (PACKS * 128, NY), 0)
    col = lax.broadcasted_iota(jnp.int32, (PACKS * 128, NY), 1)
    col = col + (NY - 1 - 2 * col) * cols_back
    pack, inner = spot // 128, spot % 128
    wanted = inner % 8 * 32 + pack * SHORT + inner // 8
    order = jnp.where((wanted == col) & (inner < SHORT * 8), 1.0, 0.0).astype(jnp.bfloat16)
    value = jnp.concatenate([rest_ref[pack] for pack in range(PACKS)], axis=1)
    high = value.astype(jnp.bfloat16)
    rest = (value - high.astype(jnp.float32)).astype(jnp.bfloat16)
    value = jnp.dot(high, order, preferred_element_type=jnp.float32)
    value = value + jnp.dot(rest, order, preferred_element_type=jnp.float32)
    for i in range(count):
        last_ref[i] = value[i * TROWS : (i + 1) * TROWS, :]
    copies[2].start()
    for copy in copies:
        copy.wait()


def call(kernel, shapes, scratch, ins, *args, limit=20, us=0, outs=None):
    cost = pl.CostEstimate(flops=us * 10**9, bytes_accessed=us * 3 * 10**6, transcendentals=0)
    return pl.pallas_call(
        kernel,
        out_shape=shapes,
        in_specs=ins,
        out_specs=outs or jax.tree.map(lambda _: VMEM, shapes),
        scratch_shapes=scratch,
        cost_estimate=cost if us else None,
        compiler_params=pltpu.CompilerParams(vmem_limit_bytes=limit * 1024 * 1024),
    )(*args)


def f32(*shape):
    return jax.ShapeDtypeStruct(shape, jnp.float32)


def local(spectra, wind_speed, wind_dir, sea_cell):
    group = lax.axis_index("grp")
    table, courant = (
        lax.dynamic_index_in_dim(jnp.asarray(t), group, 0, keepdims=False)
        for t in coefficient_tables()
    )
    mirror_x = ((group == 1) | (group == 2)).astype(jnp.int32)
    mirror_y = (group >= 2).astype(jnp.int32)
    odd = lax.axis_index("comp") % 2
    flip = (odd ^ mirror_x).astype(jnp.int32)
    flags = jnp.stack([mirror_x, mirror_y, flip])
    hbm = pl.BlockSpec(memory_space=pltpu.HBM)
    packed = call(
        pack_kernel,
        f32(TILES * SLOTS, 128),
        [
            pltpu.VMEM((PARTS, LOCAL, SEA // PARTS), jnp.float32),
            pltpu.VMEM((2, SEA // 128, 128), jnp.float32),
            pltpu.VMEM((2, SEA // PARTS, 128), jnp.float32),
            pltpu.VMEM((128, SEA // PARTS), jnp.float32),
            pltpu.VMEM((TILES * SLOTS, 128), jnp.float32),
            pltpu.SemaphoreType.DMA((PARTS,)),
            pltpu.SemaphoreType.DMA((2,)),
            pltpu.SemaphoreType.DMA((PARTS,)),
        ],
        [hbm] * 3,
        spectra,
        wind_speed.reshape(SEA // 128, 128),
        wind_dir.reshape(SEA // 128, 128),
        limit=57,
        outs=hbm,
    )
    received = lax.all_to_all(
        packed.reshape(TILES, 1, SLOTS * 128), "comp", split_axis=0, concat_axis=0, tiled=True
    ).reshape(TILES * SLOTS, 128)
    cells = sea_cell.reshape(TILES, SEND).T
    cells = cells ^ (mirror_x * (NY * (TROWS - 1)) + mirror_y * (NY - 1)) ^ (flip * (NY * TROWS // 2))
    hot = call(
        onehot_kernel,
        jax.ShapeDtypeStruct((TROWS * NY, SEA), jnp.bfloat16),
        [],
        [VMEM],
        cells,
    )
    received, hot = lax.optimization_barrier((received, hot))
    points, wind_here, partial = call(
        moments_kernel,
        (f32(SEND, ROWS, 128), f32(2 * SEND, 128), f32(GROUPS, 2 * SEND, 128)),
        [],
        [VMEM] * 2,
        received,
        table,
    )
    partial = lax.all_to_all(partial, "grp", split_axis=0, concat_axis=0, tiled=True)
    bf16 = functools.partial(jax.ShapeDtypeStruct, dtype=jnp.bfloat16)
    first, main, side, kept = call(
        place_kernel,
        (f32(4, LINES + PAD, 128), bf16((256, SEA)), bf16((256, SEA)), bf16((HALF, SEA))),
        [
            pltpu.VMEM((DEPTH, SEA), jnp.float32),
            pltpu.VMEM((HALF, SEA), jnp.bfloat16),
            pltpu.SemaphoreType.DMA((2,)),
        ],
        [VMEM] * 4 + [hbm],
        points,
        wind_here,
        partial,
        table,
        hot,
        limit=44,
    )
    second = call(
        place_rest_kernel,
        f32(4, LINES, 128),
        [],
        [VMEM] * 3,
        main,
        side,
        kept,
        us=2,
    )
    across, within = [], []
    for g in range(GROUPS):
        for i in range(TILES - 1):
            low, high = g * TILES + i, g * TILES + i + 1
            (across if i % 2 else within).extend([(low, high), (high, low)])
    got_first = lax.ppermute(first, ("grp", "comp"), across)
    got_second = lax.ppermute(second, ("grp", "comp"), within)
    once, done = call(
        inner_kernel,
        (f32(5, LINES, 128), f32(2, 3, 128, 128)),
        [pltpu.VMEM((2 * LINES, 128), jnp.float32), pltpu.VMEM((5, 2, 8, 128), jnp.float32)],
        [SMEM] + [VMEM] * 3,
        flags,
        courant,
        first,
        second,
        us=3,
    )
    near = call(
        near_kernel,
        f32(4, 3, 128, 128),
        [
            pltpu.VMEM((4, LINES, 128), jnp.float32),
            pltpu.VMEM((4 * LINES, 128), jnp.float32),
            pltpu.VMEM((4, 2, 8, 128), jnp.float32),
        ],
        [SMEM] + [VMEM] * 5,
        flags,
        courant,
        first,
        second,
        got_second,
        once,
        us=0,
    )
    return call(
        outer_kernel,
        f32(LOCAL, TROWS, NY),
        [
            pltpu.VMEM((4, LINES, 128), jnp.float32),
            pltpu.VMEM((4 * LINES, 128), jnp.float32),
            pltpu.VMEM((4, 2, 8, 128), jnp.float32),
            pltpu.VMEM((2, MAIN, TROWS, 128), jnp.float32),
            pltpu.VMEM((PACKS, 32 * TROWS, 128), jnp.float32),
            pltpu.VMEM((32, TROWS, NY), jnp.float32),
            pltpu.SemaphoreType.DMA((3,)),
        ],
        [SMEM] + [VMEM] * 7,
        flags,
        courant,
        first,
        second,
        got_first,
        once,
        done,
        near,
        outs=hbm,
    )


def solution(mesh):
    in_specs = (P("grp", "comp"), P("comp"), P("comp"), P("comp"))
    out_specs = P("grp", "comp", None)
    return jax.shard_map(local, mesh=mesh, in_specs=in_specs, out_specs=out_specs, check_vma=False)
```

```python
import functools
import math

import jax
import jax.numpy as jnp
import numpy as np
from jax import lax
from jax.experimental import pallas as pl
from jax.experimental.pallas import tpu as pltpu
from jax.sharding import PartitionSpec as P

DIRS = 24
FREQ = 25
TROWS = 8
NY = 256
SEA = 1536
SEND = 12
GROUPS = 4
TILES = 128
LOCAL = DIRS * FREQ // GROUPS
ROWS = 152
DEPTH = 160
MAIN = 128
EXTRA = ROWS - MAIN
PER_TILE = 5
SLOTS = 15
GRAV = 9.81
LOW_FREQ = 0.0418
FREQ_STEP = 1.1

VMEM = pl.BlockSpec(memory_space=pltpu.VMEM)
SMEM = pl.BlockSpec(memory_space=pltpu.SMEM)

W_E, W_I, C_COS, C_SIN, C_OUT = range(5)
PHASES = 32
PACKS = 4
SHORT = PHASES // PACKS
LINES = (PHASES + SHORT) * 8
CHUNK = 4
PAD = 8
PARTS = 4
HALF = TROWS * NY // 2


def coefficient_tables():
    table = np.zeros((GROUPS, ROWS, 128), np.float64)
    courant = np.zeros((GROUPS, 8, 256), np.float64)
    for group in range(GROUPS):
        for row in range(LOCAL):
            d, j = row // FREQ + group * (DIRS // GROUPS), row % FREQ
            angle = 2.0 * math.pi * (d + 0.5) / DIRS
            freq = LOW_FREQ * FREQ_STEP**j
            s = 2.0 * math.pi * freq
            w = 2.0 * math.pi / DIRS * 0.1 * freq
            reach = 0.45 * (2.0 * math.pi * LOW_FREQ) / s
            ux, uy = abs(reach * math.cos(angle)), abs(reach * math.sin(angle))
            push = 0.1 * 28.0 * 0.035 * s / GRAV
            table[group, row, :5] = (
                w, w / s, push * math.cos(angle), push * math.sin(angle), 0.4 * s * s
            )
            if row < MAIN:
                lanes = [row]
            else:
                lanes = [128 + pack * 32 + row - MAIN for pack in range(PACKS)]
            for lane in lanes:
                courant[group, :4, lane] = (ux, ux * (1.0 - ux), uy, uy * (1.0 - uy))
    return table.astype(np.float32), courant.astype(np.float32)


def pack_kernel(x_hbm, speed_hbm, heading_hbm, out_hbm, x_ref, wind_ref, z_ref, b_ref, m_ref,
                sem_in, sem_wind, sem_out):
    width = SEA // PARTS
    tiles = TILES // PARTS
    ins = [
        pltpu.make_async_copy(x_hbm.at[:, pl.ds(c * width, width)], x_ref.at[c], sem_in.at[c])
        for c in range(PARTS)
    ]
    winds = [
        pltpu.make_async_copy(ref, wind_ref.at[i], sem_wind.at[i])
        for i, ref in enumerate((speed_hbm, heading_hbm))
    ]
    outs = [
        pltpu.make_async_copy(
            m_ref.at[pl.ds(c * tiles * SLOTS, tiles * SLOTS)],
            out_hbm.at[pl.ds(c * tiles * SLOTS, tiles * SLOTS)],
            sem_out.at[c],
        )
        for c in range(PARTS)
    ]
    ins[0].start()
    winds[0].start()
    winds[1].start()
    for c in range(1, PARTS):
        ins[c].start()
    b_ref[EXTRA:128, :] = jnp.zeros((128 - EXTRA, width), jnp.float32)
    for c in range(PARTS):
        ins[c].wait()
        if c == 0:
            winds[0].wait()
            winds[1].wait()
        b_ref[0 : LOCAL - MAIN, :] = x_ref[c, MAIN:LOCAL, :]
        for block in range(width // 128):
            cols = slice(block * 128, block * 128 + 128)
            at = c * (width // 128) + block
            for i in range(2):
                row = LOCAL - MAIN + i
                b_ref[row : row + 1, cols] = wind_ref[i, at : at + 1, :]
            z_ref[0, cols, :] = x_ref[c, 0:MAIN, cols].T
            z_ref[1, cols, :] = b_ref[:, cols].T
        first = c * tiles * SLOTS
        for k in range(SEND):
            m_ref[pl.ds(first + k, tiles, stride=SLOTS), :] = z_ref[
                0, pl.ds(k, tiles, stride=SEND), :
            ]
        for tile in range(SLOTS - SEND):
            total = None
            for k in range(tile * PER_TILE, min(SEND, (tile + 1) * PER_TILE)):
                piece = z_ref[1, pl.ds(k, tiles, stride=SEND), :]
                shift = (k % PER_TILE) * EXTRA
                piece = pltpu.roll(piece, shift, 1) if shift else piece
                total = piece if total is None else total + piece
            m_ref[pl.ds(first + SEND + tile, tiles, stride=SLOTS), :] = total
        outs[c].start()
    for c in range(PARTS):
        outs[c].wait()


def moments_kernel(r_ref, tab_ref, y_ref, wind_ref, e_ref):
    extra = None
    we = jnp.broadcast_to(tab_ref[:, W_E : W_E + 1], (ROWS, 128))
    wi = jnp.broadcast_to(tab_ref[:, W_I : W_I + 1], (ROWS, 128))
    for k in range(SEND):
        if k % PER_TILE == 0:
            extra = r_ref[pl.ds(SEND + k // PER_TILE, TILES, stride=SLOTS), :].T
        part = extra[(k % PER_TILE) * EXTRA : (k % PER_TILE + 1) * EXTRA, :]
        main = r_ref[pl.ds(k, TILES, stride=SLOTS), :].T
        y_ref[k, 0:MAIN, :] = main
        y_ref[k, MAIN:ROWS, :] = part
        wind_ref[k : k + 1, :] = part[LOCAL - MAIN : LOCAL - MAIN + 1, :]
        wind_ref[SEND + k : SEND + k + 1, :] = part[LOCAL - MAIN + 1 : EXTRA, :]
        y = y_ref[k]
        energy = jnp.sum(y * we, axis=0, keepdims=True)
        inverse = jnp.sum(y * wi, axis=0, keepdims=True)
        for g in range(GROUPS):
            e_ref[g, k : k + 1, :] = energy
            e_ref[g, SEND + k : SEND + k + 1, :] = inverse


def onehot_kernel(cell_ref, out_ref):
    row = lax.broadcasted_iota(jnp.int32, (16, 128), 0)
    base = row % 8 * 32 + row // 8
    spots = [cell_ref[k : k + 1, :] - base for k in range(SEND)]

    def body(e, carry):
        for phase in range(0, PHASES, 2):
            pack, short = phase // SHORT, phase % SHORT
            line = ((e // 4 * PACKS + pack) * 4 + e % 4) * SHORT * 8 + short * 8
            for k in range(SEND):
                hit = spots[k] == e * NY + phase
                out_ref[pl.ds(pl.multiple_of(line, 16), 16), k * 128 : (k + 1) * 128] = jnp.where(
                    hit, 1.0, 0.0
                ).astype(jnp.bfloat16)
        return carry

    lax.fori_loop(0, TROWS, body, 0)


def spread(held_ref, main, side, ref, packs):
    turned = (((1,), (1,)), ((), ()))
    block = SHORT * 8
    hot = held_ref[packs[0] * 4 * block : (packs[-1] + 1) * 4 * block, :]
    out = lax.dot_general(hot, main, turned, preferred_element_type=jnp.float32)
    out = out[:, 0:128] + out[:, 128:256]
    rest = lax.dot_general(hot, side, turned, preferred_element_type=jnp.float32)
    rest = rest[:, 0:128] + rest[:, 128:256]
    lane = lax.broadcasted_iota(jnp.int32, (block, 128), 1)
    for i in range(4):
        total = ref[i, PHASES * 8 : LINES, :] if packs[0] else None
        for pack in packs:
            line = ((pack - packs[0]) * 4 + i) * block
            ref[i, pack * block : (pack + 1) * block, :] = out[line : line + block]
            part = rest[line : line + block]
            total = part if total is None else jnp.where(lane < pack * 32, total, part)
        ref[i, PHASES * 8 : LINES, :] = total


def place_kernel(y_ref, wind_ref, e_ref, tab_ref, hot_ref, first_ref, main_ref, side_ref,
                 kept_ref, s_ref, held_ref, sem):
    quarter = HALF // 2
    copies = [
        pltpu.make_async_copy(
            hot_ref.at[pl.ds(h * quarter, quarter)],
            held_ref.at[pl.ds(h * quarter, quarter)],
            sem.at[h],
        )
        for h in range(2)
    ]
    copies.append(pltpu.make_async_copy(hot_ref.at[pl.ds(HALF, HALF)], kept_ref, sem.at[2]))
    copies[0].start()
    copies[1].start()
    moments = e_ref[0] + e_ref[1] + e_ref[2] + e_ref[3]
    energy, inverse = moments[0:SEND], moments[SEND : 2 * SEND]
    mean = energy / inverse
    wavenumber = mean * mean / GRAV
    steepness = energy * wavenumber * wavenumber
    ratio = steepness / (steepness + 0.02)
    decay = ratio / (mean * mean)
    speed, heading = wind_ref[0:SEND, :], wind_ref[SEND : 2 * SEND, :]
    along = speed * jnp.cos(heading)
    across = speed * jnp.sin(heading)
    ccos = jnp.broadcast_to(tab_ref[:, C_COS : C_COS + 1], (ROWS, 128))
    csin = jnp.broadcast_to(tab_ref[:, C_SIN : C_SIN + 1], (ROWS, 128))
    cout = jnp.broadcast_to(tab_ref[:, C_OUT : C_OUT + 1], (ROWS, 128))
    row = lax.broadcasted_iota(jnp.int32, (ROWS, 128), 0)
    s_ref[ROWS:DEPTH, :] = jnp.zeros((DEPTH - ROWS, SEA), jnp.float32)
    for k in range(SEND):
        grow = ccos * along[k : k + 1] + csin * across[k : k + 1]
        rate = jnp.maximum(grow - 0.1, 0.0) - cout * decay[k : k + 1]
        value = y_ref[k] * jnp.exp(rate)
        value = jnp.where(row < LOCAL, value, 0.0)
        s_ref[0:ROWS, k * 128 : (k + 1) * 128] = value
    value = s_ref[...]
    high = value.astype(jnp.bfloat16)
    rest = (value - high.astype(jnp.float32)).astype(jnp.bfloat16)
    main_ref[0:MAIN, :] = high[0:MAIN]
    main_ref[MAIN:256, :] = rest[0:MAIN]
    for pack in range(PACKS):
        side_ref[pack * 32 : pack * 32 + 32, :] = high[MAIN:DEPTH]
        side_ref[128 + pack * 32 : 128 + pack * 32 + 32, :] = rest[MAIN:DEPTH]
    first_ref[:, LINES : LINES + PAD, :] = jnp.zeros((4, PAD, 128), jnp.float32)
    copies[0].wait()
    copies[2].start()
    spread(held_ref, main_ref[...], side_ref[...], first_ref, (0, 1))
    copies[1].wait()
    spread(held_ref, main_ref[...], side_ref[...], first_ref, (2, 3))
    copies[2].wait()


def place_rest_kernel(main_ref, side_ref, kept_ref, second_ref):
    spread(kept_ref, main_ref[...], side_ref[...], second_ref, (0, 1, 2, 3))


def limited(a, b):
    m = (a + (b + b)) * (1.0 / 6.0)
    least = jnp.minimum(jnp.maximum(a, b), 0.0)
    most = jnp.maximum(jnp.minimum(a, b), 0.0)
    return jnp.minimum(jnp.maximum(m, least), most)


def next_main(x):
    return pltpu.roll(x, 7, 0)


def last_main(x):
    return pltpu.roll(x, 1, 0)


def next_side(x):
    lane = lax.broadcasted_iota(jnp.int32, (8, 128), 1)
    x = pltpu.roll(x, 96, 1)
    return jnp.where(lane >= 96, pltpu.roll(x, 7, 0), x)


def last_side(x):
    lane = lax.broadcasted_iota(jnp.int32, (8, 128), 1)
    x = pltpu.roll(x, 32, 1)
    return jnp.where(lane < 32, pltpu.roll(x, 1, 0), x)


def substep(rows, seas, put, keep_ref, coef, base, phases, after, before):
    ux, kx, uy, ky = coef
    count = len(rows) - 3

    def load(spot, phase):
        ref, at = spot
        return ref[at, pl.ds(pl.multiple_of(base + phase * 8, 8), 8), :]

    for i in range(count):
        spot = rows[i + 2]
        end = load(spot, phases - 1)
        ahead = load(spot, 0) - before(end)
        prior = before(end - load(spot, phases - 2))
        keep_ref[i, 0] = ahead
        keep_ref[i, 1] = uy * before(end) + ky * limited(prior, ahead)

    def body(chunk, carry):
        first = chunk * CHUNK
        following = jnp.where(first + CHUNK == phases, 0, first + CHUNK)
        wraps = first + CHUNK == phases
        q = [load(rows[1], first + j) for j in range(CHUNK)]
        diff = [q[j] - load(rows[0], first + j) for j in range(CHUNK)]
        flux = None
        for i in range(-1, count):
            up = [load(rows[i + 3], first + j) for j in range(CHUNK)]
            slope = [up[j] - q[j] for j in range(CHUNK)]
            gone = [ux * q[j] + kx * limited(diff[j], slope[j]) for j in range(CHUNK)]
            if i >= 0:
                behind, past = keep_ref[i, 0], keep_ref[i, 1]
                edge = load(rows[i + 2], following)
                edge = jnp.where(wraps, after(edge), edge)
                for j in range(CHUNK):
                    ahead = (q[j + 1] if j + 1 < CHUNK else edge) - q[j]
                    side = uy * q[j] + ky * limited(behind, ahead)
                    new = q[j] - ((gone[j] - flux[j]) + (side - past))
                    sea = q[j] if seas is None else load(seas[i], first + j)
                    put(i, first + j, jnp.where(sea > 0.0, new, 0.0))
                    behind, past = ahead, side
                keep_ref[i, 0] = behind
                keep_ref[i, 1] = past
            q, diff, flux = up, slope, gone
        return carry

    lax.fori_loop(0, phases // CHUNK, body, 0)


def halves(tab_ref):
    for base, phases, lanes, after, before in (
        (0, PHASES, 0, next_main, last_main),
        (PHASES * 8, SHORT, 128, next_side, last_side),
    ):
        coef = [
            jnp.broadcast_to(tab_ref[n : n + 1, lanes : lanes + 128], (8, 128)) for n in range(4)
        ]
        yield coef, base, phases, after, before


def writer(ref, base, offset):
    def put(i, phase, value):
        ref[i + offset, pl.ds(pl.multiple_of(base + phase * 8, 8), 8), :] = value

    return put


def last_writer(ref, base, offset, cols_back):
    def put(i, phase, value):
        if base == 0:
            phase = phase + (PHASES - 1 - 2 * phase) * cols_back
        line = (i + offset) * LINES + base + phase * 8
        ref[pl.ds(pl.multiple_of(line, 8), 8), :] = value

    return put


def field(flip, first_ref, second_ref):
    parts = (second_ref, first_ref) if flip else (first_ref, second_ref)
    return [(ref, i) for ref in parts for i in range(4)]


def turned_main(ref, at, half, cols_back):
    parts = []
    for s in range(half * 4, half * 4 + 4):
        start = at * LINES + s + (7 - 2 * s) * cols_back
        parts.append(ref[pl.ds(start, PHASES, stride=8), :])
    return jnp.concatenate(parts, axis=0).T


def turned_side(ref, at):
    line = at * LINES + PHASES * 8
    empty = jnp.zeros((128 - SHORT * 8, 128), jnp.float32)
    return jnp.concatenate([ref[line : line + SHORT * 8, :], empty], axis=0).T


def inner_kernel(flag_ref, tab_ref, first_ref, second_ref, once_ref, done_ref, twice_ref, keep_ref):
    once = [(once_ref, i) for i in range(5)]
    for flip in range(2):

        @pl.when(flag_ref[2] == flip)
        def _():
            cells = field(flip, first_ref, second_ref)
            for half in halves(tab_ref):
                base = half[1]
                substep(cells, None, writer(once_ref, base, 0), keep_ref, *half)
                put = last_writer(twice_ref, base, 0, flag_ref[1])
                substep(once, cells[4:6], put, keep_ref, *half)

    for i in range(2):
        done_ref[i, 0] = turned_main(twice_ref, i, 0, flag_ref[1])
        done_ref[i, 1] = turned_main(twice_ref, i, 1, flag_ref[1])
        done_ref[i, 2] = turned_side(twice_ref, i)


def edge(lower, cells, got_ref, inner_ref, once_ref, twice_ref, keep_ref, cols_back, half):
    base = half[1]
    once = [(inner_ref, i) for i in range(5)]
    if lower:
        near = [(got_ref, i) for i in range(4)] + cells[0:3]
        seas, fresh = cells[0:4], [(once_ref, i) for i in range(4)]
        once = fresh + once[0:3]
    else:
        near = cells[5:8] + [(got_ref, i) for i in range(2)]
        seas, fresh = cells[6:8], [(once_ref, i) for i in range(2)]
        once = once[2:5] + fresh
    substep(near, None, writer(once_ref, base, 0), keep_ref, *half)
    substep(once, seas, last_writer(twice_ref, base, 0, cols_back), keep_ref, *half)
    return len(seas)


def near_kernel(flag_ref, tab_ref, first_ref, second_ref, got_ref, inner_ref, done_ref, once_ref,
                twice_ref, keep_ref):
    cols_back = flag_ref[1]
    for flip in range(2):

        @pl.when(flag_ref[2] == flip)
        def _():
            cells = field(flip, first_ref, second_ref)
            for half in halves(tab_ref):
                count = edge(flip == 1, cells, got_ref, inner_ref, once_ref, twice_ref, keep_ref,
                             cols_back, half)
            for i in range(count):
                done_ref[i, 0] = turned_main(twice_ref, i, 0, cols_back)
                done_ref[i, 1] = turned_main(twice_ref, i, 1, cols_back)
                done_ref[i, 2] = turned_side(twice_ref, i)


def outer_kernel(flag_ref, tab_ref, first_ref, second_ref, got_ref, inner_ref, done_ref, near_ref,
                 out_hbm, once_ref, twice_ref, keep_ref, turn_ref, rest_ref, last_ref, sem):
    rows_back = flag_ref[0]
    cols_back = flag_ref[1]

    def blocks(flip, part):
        for e in range(TROWS):
            r = e + (TROWS - 1 - 2 * e) * rows_back
            if e in (4, 5):
                yield r, done_ref[e - 4, part]
                continue
            lower, at = e < 4, e if e < 4 else e - 6
            if lower == (flip == 1):
                yield r, near_ref[at, part]
            elif part == 2:
                yield r, turned_side(twice_ref, at)
            else:
                yield r, turned_main(twice_ref, at, part, cols_back)

    def compute(flip, half):
        cells = field(flip, first_ref, second_ref)
        edge(flip == 0, cells, got_ref, inner_ref, once_ref, twice_ref, keep_ref, cols_back, half)

    main, side = halves(tab_ref)
    copies = [
        pltpu.make_async_copy(
            turn_ref.at[half],
            out_hbm.at[pl.ds(0, MAIN), :, pl.ds(half * 128, 128)],
            sem.at[half],
        )
        for half in range(2)
    ]
    count = LOCAL - MAIN
    copies.append(
        pltpu.make_async_copy(
            last_ref.at[pl.ds(0, count)], out_hbm.at[pl.ds(MAIN, count)], sem.at[2]
        )
    )
    for flip in range(2):

        @pl.when(flag_ref[2] == flip)
        def _():
            compute(flip, side)
            for r, block in blocks(flip, 2):
                for pack in range(PACKS):
                    rest_ref[pack, pl.ds(r, 32, stride=TROWS), :] = block[
                        pack * 32 : pack * 32 + 32
                    ]

    spot = lax.broadcasted_iota(jnp.int32, (PACKS * 128, NY), 0)
    col = lax.broadcasted_iota(jnp.int32, (PACKS * 128, NY), 1)
    col = col + (NY - 1 - 2 * col) * cols_back
    pack, inner = spot // 128, spot % 128
    wanted = inner % 8 * 32 + pack * SHORT + inner // 8
    order = jnp.where((wanted == col) & (inner < SHORT * 8), 1.0, 0.0).astype(jnp.bfloat16)
    value = jnp.concatenate([rest_ref[pack] for pack in range(PACKS)], axis=1)
    high = value.astype(jnp.bfloat16)
    rest = (value - high.astype(jnp.float32)).astype(jnp.bfloat16)
    value = jnp.dot(high, order, preferred_element_type=jnp.float32)
    value = value + jnp.dot(rest, order, preferred_element_type=jnp.float32)
    for i in range(count):
        last_ref[i] = value[i * TROWS : (i + 1) * TROWS, :]
    copies[2].start()
    for flip in range(2):

        @pl.when(flag_ref[2] == flip)
        def _():
            compute(flip, main)

    for half in range(2):
        lines = turn_ref.at[half].reshape(MAIN * TROWS, 128)
        for flip in range(2):

            @pl.when(flag_ref[2] == flip)
            def _():
                for r, block in blocks(flip, half):
                    lines[pl.ds(r, MAIN, stride=TROWS), :] = block

        copies[half].start()
    for copy in copies:
        copy.wait()


def call(kernel, shapes, scratch, ins, *args, limit=20, us=0, outs=None):
    cost = pl.CostEstimate(flops=us * 10**9, bytes_accessed=us * 3 * 10**6, transcendentals=0)
    return pl.pallas_call(
        kernel,
        out_shape=shapes,
        in_specs=ins,
        out_specs=outs or jax.tree.map(lambda _: VMEM, shapes),
        scratch_shapes=scratch,
        cost_estimate=cost if us else None,
        compiler_params=pltpu.CompilerParams(vmem_limit_bytes=limit * 1024 * 1024),
    )(*args)


def f32(*shape):
    return jax.ShapeDtypeStruct(shape, jnp.float32)


def local(spectra, wind_speed, wind_dir, sea_cell):
    group = lax.axis_index("grp")
    table, courant = (
        lax.dynamic_index_in_dim(jnp.asarray(t), group, 0, keepdims=False)
        for t in coefficient_tables()
    )
    mirror_x = ((group == 1) | (group == 2)).astype(jnp.int32)
    mirror_y = (group >= 2).astype(jnp.int32)
    odd = lax.axis_index("comp") % 2
    flip = (odd ^ mirror_x).astype(jnp.int32)
    flags = jnp.stack([mirror_x, mirror_y, flip])
    hbm = pl.BlockSpec(memory_space=pltpu.HBM)
    packed = call(
        pack_kernel,
        f32(TILES * SLOTS, 128),
        [
            pltpu.VMEM((PARTS, LOCAL, SEA // PARTS), jnp.float32),
            pltpu.VMEM((2, SEA // 128, 128), jnp.float32),
            pltpu.VMEM((2, SEA // PARTS, 128), jnp.float32),
            pltpu.VMEM((128, SEA // PARTS), jnp.float32),
            pltpu.VMEM((TILES * SLOTS, 128), jnp.float32),
            pltpu.SemaphoreType.DMA((PARTS,)),
            pltpu.SemaphoreType.DMA((2,)),
            pltpu.SemaphoreType.DMA((PARTS,)),
        ],
        [hbm] * 3,
        spectra,
        wind_speed.reshape(SEA // 128, 128),
        wind_dir.reshape(SEA // 128, 128),
        limit=57,
        outs=hbm,
    )
    received = lax.all_to_all(
        packed.reshape(TILES, 1, SLOTS * 128), "comp", split_axis=0, concat_axis=0, tiled=True
    ).reshape(TILES * SLOTS, 128)
    cells = sea_cell.reshape(TILES, SEND).T
    cells = cells ^ (mirror_x * (NY * (TROWS - 1)) + mirror_y * (NY - 1)) ^ (flip * (NY * TROWS // 2))
    hot = call(
        onehot_kernel,
        jax.ShapeDtypeStruct((TROWS * NY, SEA), jnp.bfloat16),
        [],
        [VMEM],
        cells,
    )
    received, hot = lax.optimization_barrier((received, hot))
    points, wind_here, partial = call(
        moments_kernel,
        (f32(SEND, ROWS, 128), f32(2 * SEND, 128), f32(GROUPS, 2 * SEND, 128)),
        [],
        [VMEM] * 2,
        received,
        table,
    )
    partial = lax.all_to_all(partial, "grp", split_axis=0, concat_axis=0, tiled=True)
    bf16 = functools.partial(jax.ShapeDtypeStruct, dtype=jnp.bfloat16)
    first, main, side, kept = call(
        place_kernel,
        (f32(4, LINES + PAD, 128), bf16((256, SEA)), bf16((256, SEA)), bf16((HALF, SEA))),
        [
            pltpu.VMEM((DEPTH, SEA), jnp.float32),
            pltpu.VMEM((HALF, SEA), jnp.bfloat16),
            pltpu.SemaphoreType.DMA((3,)),
        ],
        [VMEM] * 4 + [hbm],
        points,
        wind_here,
        partial,
        table,
        hot,
        limit=44,
    )
    second = call(
        place_rest_kernel,
        f32(4, LINES, 128),
        [],
        [VMEM] * 3,
        main,
        side,
        kept,
        us=2,
    )
    across, within = [], []
    for g in range(GROUPS):
        for i in range(TILES - 1):
            low, high = g * TILES + i, g * TILES + i + 1
            (across if i % 2 else within).extend([(low, high), (high, low)])
    got_first = lax.ppermute(first, ("grp", "comp"), across)
    got_second = lax.ppermute(second, ("grp", "comp"), within)
    once, done = call(
        inner_kernel,
        (f32(5, LINES, 128), f32(2, 3, 128, 128)),
        [pltpu.VMEM((2 * LINES, 128), jnp.float32), pltpu.VMEM((5, 2, 8, 128), jnp.float32)],
        [SMEM] + [VMEM] * 3,
        flags,
        courant,
        first,
        second,
        us=3,
    )
    near = call(
        near_kernel,
        f32(4, 3, 128, 128),
        [
            pltpu.VMEM((4, LINES, 128), jnp.float32),
            pltpu.VMEM((4 * LINES, 128), jnp.float32),
            pltpu.VMEM((4, 2, 8, 128), jnp.float32),
        ],
        [SMEM] + [VMEM] * 5,
        flags,
        courant,
        first,
        second,
        got_second,
        once,
        us=0,
    )
    return call(
        outer_kernel,
        f32(LOCAL, TROWS, NY),
        [
            pltpu.VMEM((4, LINES, 128), jnp.float32),
            pltpu.VMEM((4 * LINES, 128), jnp.float32),
            pltpu.VMEM((4, 2, 8, 128), jnp.float32),
            pltpu.VMEM((2, MAIN, TROWS, 128), jnp.float32),
            pltpu.VMEM((PACKS, 32 * TROWS, 128), jnp.float32),
            pltpu.VMEM((32, TROWS, NY), jnp.float32),
            pltpu.SemaphoreType.DMA((3,)),
        ],
        [SMEM] + [VMEM] * 7,
        flags,
        courant,
        first,
        second,
        got_first,
        once,
        done,
        near,
        outs=hbm,
    )


def solution(mesh):
    in_specs = (P("grp", "comp"), P("comp"), P("comp"), P("comp"))
    out_specs = P("grp", "comp", None)
    return jax.shard_map(local, mesh=mesh, in_specs=in_specs, out_specs=out_specs, check_vma=False)
```

```python
import functools
import math

import jax
import jax.numpy as jnp
import numpy as np
from jax import lax
from jax.experimental import pallas as pl
from jax.experimental.pallas import tpu as pltpu
from jax.sharding import PartitionSpec as P

DIRS = 24
FREQ = 25
TROWS = 8
NY = 256
SEA = 1536
SEND = 12
GROUPS = 4
TILES = 128
LOCAL = DIRS * FREQ // GROUPS
ROWS = 152
DEPTH = 160
MAIN = 128
EXTRA = ROWS - MAIN
PER_TILE = 5
SLOTS = 15
GRAV = 9.81
LOW_FREQ = 0.0418
FREQ_STEP = 1.1

VMEM = pl.BlockSpec(memory_space=pltpu.VMEM)

W_E, W_I, C_COS, C_SIN, C_OUT = range(5)
PHASES = 32
PACKS = 4
SHORT = PHASES // PACKS
LINES = (PHASES + SHORT) * 8
CHUNK = 4
PAD = 8
PARTS = 4
HALF = TROWS * NY // 2


def coefficient_tables():
    table = np.zeros((GROUPS, ROWS, 128), np.float64)
    courant = np.zeros((GROUPS, 8, 256), np.float64)
    for group in range(GROUPS):
        for row in range(LOCAL):
            d, j = row // FREQ + group * (DIRS // GROUPS), row % FREQ
            angle = 2.0 * math.pi * (d + 0.5) / DIRS
            freq = LOW_FREQ * FREQ_STEP**j
            s = 2.0 * math.pi * freq
            w = 2.0 * math.pi / DIRS * 0.1 * freq
            reach = 0.45 * (2.0 * math.pi * LOW_FREQ) / s
            ux, uy = abs(reach * math.cos(angle)), abs(reach * math.sin(angle))
            push = 0.1 * 28.0 * 0.035 * s / GRAV
            table[group, row, :5] = (
                w, w / s, push * math.cos(angle), push * math.sin(angle), 0.4 * s * s
            )
            if row < MAIN:
                lanes = [row]
            else:
                lanes = [128 + pack * 32 + row - MAIN for pack in range(PACKS)]
            for lane in lanes:
                courant[group, :4, lane] = (ux, ux * (1.0 - ux), uy, uy * (1.0 - uy))
    return table.astype(np.float32), courant.astype(np.float32)


def pack_kernel(x_hbm, speed_hbm, heading_hbm, out_hbm, x_ref, wind_ref, z_ref, b_ref, m_ref,
                sem_in, sem_wind, sem_out):
    width = SEA // PARTS
    tiles = TILES // PARTS
    ins = [
        pltpu.make_async_copy(x_hbm.at[:, pl.ds(c * width, width)], x_ref.at[c], sem_in.at[c])
        for c in range(PARTS)
    ]
    winds = [
        pltpu.make_async_copy(ref, wind_ref.at[i], sem_wind.at[i])
        for i, ref in enumerate((speed_hbm, heading_hbm))
    ]
    outs = [
        pltpu.make_async_copy(
            m_ref.at[pl.ds(c * tiles * SLOTS, tiles * SLOTS)],
            out_hbm.at[pl.ds(c * tiles * SLOTS, tiles * SLOTS)],
            sem_out.at[c],
        )
        for c in range(PARTS)
    ]
    ins[0].start()
    winds[0].start()
    winds[1].start()
    ins[1].start()
    b_ref[PER_TILE * EXTRA : 128, :] = jnp.zeros((128 - PER_TILE * EXTRA, width), jnp.float32)
    lane = lax.broadcasted_iota(jnp.int32, (tiles, 128), 1)
    for c in range(PARTS):
        ins[c].wait()
        if c + 2 < PARTS:
            ins[c + 2].start()
        if c == 0:
            winds[0].wait()
            winds[1].wait()
        for copy in range(PER_TILE):
            b_ref[copy * EXTRA : copy * EXTRA + LOCAL - MAIN, :] = x_ref[c, MAIN:LOCAL, :]
        for block in range(width // 128):
            cols = slice(block * 128, block * 128 + 128)
            at = c * (width // 128) + block
            for copy in range(PER_TILE):
                for i in range(2):
                    row = copy * EXTRA + LOCAL - MAIN + i
                    b_ref[row : row + 1, cols] = wind_ref[i, at : at + 1, :]
            z_ref[0, cols, :] = x_ref[c, 0:MAIN, cols].T
            z_ref[1, cols, :] = b_ref[:, cols].T
        first = c * tiles * SLOTS
        for k in range(SEND):
            m_ref[pl.ds(first + k, tiles, stride=SLOTS), :] = z_ref[
                0, pl.ds(k, tiles, stride=SEND), :
            ]
        for tile in range(SLOTS - SEND):
            total = None
            for k in range(tile * PER_TILE, min(SEND, (tile + 1) * PER_TILE)):
                piece = z_ref[1, pl.ds(k, tiles, stride=SEND), :]
                start = (k % PER_TILE) * EXTRA
                total = piece if total is None else jnp.where(lane < start, total, piece)
            m_ref[pl.ds(first + SEND + tile, tiles, stride=SLOTS), :] = total
        outs[c].start()
    for c in range(PARTS):
        outs[c].wait()


def moments_kernel(r_ref, tab_ref, y_ref, wind_ref, e_ref):
    extra = None
    we = jnp.broadcast_to(tab_ref[:, W_E : W_E + 1], (ROWS, 128))
    wi = jnp.broadcast_to(tab_ref[:, W_I : W_I + 1], (ROWS, 128))
    for k in range(SEND):
        if k % PER_TILE == 0:
            extra = r_ref[pl.ds(SEND + k // PER_TILE, TILES, stride=SLOTS), :].T
        part = extra[(k % PER_TILE) * EXTRA : (k % PER_TILE + 1) * EXTRA, :]
        main = r_ref[pl.ds(k, TILES, stride=SLOTS), :].T
        y_ref[k, 0:MAIN, :] = main
        y_ref[k, MAIN:ROWS, :] = part
        wind_ref[k : k + 1, :] = part[LOCAL - MAIN : LOCAL - MAIN + 1, :]
        wind_ref[SEND + k : SEND + k + 1, :] = part[LOCAL - MAIN + 1 : EXTRA, :]
        y = y_ref[k]
        energy = jnp.sum(y * we, axis=0, keepdims=True)
        inverse = jnp.sum(y * wi, axis=0, keepdims=True)
        for g in range(GROUPS):
            e_ref[g, k : k + 1, :] = energy
            e_ref[g, SEND + k : SEND + k + 1, :] = inverse


def onehot_kernel(cell_ref, out_ref):
    row = lax.broadcasted_iota(jnp.int32, (16, 128), 0)
    base = row % 8 * 32 + row // 8
    spots = [cell_ref[k : k + 1, :] - base for k in range(SEND)]

    def body(e, carry):
        for phase in range(0, PHASES, 2):
            pack, short = phase // SHORT, phase % SHORT
            line = ((e // 4 * PACKS + pack) * 4 + e % 4) * SHORT * 8 + short * 8
            for k in range(SEND):
                hit = spots[k] == e * NY + phase
                out_ref[pl.ds(pl.multiple_of(line, 16), 16), k * 128 : (k + 1) * 128] = jnp.where(
                    hit, 1.0, 0.0
                ).astype(jnp.bfloat16)
        return carry

    lax.fori_loop(0, TROWS, body, 0)


def spread(held_ref, main, side, ref, packs):
    turned = (((1,), (1,)), ((), ()))
    block = SHORT * 8
    hot = held_ref[packs[0] * 4 * block : (packs[-1] + 1) * 4 * block, :]
    out = lax.dot_general(hot, main, turned, preferred_element_type=jnp.float32)
    out = out[:, 0:128] + out[:, 128:256]
    rest = lax.dot_general(hot, side, turned, preferred_element_type=jnp.float32)
    rest = rest[:, 0:128] + rest[:, 128:256]
    lane = lax.broadcasted_iota(jnp.int32, (block, 128), 1)
    for i in range(4):
        total = ref[i, PHASES * 8 : LINES, :] if packs[0] else None
        for pack in packs:
            line = ((pack - packs[0]) * 4 + i) * block
            ref[i, pack * block : (pack + 1) * block, :] = out[line : line + block]
            part = rest[line : line + block]
            total = part if total is None else jnp.where(lane < pack * 32, total, part)
        ref[i, PHASES * 8 : LINES, :] = total


def place_kernel(y_ref, wind_ref, e_ref, tab_ref, hot_ref, first_ref, main_ref, side_ref,
                 kept_ref, s_ref, held_ref, sem):
    quarter = HALF // 2
    copies = [
        pltpu.make_async_copy(
            hot_ref.at[pl.ds(h * quarter, quarter)],
            held_ref.at[pl.ds(h * quarter, quarter)],
            sem.at[h],
        )
        for h in range(2)
    ]
    copies.append(pltpu.make_async_copy(hot_ref.at[pl.ds(HALF, HALF)], kept_ref, sem.at[2]))
    copies[0].start()
    copies[1].start()
    moments = e_ref[0] + e_ref[1] + e_ref[2] + e_ref[3]
    energy, inverse = moments[0:SEND], moments[SEND : 2 * SEND]
    mean = energy / inverse
    wavenumber = mean * mean / GRAV
    steepness = energy * wavenumber * wavenumber
    ratio = steepness / (steepness + 0.02)
    decay = ratio / (mean * mean)
    speed, heading = wind_ref[0:SEND, :], wind_ref[SEND : 2 * SEND, :]
    along = speed * jnp.cos(heading)
    across = speed * jnp.sin(heading)
    ccos = jnp.broadcast_to(tab_ref[:, C_COS : C_COS + 1], (ROWS, 128))
    csin = jnp.broadcast_to(tab_ref[:, C_SIN : C_SIN + 1], (ROWS, 128))
    cout = jnp.broadcast_to(tab_ref[:, C_OUT : C_OUT + 1], (ROWS, 128))
    row = lax.broadcasted_iota(jnp.int32, (ROWS, 128), 0)
    s_ref[ROWS:DEPTH, :] = jnp.zeros((DEPTH - ROWS, SEA), jnp.float32)
    for k in range(SEND):
        grow = ccos * along[k : k + 1] + csin * across[k : k + 1]
        rate = jnp.maximum(grow - 0.1, 0.0) - cout * decay[k : k + 1]
        value = y_ref[k] * jnp.exp(rate)
        value = jnp.where(row < LOCAL, value, 0.0)
        s_ref[0:ROWS, k * 128 : (k + 1) * 128] = value
    value = s_ref[...]
    high = value.astype(jnp.bfloat16)
    rest = (value - high.astype(jnp.float32)).astype(jnp.bfloat16)
    main_ref[0:MAIN, :] = high[0:MAIN]
    main_ref[MAIN:256, :] = rest[0:MAIN]
    for pack in range(PACKS):
        side_ref[pack * 32 : pack * 32 + 32, :] = high[MAIN:DEPTH]
        side_ref[128 + pack * 32 : 128 + pack * 32 + 32, :] = rest[MAIN:DEPTH]
    first_ref[:, LINES : LINES + PAD, :] = jnp.zeros((4, PAD, 128), jnp.float32)
    copies[0].wait()
    copies[2].start()
    spread(held_ref, main_ref[...], side_ref[...], first_ref, (0, 1))
    copies[1].wait()
    spread(held_ref, main_ref[...], side_ref[...], first_ref, (2, 3))
    copies[2].wait()


def place_rest_kernel(main_ref, side_ref, kept_ref, second_ref):
    spread(kept_ref, main_ref[...], side_ref[...], second_ref, (0, 1, 2, 3))


def limited(a, b):
    m = (a + (b + b)) * (1.0 / 6.0)
    least = jnp.minimum(jnp.maximum(a, b), 0.0)
    most = jnp.maximum(jnp.minimum(a, b), 0.0)
    return jnp.minimum(jnp.maximum(m, least), most)


def next_main(x):
    return pltpu.roll(x, 7, 0)


def last_main(x):
    return pltpu.roll(x, 1, 0)


def next_side(x):
    lane = lax.broadcasted_iota(jnp.int32, (8, 128), 1)
    x = pltpu.roll(x, 96, 1)
    return jnp.where(lane >= 96, pltpu.roll(x, 7, 0), x)


def last_side(x):
    lane = lax.broadcasted_iota(jnp.int32, (8, 128), 1)
    x = pltpu.roll(x, 32, 1)
    return jnp.where(lane < 32, pltpu.roll(x, 1, 0), x)


def substep(rows, seas, put, keep_ref, coef, base, phases, after, before):
    ux, kx, uy, ky = coef
    count = len(rows) - 3

    def load(spot, phase):
        ref, at = spot
        return ref[at, pl.ds(pl.multiple_of(base + phase * 8, 8), 8), :]

    for i in range(count):
        spot = rows[i + 2]
        end = load(spot, phases - 1)
        ahead = load(spot, 0) - before(end)
        prior = before(end - load(spot, phases - 2))
        keep_ref[i, 0] = ahead
        keep_ref[i, 1] = uy * before(end) + ky * limited(prior, ahead)

    def body(chunk, carry):
        first = chunk * CHUNK
        following = jnp.where(first + CHUNK == phases, 0, first + CHUNK)
        wraps = first + CHUNK == phases
        q = [load(rows[1], first + j) for j in range(CHUNK)]
        diff = [q[j] - load(rows[0], first + j) for j in range(CHUNK)]
        flux = None
        for i in range(-1, count):
            up = [load(rows[i + 3], first + j) for j in range(CHUNK)]
            slope = [up[j] - q[j] for j in range(CHUNK)]
            gone = [ux * q[j] + kx * limited(diff[j], slope[j]) for j in range(CHUNK)]
            if i >= 0:
                behind, past = keep_ref[i, 0], keep_ref[i, 1]
                edge = load(rows[i + 2], following)
                edge = jnp.where(wraps, after(edge), edge)
                for j in range(CHUNK):
                    ahead = (q[j + 1] if j + 1 < CHUNK else edge) - q[j]
                    side = uy * q[j] + ky * limited(behind, ahead)
                    new = q[j] - ((gone[j] - flux[j]) + (side - past))
                    sea = q[j] if seas is None else load(seas[i], first + j)
                    put(i, first + j, jnp.where(sea > 0.0, new, 0.0))
                    behind, past = ahead, side
                keep_ref[i, 0] = behind
                keep_ref[i, 1] = past
            q, diff, flux = up, slope, gone
        return carry

    lax.fori_loop(0, phases // CHUNK, body, 0)


def flags():
    group = lax.axis_index("grp")
    mirror_x = ((group == 1) | (group == 2)).astype(jnp.int32)
    mirror_y = (group >= 2).astype(jnp.int32)
    odd = lax.axis_index("comp").astype(jnp.int32) % 2
    return mirror_x, mirror_y, odd ^ mirror_x


def halves(tab_ref):
    for base, phases, lanes, after, before in (
        (0, PHASES, 0, next_main, last_main),
        (PHASES * 8, SHORT, 128, next_side, last_side),
    ):
        coef = [
            jnp.broadcast_to(tab_ref[n : n + 1, lanes : lanes + 128], (8, 128)) for n in range(4)
        ]
        yield coef, base, phases, after, before


def writer(ref, base, offset):
    def put(i, phase, value):
        ref[i + offset, pl.ds(pl.multiple_of(base + phase * 8, 8), 8), :] = value

    return put


def last_writer(ref, base, offset, cols_back):
    def put(i, phase, value):
        if base == 0:
            phase = phase + (PHASES - 1 - 2 * phase) * cols_back
        line = (i + offset) * LINES + base + phase * 8
        ref[pl.ds(pl.multiple_of(line, 8), 8), :] = value

    return put


def field(flip, first_ref, second_ref):
    parts = (second_ref, first_ref) if flip else (first_ref, second_ref)
    return [(ref, i) for ref in parts for i in range(4)]


def turned_main(ref, at, half, cols_back):
    parts = []
    for s in range(half * 4, half * 4 + 4):
        start = at * LINES + s + (7 - 2 * s) * cols_back
        parts.append(ref[pl.ds(start, PHASES, stride=8), :])
    return jnp.concatenate(parts, axis=0).T


def turned_side(ref, at):
    line = at * LINES + PHASES * 8
    empty = jnp.zeros((128 - SHORT * 8, 128), jnp.float32)
    return jnp.concatenate([ref[line : line + SHORT * 8, :], empty], axis=0).T


def inner_kernel(tab_ref, first_ref, second_ref, once_ref, done_ref, twice_ref, keep_ref):
    once = [(once_ref, i) for i in range(5)]
    _, cols_back, side_up = flags()
    for flip in range(2):

        @pl.when(side_up == flip)
        def _():
            cells = field(flip, first_ref, second_ref)
            for half in halves(tab_ref):
                base = half[1]
                substep(cells, None, writer(once_ref, base, 0), keep_ref, *half)
                put = last_writer(twice_ref, base, 0, cols_back)
                substep(once, cells[4:6], put, keep_ref, *half)

    for i in range(2):
        done_ref[i, 0] = turned_main(twice_ref, i, 0, cols_back)
        done_ref[i, 1] = turned_main(twice_ref, i, 1, cols_back)
        done_ref[i, 2] = turned_side(twice_ref, i)


def edge(lower, cells, got_ref, inner_ref, once_ref, twice_ref, keep_ref, cols_back, half):
    base = half[1]
    once = [(inner_ref, i) for i in range(5)]
    if lower:
        near = [(got_ref, i) for i in range(4)] + cells[0:3]
        seas, fresh = cells[0:4], [(once_ref, i) for i in range(4)]
        once = fresh + once[0:3]
    else:
        near = cells[5:8] + [(got_ref, i) for i in range(2)]
        seas, fresh = cells[6:8], [(once_ref, i) for i in range(2)]
        once = once[2:5] + fresh
    substep(near, None, writer(once_ref, base, 0), keep_ref, *half)
    substep(once, seas, last_writer(twice_ref, base, 0, cols_back), keep_ref, *half)
    return len(seas)


def near_kernel(tab_ref, first_ref, second_ref, got_ref, inner_ref, done_ref, once_ref,
                twice_ref, keep_ref):
    _, cols_back, side_up = flags()
    for flip in range(2):

        @pl.when(side_up == flip)
        def _():
            cells = field(flip, first_ref, second_ref)
            for half in halves(tab_ref):
                count = edge(flip == 1, cells, got_ref, inner_ref, once_ref, twice_ref, keep_ref,
                             cols_back, half)
            for i in range(count):
                done_ref[i, 0] = turned_main(twice_ref, i, 0, cols_back)
                done_ref[i, 1] = turned_main(twice_ref, i, 1, cols_back)
                done_ref[i, 2] = turned_side(twice_ref, i)


def outer_kernel(tab_ref, first_ref, second_ref, got_ref, inner_ref, done_ref, near_ref,
                 out_hbm, once_ref, twice_ref, keep_ref, turn_ref, rest_ref, last_ref, sem):
    rows_back, cols_back, side_up = flags()

    def blocks(flip, part):
        for e in range(TROWS):
            r = e + (TROWS - 1 - 2 * e) * rows_back
            if e in (4, 5):
                yield r, done_ref[e - 4, part]
                continue
            lower, at = e < 4, e if e < 4 else e - 6
            if lower == (flip == 1):
                yield r, near_ref[at, part]
            elif part == 2:
                yield r, turned_side(twice_ref, at)
            else:
                yield r, turned_main(twice_ref, at, part, cols_back)

    def compute(flip, half):
        cells = field(flip, first_ref, second_ref)
        edge(flip == 0, cells, got_ref, inner_ref, once_ref, twice_ref, keep_ref, cols_back, half)

    main, side = halves(tab_ref)
    copies = [
        pltpu.make_async_copy(
            turn_ref.at[half],
            out_hbm.at[pl.ds(0, MAIN), :, pl.ds(half * 128, 128)],
            sem.at[half],
        )
        for half in range(2)
    ]
    count = LOCAL - MAIN
    copies.append(
        pltpu.make_async_copy(
            last_ref.at[pl.ds(0, count)], out_hbm.at[pl.ds(MAIN, count)], sem.at[2]
        )
    )
    for flip in range(2):

        @pl.when(side_up == flip)
        def _():
            compute(flip, side)
            for r, block in blocks(flip, 2):
                for pack in range(PACKS):
                    rest_ref[pack, pl.ds(r, 32, stride=TROWS), :] = block[
                        pack * 32 : pack * 32 + 32
                    ]

    spot = lax.broadcasted_iota(jnp.int32, (PACKS * 128, NY), 0)
    col = lax.broadcasted_iota(jnp.int32, (PACKS * 128, NY), 1)
    col = col + (NY - 1 - 2 * col) * cols_back
    pack, inner = spot // 128, spot % 128
    wanted = inner % 8 * 32 + pack * SHORT + inner // 8
    order = jnp.where((wanted == col) & (inner < SHORT * 8), 1.0, 0.0).astype(jnp.bfloat16)
    value = jnp.concatenate([rest_ref[pack] for pack in range(PACKS)], axis=1)
    high = value.astype(jnp.bfloat16)
    rest = (value - high.astype(jnp.float32)).astype(jnp.bfloat16)
    value = jnp.dot(high, order, preferred_element_type=jnp.float32)
    value = value + jnp.dot(rest, order, preferred_element_type=jnp.float32)
    for i in range(count):
        last_ref[i] = value[i * TROWS : (i + 1) * TROWS, :]
    copies[2].start()
    for flip in range(2):

        @pl.when(side_up == flip)
        def _():
            compute(flip, main)

    for half in range(2):
        lines = turn_ref.at[half].reshape(MAIN * TROWS, 128)
        for flip in range(2):

            @pl.when(side_up == flip)
            def _():
                for r, block in blocks(flip, half):
                    lines[pl.ds(r, MAIN, stride=TROWS), :] = block

        copies[half].start()
    for copy in copies:
        copy.wait()


def call(kernel, shapes, scratch, ins, *args, limit=20, us=0, outs=None):
    cost = pl.CostEstimate(flops=us * 10**9, bytes_accessed=us * 3 * 10**6, transcendentals=0)
    return pl.pallas_call(
        kernel,
        out_shape=shapes,
        in_specs=ins,
        out_specs=outs or jax.tree.map(lambda _: VMEM, shapes),
        scratch_shapes=scratch,
        cost_estimate=cost if us else None,
        compiler_params=pltpu.CompilerParams(vmem_limit_bytes=limit * 1024 * 1024),
    )(*args)


def f32(*shape):
    return jax.ShapeDtypeStruct(shape, jnp.float32)


def local(spectra, wind_speed, wind_dir, sea_cell):
    group = lax.axis_index("grp")
    table, courant = (
        lax.dynamic_index_in_dim(jnp.asarray(t), group, 0, keepdims=False)
        for t in coefficient_tables()
    )
    mirror_x, mirror_y, flip = flags()
    hbm = pl.BlockSpec(memory_space=pltpu.HBM)
    packed = call(
        pack_kernel,
        f32(TILES * SLOTS, 128),
        [
            pltpu.VMEM((PARTS, LOCAL, SEA // PARTS), jnp.float32),
            pltpu.VMEM((2, SEA // 128, 128), jnp.float32),
            pltpu.VMEM((2, SEA // PARTS, 128), jnp.float32),
            pltpu.VMEM((128, SEA // PARTS), jnp.float32),
            pltpu.VMEM((TILES * SLOTS, 128), jnp.float32),
            pltpu.SemaphoreType.DMA((PARTS,)),
            pltpu.SemaphoreType.DMA((2,)),
            pltpu.SemaphoreType.DMA((PARTS,)),
        ],
        [hbm] * 3,
        spectra,
        wind_speed.reshape(SEA // 128, 128),
        wind_dir.reshape(SEA // 128, 128),
        limit=57,
        outs=hbm,
    )
    received = lax.all_to_all(
        packed.reshape(TILES, 1, SLOTS * 128), "comp", split_axis=0, concat_axis=0, tiled=True
    ).reshape(TILES * SLOTS, 128)
    cells = sea_cell.reshape(TILES, SEND).T
    cells = cells ^ (mirror_x * (NY * (TROWS - 1)) + mirror_y * (NY - 1)) ^ (flip * (NY * TROWS // 2))
    hot = call(
        onehot_kernel,
        jax.ShapeDtypeStruct((TROWS * NY, SEA), jnp.bfloat16),
        [],
        [VMEM],
        cells,
    )
    received, hot = lax.optimization_barrier((received, hot))
    points, wind_here, partial = call(
        moments_kernel,
        (f32(SEND, ROWS, 128), f32(2 * SEND, 128), f32(GROUPS, 2 * SEND, 128)),
        [],
        [VMEM] * 2,
        received,
        table,
    )
    partial = lax.all_to_all(partial, "grp", split_axis=0, concat_axis=0, tiled=True)
    bf16 = functools.partial(jax.ShapeDtypeStruct, dtype=jnp.bfloat16)
    first, main, side, kept = call(
        place_kernel,
        (f32(4, LINES + PAD, 128), bf16((256, SEA)), bf16((256, SEA)), bf16((HALF, SEA))),
        [
            pltpu.VMEM((DEPTH, SEA), jnp.float32),
            pltpu.VMEM((HALF, SEA), jnp.bfloat16),
            pltpu.SemaphoreType.DMA((3,)),
        ],
        [VMEM] * 4 + [hbm],
        points,
        wind_here,
        partial,
        table,
        hot,
        limit=44,
    )
    second = call(
        place_rest_kernel,
        f32(4, LINES, 128),
        [],
        [VMEM] * 3,
        main,
        side,
        kept,
        us=2,
    )
    across, within = [], []
    for g in range(GROUPS):
        for i in range(TILES - 1):
            low, high = g * TILES + i, g * TILES + i + 1
            (across if i % 2 else within).extend([(low, high), (high, low)])
    got_first = lax.ppermute(first, ("grp", "comp"), across)
    got_second = lax.ppermute(second, ("grp", "comp"), within)
    once, done = call(
        inner_kernel,
        (f32(5, LINES, 128), f32(2, 3, 128, 128)),
        [pltpu.VMEM((2 * LINES, 128), jnp.float32), pltpu.VMEM((5, 2, 8, 128), jnp.float32)],
        [VMEM] * 3,
        courant,
        first,
        second,
        us=3,
    )
    near = call(
        near_kernel,
        f32(4, 3, 128, 128),
        [
            pltpu.VMEM((4, LINES, 128), jnp.float32),
            pltpu.VMEM((4 * LINES, 128), jnp.float32),
            pltpu.VMEM((4, 2, 8, 128), jnp.float32),
        ],
        [VMEM] * 5,
        courant,
        first,
        second,
        got_second,
        once,
        us=0,
    )
    return call(
        outer_kernel,
        f32(LOCAL, TROWS, NY),
        [
            pltpu.VMEM((4, LINES, 128), jnp.float32),
            pltpu.VMEM((4 * LINES, 128), jnp.float32),
            pltpu.VMEM((4, 2, 8, 128), jnp.float32),
            pltpu.VMEM((2, MAIN, TROWS, 128), jnp.float32),
            pltpu.VMEM((PACKS, 32 * TROWS, 128), jnp.float32),
            pltpu.VMEM((32, TROWS, NY), jnp.float32),
            pltpu.SemaphoreType.DMA((3,)),
        ],
        [VMEM] * 7,
        courant,
        first,
        second,
        got_first,
        once,
        done,
        near,
        outs=hbm,
    )


def solution(mesh):
    in_specs = (P("grp", "comp"), P("comp"), P("comp"), P("comp"))
    out_specs = P("grp", "comp", None)
    return jax.shard_map(local, mesh=mesh, in_specs=in_specs, out_specs=out_specs, check_vma=False)
```

```python
import functools
import math

import jax
import jax.numpy as jnp
import numpy as np
from jax import lax
from jax.experimental import pallas as pl
from jax.experimental.pallas import tpu as pltpu
from jax.sharding import PartitionSpec as P

DIRS = 24
FREQ = 25
TROWS = 8
NY = 256
SEA = 1536
SEND = 12
GROUPS = 4
TILES = 128
LOCAL = DIRS * FREQ // GROUPS
ROWS = 152
DEPTH = 160
MAIN = 128
EXTRA = ROWS - MAIN
PER_TILE = 5
SLOTS = 15
GRAV = 9.81
LOW_FREQ = 0.0418
FREQ_STEP = 1.1

VMEM = pl.BlockSpec(memory_space=pltpu.VMEM)

W_E, W_I, C_COS, C_SIN, C_OUT = range(5)
PHASES = 32
PACKS = 4
SHORT = PHASES // PACKS
LINES = (PHASES + SHORT) * 8
CHUNK = 4
PAD = 8
PARTS = 4
HALF = TROWS * NY // 2


def coefficient_tables():
    table = np.zeros((GROUPS, ROWS, 128), np.float64)
    courant = np.zeros((GROUPS, 8, 256), np.float64)
    for group in range(GROUPS):
        for row in range(LOCAL):
            d, j = row // FREQ + group * (DIRS // GROUPS), row % FREQ
            angle = 2.0 * math.pi * (d + 0.5) / DIRS
            freq = LOW_FREQ * FREQ_STEP**j
            s = 2.0 * math.pi * freq
            w = 2.0 * math.pi / DIRS * 0.1 * freq
            reach = 0.45 * (2.0 * math.pi * LOW_FREQ) / s
            ux, uy = abs(reach * math.cos(angle)), abs(reach * math.sin(angle))
            push = 0.1 * 28.0 * 0.035 * s / GRAV
            table[group, row, :5] = (
                w, w / s, push * math.cos(angle), push * math.sin(angle), 0.4 * s * s
            )
            if row < MAIN:
                lanes = [row]
            else:
                lanes = [128 + pack * 32 + row - MAIN for pack in range(PACKS)]
            for lane in lanes:
                courant[group, :4, lane] = (ux, ux * (1.0 - ux), uy, uy * (1.0 - uy))
    return table.astype(np.float32), courant.astype(np.float32)


def pack_kernel(x_hbm, speed_hbm, heading_hbm, out_hbm, x_ref, wind_ref, z_ref, b_ref, m_ref,
                sem_in, sem_wind, sem_out):
    width = SEA // PARTS
    tiles = TILES // PARTS
    ins = [
        pltpu.make_async_copy(x_hbm.at[:, pl.ds(c * width, width)], x_ref.at[c], sem_in.at[c])
        for c in range(PARTS)
    ]
    winds = [
        pltpu.make_async_copy(ref, wind_ref.at[i], sem_wind.at[i])
        for i, ref in enumerate((speed_hbm, heading_hbm))
    ]
    outs = [
        pltpu.make_async_copy(
            m_ref.at[pl.ds(c * tiles * SLOTS, tiles * SLOTS)],
            out_hbm.at[pl.ds(c * tiles * SLOTS, tiles * SLOTS)],
            sem_out.at[c],
        )
        for c in range(PARTS)
    ]
    ins[0].start()
    winds[0].start()
    winds[1].start()
    for c in range(1, PARTS):
        ins[c].start()
    b_ref[PER_TILE * EXTRA : 128, :] = jnp.zeros((128 - PER_TILE * EXTRA, width), jnp.float32)
    lane = lax.broadcasted_iota(jnp.int32, (tiles, 128), 1)
    for c in range(PARTS):
        ins[c].wait()
        if c == 0:
            winds[0].wait()
            winds[1].wait()
        for copy in range(PER_TILE):
            b_ref[copy * EXTRA : copy * EXTRA + LOCAL - MAIN, :] = x_ref[c, MAIN:LOCAL, :]
        for block in range(width // 128):
            cols = slice(block * 128, block * 128 + 128)
            at = c * (width // 128) + block
            for copy in range(PER_TILE):
                for i in range(2):
                    row = copy * EXTRA + LOCAL - MAIN + i
                    b_ref[row : row + 1, cols] = wind_ref[i, at : at + 1, :]
            z_ref[0, cols, :] = x_ref[c, 0:MAIN, cols].T
            z_ref[1, cols, :] = b_ref[:, cols].T
        first = c * tiles * SLOTS
        for k in range(SEND):
            m_ref[pl.ds(first + k, tiles, stride=SLOTS), :] = z_ref[
                0, pl.ds(k, tiles, stride=SEND), :
            ]
        for tile in range(SLOTS - SEND):
            total = None
            for k in range(tile * PER_TILE, min(SEND, (tile + 1) * PER_TILE)):
                piece = z_ref[1, pl.ds(k, tiles, stride=SEND), :]
                start = (k % PER_TILE) * EXTRA
                total = piece if total is None else jnp.where(lane < start, total, piece)
            m_ref[pl.ds(first + SEND + tile, tiles, stride=SLOTS), :] = total
        outs[c].start()
    for c in range(PARTS):
        outs[c].wait()


def moments_kernel(r_ref, tab_ref, y_ref, wind_ref, e_ref):
    extra = None
    we = jnp.broadcast_to(tab_ref[:, W_E : W_E + 1], (ROWS, 128))
    wi = jnp.broadcast_to(tab_ref[:, W_I : W_I + 1], (ROWS, 128))
    for k in range(SEND):
        if k % PER_TILE == 0:
            extra = r_ref[pl.ds(SEND + k // PER_TILE, TILES, stride=SLOTS), :].T
        part = extra[(k % PER_TILE) * EXTRA : (k % PER_TILE + 1) * EXTRA, :]
        main = r_ref[pl.ds(k, TILES, stride=SLOTS), :].T
        y_ref[k, 0:MAIN, :] = main
        y_ref[k, MAIN:ROWS, :] = part
        wind_ref[k : k + 1, :] = part[LOCAL - MAIN : LOCAL - MAIN + 1, :]
        wind_ref[SEND + k : SEND + k + 1, :] = part[LOCAL - MAIN + 1 : EXTRA, :]
        y = y_ref[k]
        energy = jnp.sum(y * we, axis=0, keepdims=True)
        inverse = jnp.sum(y * wi, axis=0, keepdims=True)
        for g in range(GROUPS):
            e_ref[g, k : k + 1, :] = energy
            e_ref[g, SEND + k : SEND + k + 1, :] = inverse


def onehot_kernel(cell_ref, out_ref):
    row = lax.broadcasted_iota(jnp.int32, (16, 128), 0)
    base = row % 8 * 32 + row // 8
    spots = [cell_ref[k : k + 1, :] - base for k in range(SEND)]

    def body(e, carry):
        for phase in range(0, PHASES, 2):
            pack, short = phase // SHORT, phase % SHORT
            line = ((e // 4 * PACKS + pack) * 4 + e % 4) * SHORT * 8 + short * 8
            for k in range(SEND):
                hit = spots[k] == e * NY + phase
                out_ref[pl.ds(pl.multiple_of(line, 16), 16), k * 128 : (k + 1) * 128] = jnp.where(
                    hit, 1.0, 0.0
                ).astype(jnp.bfloat16)
        return carry

    lax.fori_loop(0, TROWS, body, 0)


def spread(held_ref, main, side, ref, packs):
    turned = (((1,), (1,)), ((), ()))
    block = SHORT * 8
    hot = held_ref[packs[0] * 4 * block : (packs[-1] + 1) * 4 * block, :]
    out = lax.dot_general(hot, main, turned, preferred_element_type=jnp.float32)
    out = out[:, 0:128] + out[:, 128:256]
    rest = lax.dot_general(hot, side, turned, preferred_element_type=jnp.float32)
    rest = rest[:, 0:128] + rest[:, 128:256]
    lane = lax.broadcasted_iota(jnp.int32, (block, 128), 1)
    for i in range(4):
        total = ref[i, PHASES * 8 : LINES, :] if packs[0] else None
        for pack in packs:
            line = ((pack - packs[0]) * 4 + i) * block
            ref[i, pack * block : (pack + 1) * block, :] = out[line : line + block]
            part = rest[line : line + block]
            total = part if total is None else jnp.where(lane < pack * 32, total, part)
        ref[i, PHASES * 8 : LINES, :] = total


def place_kernel(y_ref, wind_ref, e_ref, tab_ref, hot_ref, first_ref, main_ref, side_ref,
                 kept_ref, s_ref, held_ref, sem):
    quarter = HALF // 2
    copies = [
        pltpu.make_async_copy(
            hot_ref.at[pl.ds(h * quarter, quarter)],
            held_ref.at[pl.ds(h * quarter, quarter)],
            sem.at[h],
        )
        for h in range(2)
    ]
    copies.append(pltpu.make_async_copy(hot_ref.at[pl.ds(HALF, HALF)], kept_ref, sem.at[2]))
    copies[0].start()
    copies[1].start()
    moments = e_ref[0] + e_ref[1] + e_ref[2] + e_ref[3]
    energy, inverse = moments[0:SEND], moments[SEND : 2 * SEND]
    mean = energy / inverse
    wavenumber = mean * mean / GRAV
    steepness = energy * wavenumber * wavenumber
    ratio = steepness / (steepness + 0.02)
    decay = ratio / (mean * mean)
    speed, heading = wind_ref[0:SEND, :], wind_ref[SEND : 2 * SEND, :]
    along = speed * jnp.cos(heading)
    across = speed * jnp.sin(heading)
    ccos = jnp.broadcast_to(tab_ref[:, C_COS : C_COS + 1], (ROWS, 128))
    csin = jnp.broadcast_to(tab_ref[:, C_SIN : C_SIN + 1], (ROWS, 128))
    cout = jnp.broadcast_to(tab_ref[:, C_OUT : C_OUT + 1], (ROWS, 128))
    row = lax.broadcasted_iota(jnp.int32, (ROWS, 128), 0)
    s_ref[ROWS:DEPTH, :] = jnp.zeros((DEPTH - ROWS, SEA), jnp.float32)
    for k in range(SEND):
        grow = ccos * along[k : k + 1] + csin * across[k : k + 1]
        rate = jnp.maximum(grow - 0.1, 0.0) - cout * decay[k : k + 1]
        value = y_ref[k] * jnp.exp(rate)
        value = jnp.where(row < LOCAL, value, 0.0)
        s_ref[0:ROWS, k * 128 : (k + 1) * 128] = value
    value = s_ref[...]
    high = value.astype(jnp.bfloat16)
    rest = (value - high.astype(jnp.float32)).astype(jnp.bfloat16)
    main_ref[0:MAIN, :] = high[0:MAIN]
    main_ref[MAIN:256, :] = rest[0:MAIN]
    for pack in range(PACKS):
        side_ref[pack * 32 : pack * 32 + 32, :] = high[MAIN:DEPTH]
        side_ref[128 + pack * 32 : 128 + pack * 32 + 32, :] = rest[MAIN:DEPTH]
    first_ref[:, LINES : LINES + PAD, :] = jnp.zeros((4, PAD, 128), jnp.float32)
    copies[0].wait()
    copies[2].start()
    spread(held_ref, main_ref[...], side_ref[...], first_ref, (0, 1))
    copies[1].wait()
    spread(held_ref, main_ref[...], side_ref[...], first_ref, (2, 3))
    copies[2].wait()


def place_rest_kernel(main_ref, side_ref, kept_ref, second_ref):
    spread(kept_ref, main_ref[...], side_ref[...], second_ref, (0, 1, 2, 3))


def limited(a, b):
    m = (a + (b + b)) * (1.0 / 6.0)
    least = jnp.minimum(jnp.maximum(a, b), 0.0)
    most = jnp.maximum(jnp.minimum(a, b), 0.0)
    return jnp.minimum(jnp.maximum(m, least), most)


def next_main(x):
    return pltpu.roll(x, 7, 0)


def last_main(x):
    return pltpu.roll(x, 1, 0)


def next_side(x):
    lane = lax.broadcasted_iota(jnp.int32, (8, 128), 1)
    x = pltpu.roll(x, 96, 1)
    return jnp.where(lane >= 96, pltpu.roll(x, 7, 0), x)


def last_side(x):
    lane = lax.broadcasted_iota(jnp.int32, (8, 128), 1)
    x = pltpu.roll(x, 32, 1)
    return jnp.where(lane < 32, pltpu.roll(x, 1, 0), x)


def substep(rows, seas, put, keep_ref, coef, base, phases, after, before):
    ux, kx, uy, ky = coef
    count = len(rows) - 3

    def load(spot, phase):
        ref, at = spot
        return ref[at, pl.ds(pl.multiple_of(base + phase * 8, 8), 8), :]

    for i in range(count):
        spot = rows[i + 2]
        end = load(spot, phases - 1)
        ahead = load(spot, 0) - before(end)
        prior = before(end - load(spot, phases - 2))
        keep_ref[i, 0] = ahead
        keep_ref[i, 1] = uy * before(end) + ky * limited(prior, ahead)

    def body(chunk, carry):
        first = chunk * CHUNK
        following = jnp.where(first + CHUNK == phases, 0, first + CHUNK)
        wraps = first + CHUNK == phases
        q = [load(rows[1], first + j) for j in range(CHUNK)]
        diff = [q[j] - load(rows[0], first + j) for j in range(CHUNK)]
        flux = None
        for i in range(-1, count):
            up = [load(rows[i + 3], first + j) for j in range(CHUNK)]
            slope = [up[j] - q[j] for j in range(CHUNK)]
            gone = [ux * q[j] + kx * limited(diff[j], slope[j]) for j in range(CHUNK)]
            if i >= 0:
                behind, past = keep_ref[i, 0], keep_ref[i, 1]
                edge = load(rows[i + 2], following)
                edge = jnp.where(wraps, after(edge), edge)
                for j in range(CHUNK):
                    ahead = (q[j + 1] if j + 1 < CHUNK else edge) - q[j]
                    side = uy * q[j] + ky * limited(behind, ahead)
                    new = q[j] - ((gone[j] - flux[j]) + (side - past))
                    sea = q[j] if seas is None else load(seas[i], first + j)
                    put(i, first + j, jnp.where(sea > 0.0, new, 0.0))
                    behind, past = ahead, side
                keep_ref[i, 0] = behind
                keep_ref[i, 1] = past
            q, diff, flux = up, slope, gone
        return carry

    lax.fori_loop(0, phases // CHUNK, body, 0)


def flags():
    group = lax.axis_index("grp")
    mirror_x = ((group == 1) | (group == 2)).astype(jnp.int32)
    mirror_y = (group >= 2).astype(jnp.int32)
    odd = lax.axis_index("comp").astype(jnp.int32) % 2
    return mirror_x, mirror_y, odd ^ mirror_x


def halves(tab_ref):
    for base, phases, lanes, after, before in (
        (0, PHASES, 0, next_main, last_main),
        (PHASES * 8, SHORT, 128, next_side, last_side),
    ):
        coef = [
            jnp.broadcast_to(tab_ref[n : n + 1, lanes : lanes + 128], (8, 128)) for n in range(4)
        ]
        yield coef, base, phases, after, before


def writer(ref, base, offset):
    def put(i, phase, value):
        ref[i + offset, pl.ds(pl.multiple_of(base + phase * 8, 8), 8), :] = value

    return put


def last_writer(ref, base, offset, cols_back):
    def put(i, phase, value):
        if base == 0:
            phase = phase + (PHASES - 1 - 2 * phase) * cols_back
        line = (i + offset) * LINES + base + phase * 8
        ref[pl.ds(pl.multiple_of(line, 8), 8), :] = value

    return put


def field(flip, first_ref, second_ref):
    parts = (second_ref, first_ref) if flip else (first_ref, second_ref)
    return [(ref, i) for ref in parts for i in range(4)]


def turned_main(ref, at, half, cols_back):
    parts = []
    for s in range(half * 4, half * 4 + 4):
        start = at * LINES + s + (7 - 2 * s) * cols_back
        parts.append(ref[pl.ds(start, PHASES, stride=8), :])
    return jnp.concatenate(parts, axis=0).T


def turned_side(ref, at):
    line = at * LINES + PHASES * 8
    empty = jnp.zeros((128 - SHORT * 8, 128), jnp.float32)
    return jnp.concatenate([ref[line : line + SHORT * 8, :], empty], axis=0).T


def inner_kernel(tab_ref, first_ref, second_ref, once_ref, done_ref, twice_ref, keep_ref):
    once = [(once_ref, i) for i in range(5)]
    _, cols_back, side_up = flags()
    for flip in range(2):

        @pl.when(side_up == flip)
        def _():
            cells = field(flip, first_ref, second_ref)
            for half in halves(tab_ref):
                base = half[1]
                substep(cells, None, writer(once_ref, base, 0), keep_ref, *half)
                put = last_writer(twice_ref, base, 0, cols_back)
                substep(once, cells[4:6], put, keep_ref, *half)

    for i in range(2):
        done_ref[i, 0] = turned_main(twice_ref, i, 0, cols_back)
        done_ref[i, 1] = turned_main(twice_ref, i, 1, cols_back)
        done_ref[i, 2] = turned_side(twice_ref, i)


def edge(lower, cells, got_ref, inner_ref, once_ref, twice_ref, keep_ref, cols_back, half):
    base = half[1]
    once = [(inner_ref, i) for i in range(5)]
    if lower:
        near = [(got_ref, i) for i in range(4)] + cells[0:3]
        seas, fresh = cells[0:4], [(once_ref, i) for i in range(4)]
        once = fresh + once[0:3]
    else:
        near = cells[5:8] + [(got_ref, i) for i in range(2)]
        seas, fresh = cells[6:8], [(once_ref, i) for i in range(2)]
        once = once[2:5] + fresh
    substep(near, None, writer(once_ref, base, 0), keep_ref, *half)
    substep(once, seas, last_writer(twice_ref, base, 0, cols_back), keep_ref, *half)
    return len(seas)


def near_kernel(tab_ref, first_ref, second_ref, got_ref, inner_ref, done_ref, once_ref,
                twice_ref, keep_ref):
    _, cols_back, side_up = flags()
    for flip in range(2):

        @pl.when(side_up == flip)
        def _():
            cells = field(flip, first_ref, second_ref)
            for half in halves(tab_ref):
                count = edge(flip == 1, cells, got_ref, inner_ref, once_ref, twice_ref, keep_ref,
                             cols_back, half)
            for i in range(count):
                done_ref[i, 0] = turned_main(twice_ref, i, 0, cols_back)
                done_ref[i, 1] = turned_main(twice_ref, i, 1, cols_back)
                done_ref[i, 2] = turned_side(twice_ref, i)


def outer_kernel(tab_ref, first_ref, second_ref, got_ref, inner_ref, done_ref, near_ref,
                 out_hbm, once_ref, twice_ref, keep_ref, turn_ref, rest_ref, last_ref, sem):
    rows_back, cols_back, side_up = flags()

    def blocks(flip, part):
        for e in range(TROWS):
            r = e + (TROWS - 1 - 2 * e) * rows_back
            if e in (4, 5):
                yield r, done_ref[e - 4, part]
                continue
            lower, at = e < 4, e if e < 4 else e - 6
            if lower == (flip == 1):
                yield r, near_ref[at, part]
            elif part == 2:
                yield r, turned_side(twice_ref, at)
            else:
                yield r, turned_main(twice_ref, at, part, cols_back)

    def compute(flip, half):
        cells = field(flip, first_ref, second_ref)
        edge(flip == 0, cells, got_ref, inner_ref, once_ref, twice_ref, keep_ref, cols_back, half)

    main, side = halves(tab_ref)
    copies = [
        pltpu.make_async_copy(
            turn_ref.at[half],
            out_hbm.at[pl.ds(0, MAIN), :, pl.ds(half * 128, 128)],
            sem.at[half],
        )
        for half in range(2)
    ]
    count = LOCAL - MAIN
    copies.append(
        pltpu.make_async_copy(
            last_ref.at[pl.ds(0, count)], out_hbm.at[pl.ds(MAIN, count)], sem.at[2]
        )
    )
    for flip in range(2):

        @pl.when(side_up == flip)
        def _():
            compute(flip, side)
            for r, block in blocks(flip, 2):
                for pack in range(PACKS):
                    rest_ref[pack, pl.ds(r, 32, stride=TROWS), :] = block[
                        pack * 32 : pack * 32 + 32
                    ]

    spot = lax.broadcasted_iota(jnp.int32, (PACKS * 128, NY), 0)
    col = lax.broadcasted_iota(jnp.int32, (PACKS * 128, NY), 1)
    col = col + (NY - 1 - 2 * col) * cols_back
    pack, inner = spot // 128, spot % 128
    wanted = inner % 8 * 32 + pack * SHORT + inner // 8
    order = jnp.where((wanted == col) & (inner < SHORT * 8), 1.0, 0.0).astype(jnp.bfloat16)
    value = jnp.concatenate([rest_ref[pack] for pack in range(PACKS)], axis=1)
    high = value.astype(jnp.bfloat16)
    rest = (value - high.astype(jnp.float32)).astype(jnp.bfloat16)
    value = jnp.dot(high, order, preferred_element_type=jnp.float32)
    value = value + jnp.dot(rest, order, preferred_element_type=jnp.float32)
    for i in range(count):
        last_ref[i] = value[i * TROWS : (i + 1) * TROWS, :]
    copies[2].start()
    for flip in range(2):

        @pl.when(side_up == flip)
        def _():
            compute(flip, main)

    for half in range(2):
        lines = turn_ref.at[half].reshape(MAIN * TROWS, 128)
        for flip in range(2):

            @pl.when(side_up == flip)
            def _():
                for r, block in blocks(flip, half):
                    lines[pl.ds(r, MAIN, stride=TROWS), :] = block

        copies[half].start()
    for copy in copies:
        copy.wait()


def call(kernel, shapes, scratch, ins, *args, limit=20, us=0, outs=None):
    cost = pl.CostEstimate(flops=us * 10**9, bytes_accessed=us * 3 * 10**6, transcendentals=0)
    return pl.pallas_call(
        kernel,
        out_shape=shapes,
        in_specs=ins,
        out_specs=outs or jax.tree.map(lambda _: VMEM, shapes),
        scratch_shapes=scratch,
        cost_estimate=cost if us else None,
        compiler_params=pltpu.CompilerParams(vmem_limit_bytes=limit * 1024 * 1024),
    )(*args)


def f32(*shape):
    return jax.ShapeDtypeStruct(shape, jnp.float32)


def local(spectra, wind_speed, wind_dir, sea_cell):
    group = lax.axis_index("grp")
    table, courant = (
        lax.dynamic_index_in_dim(jnp.asarray(t), group, 0, keepdims=False)
        for t in coefficient_tables()
    )
    mirror_x, mirror_y, flip = flags()
    hbm = pl.BlockSpec(memory_space=pltpu.HBM)
    packed = call(
        pack_kernel,
        f32(TILES * SLOTS, 128),
        [
            pltpu.VMEM((PARTS, LOCAL, SEA // PARTS), jnp.float32),
            pltpu.VMEM((2, SEA // 128, 128), jnp.float32),
            pltpu.VMEM((2, SEA // PARTS, 128), jnp.float32),
            pltpu.VMEM((128, SEA // PARTS), jnp.float32),
            pltpu.VMEM((TILES * SLOTS, 128), jnp.float32),
            pltpu.SemaphoreType.DMA((PARTS,)),
            pltpu.SemaphoreType.DMA((2,)),
            pltpu.SemaphoreType.DMA((PARTS,)),
        ],
        [hbm] * 3,
        spectra,
        wind_speed.reshape(SEA // 128, 128),
        wind_dir.reshape(SEA // 128, 128),
        limit=57,
        outs=hbm,
    )
    received = lax.all_to_all(
        packed.reshape(TILES, 1, SLOTS * 128), "comp", split_axis=0, concat_axis=0, tiled=True
    ).reshape(TILES * SLOTS, 128)
    cells = sea_cell.reshape(TILES, SEND).T
    cells = cells ^ (mirror_x * (NY * (TROWS - 1)) + mirror_y * (NY - 1)) ^ (flip * (NY * TROWS // 2))
    hot = call(
        onehot_kernel,
        jax.ShapeDtypeStruct((TROWS * NY, SEA), jnp.bfloat16),
        [],
        [VMEM],
        cells,
    )
    received, hot = lax.optimization_barrier((received, hot))
    points, wind_here, partial = call(
        moments_kernel,
        (f32(SEND, ROWS, 128), f32(2 * SEND, 128), f32(GROUPS, 2 * SEND, 128)),
        [],
        [VMEM] * 2,
        received,
        table,
    )
    partial = lax.all_to_all(partial, "grp", split_axis=0, concat_axis=0, tiled=True)
    bf16 = functools.partial(jax.ShapeDtypeStruct, dtype=jnp.bfloat16)
    first, main, side, kept = call(
        place_kernel,
        (f32(4, LINES + PAD, 128), bf16((256, SEA)), bf16((256, SEA)), bf16((HALF, SEA))),
        [
            pltpu.VMEM((DEPTH, SEA), jnp.float32),
            pltpu.VMEM((HALF, SEA), jnp.bfloat16),
            pltpu.SemaphoreType.DMA((3,)),
        ],
        [VMEM] * 4 + [hbm],
        points,
        wind_here,
        partial,
        table,
        hot,
        limit=44,
    )
    second = call(
        place_rest_kernel,
        f32(4, LINES, 128),
        [],
        [VMEM] * 3,
        main,
        side,
        kept,
        us=2,
    )
    across, within = [], []
    for g in range(GROUPS):
        for i in range(TILES - 1):
            low, high = g * TILES + i, g * TILES + i + 1
            (across if i % 2 else within).extend([(low, high), (high, low)])
    got_first = lax.ppermute(first, ("grp", "comp"), across)
    got_second = lax.ppermute(second, ("grp", "comp"), within)
    once, done = call(
        inner_kernel,
        (f32(5, LINES, 128), f32(2, 3, 128, 128)),
        [pltpu.VMEM((2 * LINES, 128), jnp.float32), pltpu.VMEM((5, 2, 8, 128), jnp.float32)],
        [VMEM] * 3,
        courant,
        first,
        second,
        us=3,
    )
    near = call(
        near_kernel,
        f32(4, 3, 128, 128),
        [
            pltpu.VMEM((4, LINES, 128), jnp.float32),
            pltpu.VMEM((4 * LINES, 128), jnp.float32),
            pltpu.VMEM((4, 2, 8, 128), jnp.float32),
        ],
        [VMEM] * 5,
        courant,
        first,
        second,
        got_second,
        once,
        us=0,
    )
    return call(
        outer_kernel,
        f32(LOCAL, TROWS, NY),
        [
            pltpu.VMEM((4, LINES, 128), jnp.float32),
            pltpu.VMEM((4 * LINES, 128), jnp.float32),
            pltpu.VMEM((4, 2, 8, 128), jnp.float32),
            pltpu.VMEM((2, MAIN, TROWS, 128), jnp.float32),
            pltpu.VMEM((PACKS, 32 * TROWS, 128), jnp.float32),
            pltpu.VMEM((32, TROWS, NY), jnp.float32),
            pltpu.SemaphoreType.DMA((3,)),
        ],
        [VMEM] * 7,
        courant,
        first,
        second,
        got_first,
        once,
        done,
        near,
        outs=hbm,
    )


def solution(mesh):
    in_specs = (P("grp", "comp"), P("comp"), P("comp"), P("comp"))
    out_specs = P("grp", "comp", None)
    return jax.shard_map(local, mesh=mesh, in_specs=in_specs, out_specs=out_specs, check_vma=False)
```

```python
import functools
import math

import jax
import jax.numpy as jnp
import numpy as np
from jax import lax
from jax.experimental import pallas as pl
from jax.experimental.pallas import tpu as pltpu
from jax.sharding import PartitionSpec as P

DIRS = 24
FREQ = 25
TROWS = 8
NY = 256
SEA = 1536
SEND = 12
GROUPS = 4
TILES = 128
LOCAL = DIRS * FREQ // GROUPS
ROWS = 152
DEPTH = 160
MAIN = 128
EXTRA = ROWS - MAIN
PER_TILE = 5
SLOTS = 15
GRAV = 9.81
LOW_FREQ = 0.0418
FREQ_STEP = 1.1

VMEM = pl.BlockSpec(memory_space=pltpu.VMEM)

W_E, W_I, C_COS, C_SIN, C_OUT = range(5)
PHASES = 32
PACKS = 4
SHORT = PHASES // PACKS
LINES = (PHASES + SHORT) * 8
CHUNK = 8
PAD = 8
PARTS = 4
HALF = TROWS * NY // 2


def coefficient_tables():
    table = np.zeros((GROUPS, ROWS, 128), np.float64)
    courant = np.zeros((GROUPS, 8, 256), np.float64)
    for group in range(GROUPS):
        for row in range(LOCAL):
            d, j = row // FREQ + group * (DIRS // GROUPS), row % FREQ
            angle = 2.0 * math.pi * (d + 0.5) / DIRS
            freq = LOW_FREQ * FREQ_STEP**j
            s = 2.0 * math.pi * freq
            w = 2.0 * math.pi / DIRS * 0.1 * freq
            reach = 0.45 * (2.0 * math.pi * LOW_FREQ) / s
            ux, uy = abs(reach * math.cos(angle)), abs(reach * math.sin(angle))
            push = 0.1 * 28.0 * 0.035 * s / GRAV
            table[group, row, :5] = (
                w, w / s, push * math.cos(angle), push * math.sin(angle), 0.4 * s * s
            )
            if row < MAIN:
                lanes = [row]
            else:
                lanes = [128 + pack * 32 + row - MAIN for pack in range(PACKS)]
            for lane in lanes:
                courant[group, :4, lane] = (ux, ux * (1.0 - ux), uy, uy * (1.0 - uy))
    return table.astype(np.float32), courant.astype(np.float32)


def pack_kernel(x_hbm, speed_hbm, heading_hbm, out_hbm, x_ref, wind_ref, z_ref, b_ref, m_ref,
                sem_in, sem_wind, sem_out):
    width = SEA // PARTS
    tiles = TILES // PARTS
    ins = [
        pltpu.make_async_copy(x_hbm.at[:, pl.ds(c * width, width)], x_ref.at[c], sem_in.at[c])
        for c in range(PARTS)
    ]
    winds = [
        pltpu.make_async_copy(ref, wind_ref.at[i], sem_wind.at[i])
        for i, ref in enumerate((speed_hbm, heading_hbm))
    ]
    outs = [
        pltpu.make_async_copy(
            m_ref.at[pl.ds(c * tiles * SLOTS, tiles * SLOTS)],
            out_hbm.at[pl.ds(c * tiles * SLOTS, tiles * SLOTS)],
            sem_out.at[c],
        )
        for c in range(PARTS)
    ]
    ins[0].start()
    winds[0].start()
    winds[1].start()
    for c in range(1, PARTS):
        ins[c].start()
    b_ref[PER_TILE * EXTRA : 128, :] = jnp.zeros((128 - PER_TILE * EXTRA, width), jnp.float32)
    lane = lax.broadcasted_iota(jnp.int32, (tiles, 128), 1)
    for c in range(PARTS):
        if c == 0:
            winds[0].wait()
            winds[1].wait()
            speed, heading = wind_ref[0], wind_ref[1]
            wind_ref[0] = speed * jnp.cos(heading)
            wind_ref[1] = speed * jnp.sin(heading)
        ins[c].wait()
        for copy in range(PER_TILE):
            b_ref[copy * EXTRA : copy * EXTRA + LOCAL - MAIN, :] = x_ref[c, MAIN:LOCAL, :]
        for block in range(width // 128):
            cols = slice(block * 128, block * 128 + 128)
            at = c * (width // 128) + block
            for copy in range(PER_TILE):
                for i in range(2):
                    row = copy * EXTRA + LOCAL - MAIN + i
                    b_ref[row : row + 1, cols] = wind_ref[i, at : at + 1, :]
            z_ref[0, cols, :] = x_ref[c, 0:MAIN, cols].T
            z_ref[1, cols, :] = b_ref[:, cols].T
        first = c * tiles * SLOTS
        for k in range(SEND):
            m_ref[pl.ds(first + k, tiles, stride=SLOTS), :] = z_ref[
                0, pl.ds(k, tiles, stride=SEND), :
            ]
        for tile in range(SLOTS - SEND):
            total = None
            for k in range(tile * PER_TILE, min(SEND, (tile + 1) * PER_TILE)):
                piece = z_ref[1, pl.ds(k, tiles, stride=SEND), :]
                start = (k % PER_TILE) * EXTRA
                total = piece if total is None else jnp.where(lane < start, total, piece)
            m_ref[pl.ds(first + SEND + tile, tiles, stride=SLOTS), :] = total
        outs[c].start()
    for c in range(PARTS):
        outs[c].wait()


def moments_kernel(r_ref, tab_ref, y_ref, wind_ref, e_ref):
    extra = None
    we = jnp.broadcast_to(tab_ref[:, W_E : W_E + 1], (ROWS, 128))
    wi = jnp.broadcast_to(tab_ref[:, W_I : W_I + 1], (ROWS, 128))
    for k in range(SEND):
        if k % PER_TILE == 0:
            extra = r_ref[pl.ds(SEND + k // PER_TILE, TILES, stride=SLOTS), :].T
        part = extra[(k % PER_TILE) * EXTRA : (k % PER_TILE + 1) * EXTRA, :]
        main = r_ref[pl.ds(k, TILES, stride=SLOTS), :].T
        y_ref[k, 0:MAIN, :] = main
        y_ref[k, MAIN:ROWS, :] = part
        wind_ref[k : k + 1, :] = part[LOCAL - MAIN : LOCAL - MAIN + 1, :]
        wind_ref[SEND + k : SEND + k + 1, :] = part[LOCAL - MAIN + 1 : EXTRA, :]
        y = y_ref[k]
        energy = jnp.sum(y * we, axis=0, keepdims=True)
        inverse = jnp.sum(y * wi, axis=0, keepdims=True)
        for g in range(GROUPS):
            e_ref[g, k : k + 1, :] = energy
            e_ref[g, SEND + k : SEND + k + 1, :] = inverse


def onehot_kernel(cell_ref, out_ref):
    row = lax.broadcasted_iota(jnp.int32, (16, 128), 0)
    base = row % 8 * 32 + row // 8
    spots = [cell_ref[k : k + 1, :] - base for k in range(SEND)]

    def body(e, carry):
        for phase in range(0, PHASES, 2):
            pack, short = phase // SHORT, phase % SHORT
            line = ((e // 4 * PACKS + pack) * 4 + e % 4) * SHORT * 8 + short * 8
            for k in range(SEND):
                hit = spots[k] == e * NY + phase
                out_ref[pl.ds(pl.multiple_of(line, 16), 16), k * 128 : (k + 1) * 128] = jnp.where(
                    hit, 1.0, 0.0
                ).astype(jnp.bfloat16)
        return carry

    lax.fori_loop(0, TROWS, body, 0)


def spread(held_ref, main, side, ref, packs):
    turned = (((1,), (1,)), ((), ()))
    block = SHORT * 8
    hot = held_ref[packs[0] * 4 * block : (packs[-1] + 1) * 4 * block, :]
    out = lax.dot_general(hot, main, turned, preferred_element_type=jnp.float32)
    out = out[:, 0:128] + out[:, 128:256]
    rest = lax.dot_general(hot, side, turned, preferred_element_type=jnp.float32)
    rest = rest[:, 0:128] + rest[:, 128:256]
    lane = lax.broadcasted_iota(jnp.int32, (block, 128), 1)
    for i in range(4):
        total = ref[i, PHASES * 8 : LINES, :] if packs[0] else None
        for pack in packs:
            line = ((pack - packs[0]) * 4 + i) * block
            ref[i, pack * block : (pack + 1) * block, :] = out[line : line + block]
            part = rest[line : line + block]
            total = part if total is None else jnp.where(lane < pack * 32, total, part)
        ref[i, PHASES * 8 : LINES, :] = total


def place_kernel(y_ref, wind_ref, e_ref, tab_ref, hot_ref, first_ref, main_ref, side_ref,
                 kept_ref, s_ref, held_ref, sem):
    quarter = HALF // 2
    copies = [
        pltpu.make_async_copy(
            hot_ref.at[pl.ds(h * quarter, quarter)],
            held_ref.at[pl.ds(h * quarter, quarter)],
            sem.at[h],
        )
        for h in range(2)
    ]
    copies.append(pltpu.make_async_copy(hot_ref.at[pl.ds(HALF, HALF)], kept_ref, sem.at[2]))
    copies[0].start()
    copies[1].start()
    moments = e_ref[0] + e_ref[1] + e_ref[2] + e_ref[3]
    energy, inverse = moments[0:SEND], moments[SEND : 2 * SEND]
    mean = energy / inverse
    wavenumber = mean * mean / GRAV
    steepness = energy * wavenumber * wavenumber
    ratio = steepness / (steepness + 0.02)
    decay = ratio / (mean * mean)
    along, across = wind_ref[0:SEND, :], wind_ref[SEND : 2 * SEND, :]
    ccos = jnp.broadcast_to(tab_ref[:, C_COS : C_COS + 1], (ROWS, 128))
    csin = jnp.broadcast_to(tab_ref[:, C_SIN : C_SIN + 1], (ROWS, 128))
    cout = jnp.broadcast_to(tab_ref[:, C_OUT : C_OUT + 1], (ROWS, 128))
    row = lax.broadcasted_iota(jnp.int32, (ROWS, 128), 0)
    s_ref[ROWS:DEPTH, :] = jnp.zeros((DEPTH - ROWS, SEA), jnp.float32)
    for k in range(SEND):
        grow = ccos * along[k : k + 1] + csin * across[k : k + 1]
        rate = jnp.maximum(grow - 0.1, 0.0) - cout * decay[k : k + 1]
        value = y_ref[k] * jnp.exp(rate)
        value = jnp.where(row < LOCAL, value, 0.0)
        s_ref[0:ROWS, k * 128 : (k + 1) * 128] = value
    value = s_ref[...]
    high = value.astype(jnp.bfloat16)
    rest = (value - high.astype(jnp.float32)).astype(jnp.bfloat16)
    main_ref[0:MAIN, :] = high[0:MAIN]
    main_ref[MAIN:256, :] = rest[0:MAIN]
    for pack in range(PACKS):
        side_ref[pack * 32 : pack * 32 + 32, :] = high[MAIN:DEPTH]
        side_ref[128 + pack * 32 : 128 + pack * 32 + 32, :] = rest[MAIN:DEPTH]
    first_ref[:, LINES : LINES + PAD, :] = jnp.zeros((4, PAD, 128), jnp.float32)
    copies[0].wait()
    copies[2].start()
    spread(held_ref, main_ref[...], side_ref[...], first_ref, (0, 1))
    copies[1].wait()
    spread(held_ref, main_ref[...], side_ref[...], first_ref, (2, 3))
    copies[2].wait()


def place_rest_kernel(main_ref, side_ref, kept_ref, second_ref):
    spread(kept_ref, main_ref[...], side_ref[...], second_ref, (0, 1, 2, 3))


def limited(a, b):
    m = (a + (b + b)) * (1.0 / 6.0)
    least = jnp.minimum(jnp.maximum(a, b), 0.0)
    most = jnp.maximum(jnp.minimum(a, b), 0.0)
    return jnp.minimum(jnp.maximum(m, least), most)


def next_main(x):
    return pltpu.roll(x, 7, 0)


def last_main(x):
    return pltpu.roll(x, 1, 0)


def next_side(x):
    lane = lax.broadcasted_iota(jnp.int32, (8, 128), 1)
    x = pltpu.roll(x, 96, 1)
    return jnp.where(lane >= 96, pltpu.roll(x, 7, 0), x)


def last_side(x):
    lane = lax.broadcasted_iota(jnp.int32, (8, 128), 1)
    x = pltpu.roll(x, 32, 1)
    return jnp.where(lane < 32, pltpu.roll(x, 1, 0), x)


def substep(rows, seas, put, keep_ref, coef, base, phases, after, before):
    ux, kx, uy, ky = coef
    count = len(rows) - 3

    def load(spot, phase):
        ref, at = spot
        return ref[at, pl.ds(pl.multiple_of(base + phase * 8, 8), 8), :]

    for i in range(count):
        spot = rows[i + 2]
        end = load(spot, phases - 1)
        ahead = load(spot, 0) - before(end)
        prior = before(end - load(spot, phases - 2))
        keep_ref[i, 0] = ahead
        keep_ref[i, 1] = uy * before(end) + ky * limited(prior, ahead)

    def body(chunk, carry):
        first = chunk * CHUNK
        following = jnp.where(first + CHUNK == phases, 0, first + CHUNK)
        wraps = first + CHUNK == phases
        q = [load(rows[1], first + j) for j in range(CHUNK)]
        diff = [q[j] - load(rows[0], first + j) for j in range(CHUNK)]
        flux = None
        for i in range(-1, count):
            up = [load(rows[i + 3], first + j) for j in range(CHUNK)]
            slope = [up[j] - q[j] for j in range(CHUNK)]
            gone = [ux * q[j] + kx * limited(diff[j], slope[j]) for j in range(CHUNK)]
            if i >= 0:
                behind, past = keep_ref[i, 0], keep_ref[i, 1]
                edge = load(rows[i + 2], following)
                edge = jnp.where(wraps, after(edge), edge)
                for j in range(CHUNK):
                    ahead = (q[j + 1] if j + 1 < CHUNK else edge) - q[j]
                    side = uy * q[j] + ky * limited(behind, ahead)
                    new = q[j] - ((gone[j] - flux[j]) + (side - past))
                    sea = q[j] if seas is None else load(seas[i], first + j)
                    put(i, first + j, jnp.where(sea > 0.0, new, 0.0))
                    behind, past = ahead, side
                keep_ref[i, 0] = behind
                keep_ref[i, 1] = past
            q, diff, flux = up, slope, gone
        return carry

    lax.fori_loop(0, phases // CHUNK, body, 0)


def flags():
    group = lax.axis_index("grp")
    mirror_x = ((group == 1) | (group == 2)).astype(jnp.int32)
    mirror_y = (group >= 2).astype(jnp.int32)
    odd = lax.axis_index("comp").astype(jnp.int32) % 2
    return mirror_x, mirror_y, odd ^ mirror_x


def halves(tab_ref):
    for base, phases, lanes, after, before in (
        (0, PHASES, 0, next_main, last_main),
        (PHASES * 8, SHORT, 128, next_side, last_side),
    ):
        coef = [
            jnp.broadcast_to(tab_ref[n : n + 1, lanes : lanes + 128], (8, 128)) for n in range(4)
        ]
        yield coef, base, phases, after, before


def writer(ref, base, offset):
    def put(i, phase, value):
        ref[i + offset, pl.ds(pl.multiple_of(base + phase * 8, 8), 8), :] = value

    return put


def last_writer(ref, base, offset, cols_back):
    def put(i, phase, value):
        if base == 0:
            phase = phase + (PHASES - 1 - 2 * phase) * cols_back
        line = (i + offset) * LINES + base + phase * 8
        ref[pl.ds(pl.multiple_of(line, 8), 8), :] = value

    return put


def field(flip, first_ref, second_ref):
    parts = (second_ref, first_ref) if flip else (first_ref, second_ref)
    return [(ref, i) for ref in parts for i in range(4)]


def turned_main(ref, at, half, cols_back):
    parts = []
    for s in range(half * 4, half * 4 + 4):
        start = at * LINES + s + (7 - 2 * s) * cols_back
        parts.append(ref[pl.ds(start, PHASES, stride=8), :])
    return jnp.concatenate(parts, axis=0).T


def turned_side(ref, at):
    line = at * LINES + PHASES * 8
    empty = jnp.zeros((128 - SHORT * 8, 128), jnp.float32)
    return jnp.concatenate([ref[line : line + SHORT * 8, :], empty], axis=0).T


def inner_kernel(tab_ref, first_ref, second_ref, once_ref, done_ref, twice_ref, keep_ref):
    once = [(once_ref, i) for i in range(5)]
    _, cols_back, side_up = flags()
    for flip in range(2):

        @pl.when(side_up == flip)
        def _():
            cells = field(flip, first_ref, second_ref)
            for half in halves(tab_ref):
                base = half[1]
                substep(cells, None, writer(once_ref, base, 0), keep_ref, *half)
                put = last_writer(twice_ref, base, 0, cols_back)
                substep(once, cells[4:6], put, keep_ref, *half)

    for i in range(2):
        done_ref[i, 0] = turned_main(twice_ref, i, 0, cols_back)
        done_ref[i, 1] = turned_main(twice_ref, i, 1, cols_back)
        done_ref[i, 2] = turned_side(twice_ref, i)


def edge(lower, cells, got_ref, inner_ref, once_ref, twice_ref, keep_ref, cols_back, half):
    base = half[1]
    once = [(inner_ref, i) for i in range(5)]
    if lower:
        near = [(got_ref, i) for i in range(4)] + cells[0:3]
        seas, fresh = cells[0:4], [(once_ref, i) for i in range(4)]
        once = fresh + once[0:3]
    else:
        near = cells[5:8] + [(got_ref, i) for i in range(2)]
        seas, fresh = cells[6:8], [(once_ref, i) for i in range(2)]
        once = once[2:5] + fresh
    substep(near, None, writer(once_ref, base, 0), keep_ref, *half)
    substep(once, seas, last_writer(twice_ref, base, 0, cols_back), keep_ref, *half)
    return len(seas)


def near_kernel(tab_ref, first_ref, second_ref, got_ref, inner_ref, done_ref, once_ref,
                twice_ref, keep_ref):
    _, cols_back, side_up = flags()
    for flip in range(2):

        @pl.when(side_up == flip)
        def _():
            cells = field(flip, first_ref, second_ref)
            for half in halves(tab_ref):
                count = edge(flip == 1, cells, got_ref, inner_ref, once_ref, twice_ref, keep_ref,
                             cols_back, half)
            for i in range(count):
                done_ref[i, 0] = turned_main(twice_ref, i, 0, cols_back)
                done_ref[i, 1] = turned_main(twice_ref, i, 1, cols_back)
                done_ref[i, 2] = turned_side(twice_ref, i)


def outer_kernel(tab_ref, first_ref, second_ref, got_ref, inner_ref, done_ref, near_ref,
                 out_hbm, once_ref, twice_ref, keep_ref, turn_ref, rest_ref, last_ref, sem):
    rows_back, cols_back, side_up = flags()

    def blocks(flip, part):
        for e in range(TROWS):
            r = e + (TROWS - 1 - 2 * e) * rows_back
            if e in (4, 5):
                yield r, done_ref[e - 4, part]
                continue
            lower, at = e < 4, e if e < 4 else e - 6
            if lower == (flip == 1):
                yield r, near_ref[at, part]
            elif part == 2:
                yield r, turned_side(twice_ref, at)
            else:
                yield r, turned_main(twice_ref, at, part, cols_back)

    def compute(flip, half):
        cells = field(flip, first_ref, second_ref)
        edge(flip == 0, cells, got_ref, inner_ref, once_ref, twice_ref, keep_ref, cols_back, half)

    main, side = halves(tab_ref)
    copies = [
        pltpu.make_async_copy(
            turn_ref.at[half],
            out_hbm.at[pl.ds(0, MAIN), :, pl.ds(half * 128, 128)],
            sem.at[half],
        )
        for half in range(2)
    ]
    count = LOCAL - MAIN
    copies.append(
        pltpu.make_async_copy(
            last_ref.at[pl.ds(0, count)], out_hbm.at[pl.ds(MAIN, count)], sem.at[2]
        )
    )
    for flip in range(2):

        @pl.when(side_up == flip)
        def _():
            compute(flip, side)
            for r, block in blocks(flip, 2):
                for pack in range(PACKS):
                    rest_ref[pack, pl.ds(r, 32, stride=TROWS), :] = block[
                        pack * 32 : pack * 32 + 32
                    ]

    spot = lax.broadcasted_iota(jnp.int32, (PACKS * 128, NY), 0)
    col = lax.broadcasted_iota(jnp.int32, (PACKS * 128, NY), 1)
    col = col + (NY - 1 - 2 * col) * cols_back
    pack, inner = spot // 128, spot % 128
    wanted = inner % 8 * 32 + pack * SHORT + inner // 8
    order = jnp.where((wanted == col) & (inner < SHORT * 8), 1.0, 0.0).astype(jnp.bfloat16)
    value = jnp.concatenate([rest_ref[pack] for pack in range(PACKS)], axis=1)
    high = value.astype(jnp.bfloat16)
    rest = (value - high.astype(jnp.float32)).astype(jnp.bfloat16)
    value = jnp.dot(high, order, preferred_element_type=jnp.float32)
    value = value + jnp.dot(rest, order, preferred_element_type=jnp.float32)
    for i in range(count):
        last_ref[i] = value[i * TROWS : (i + 1) * TROWS, :]
    copies[2].start()
    for flip in range(2):

        @pl.when(side_up == flip)
        def _():
            compute(flip, main)

    for half in range(2):
        lines = turn_ref.at[half].reshape(MAIN * TROWS, 128)
        for flip in range(2):

            @pl.when(side_up == flip)
            def _():
                for r, block in blocks(flip, half):
                    lines[pl.ds(r, MAIN, stride=TROWS), :] = block

        copies[half].start()
    for copy in copies:
        copy.wait()


def call(kernel, shapes, scratch, ins, *args, limit=20, us=0, outs=None):
    cost = pl.CostEstimate(flops=us * 10**9, bytes_accessed=us * 3 * 10**6, transcendentals=0)
    return pl.pallas_call(
        kernel,
        out_shape=shapes,
        in_specs=ins,
        out_specs=outs or jax.tree.map(lambda _: VMEM, shapes),
        scratch_shapes=scratch,
        cost_estimate=cost if us else None,
        compiler_params=pltpu.CompilerParams(vmem_limit_bytes=limit * 1024 * 1024),
    )(*args)


def f32(*shape):
    return jax.ShapeDtypeStruct(shape, jnp.float32)


def local(spectra, wind_speed, wind_dir, sea_cell):
    group = lax.axis_index("grp")
    table, courant = (
        lax.dynamic_index_in_dim(jnp.asarray(t), group, 0, keepdims=False)
        for t in coefficient_tables()
    )
    mirror_x, mirror_y, flip = flags()
    hbm = pl.BlockSpec(memory_space=pltpu.HBM)
    packed = call(
        pack_kernel,
        f32(TILES * SLOTS, 128),
        [
            pltpu.VMEM((PARTS, LOCAL, SEA // PARTS), jnp.float32),
            pltpu.VMEM((2, SEA // 128, 128), jnp.float32),
            pltpu.VMEM((2, SEA // PARTS, 128), jnp.float32),
            pltpu.VMEM((128, SEA // PARTS), jnp.float32),
            pltpu.VMEM((TILES * SLOTS, 128), jnp.float32),
            pltpu.SemaphoreType.DMA((PARTS,)),
            pltpu.SemaphoreType.DMA((2,)),
            pltpu.SemaphoreType.DMA((PARTS,)),
        ],
        [hbm] * 3,
        spectra,
        wind_speed.reshape(SEA // 128, 128),
        wind_dir.reshape(SEA // 128, 128),
        limit=57,
        outs=hbm,
    )
    received = lax.all_to_all(
        packed.reshape(TILES, 1, SLOTS * 128), "comp", split_axis=0, concat_axis=0, tiled=True
    ).reshape(TILES * SLOTS, 128)
    cells = sea_cell.reshape(TILES, SEND).T
    cells = cells ^ (mirror_x * (NY * (TROWS - 1)) + mirror_y * (NY - 1)) ^ (flip * (NY * TROWS // 2))
    hot = call(
        onehot_kernel,
        jax.ShapeDtypeStruct((TROWS * NY, SEA), jnp.bfloat16),
        [],
        [VMEM],
        cells,
    )
    received, hot = lax.optimization_barrier((received, hot))
    points, wind_here, partial = call(
        moments_kernel,
        (f32(SEND, ROWS, 128), f32(2 * SEND, 128), f32(GROUPS, 2 * SEND, 128)),
        [],
        [VMEM] * 2,
        received,
        table,
    )
    partial = lax.all_to_all(partial, "grp", split_axis=0, concat_axis=0, tiled=True)
    bf16 = functools.partial(jax.ShapeDtypeStruct, dtype=jnp.bfloat16)
    first, main, side, kept = call(
        place_kernel,
        (f32(4, LINES + PAD, 128), bf16((256, SEA)), bf16((256, SEA)), bf16((HALF, SEA))),
        [
            pltpu.VMEM((DEPTH, SEA), jnp.float32),
            pltpu.VMEM((HALF, SEA), jnp.bfloat16),
            pltpu.SemaphoreType.DMA((3,)),
        ],
        [VMEM] * 4 + [hbm],
        points,
        wind_here,
        partial,
        table,
        hot,
        limit=44,
    )
    second = call(
        place_rest_kernel,
        f32(4, LINES, 128),
        [],
        [VMEM] * 3,
        main,
        side,
        kept,
        us=2,
    )
    across, within = [], []
    for g in range(GROUPS):
        for i in range(TILES - 1):
            low, high = g * TILES + i, g * TILES + i + 1
            (across if i % 2 else within).extend([(low, high), (high, low)])
    got_first = lax.ppermute(first, ("grp", "comp"), across)
    got_second = lax.ppermute(second, ("grp", "comp"), within)
    once, done = call(
        inner_kernel,
        (f32(5, LINES, 128), f32(2, 3, 128, 128)),
        [pltpu.VMEM((2 * LINES, 128), jnp.float32), pltpu.VMEM((5, 2, 8, 128), jnp.float32)],
        [VMEM] * 3,
        courant,
        first,
        second,
        us=3,
    )
    near = call(
        near_kernel,
        f32(4, 3, 128, 128),
        [
            pltpu.VMEM((4, LINES, 128), jnp.float32),
            pltpu.VMEM((4 * LINES, 128), jnp.float32),
            pltpu.VMEM((4, 2, 8, 128), jnp.float32),
        ],
        [VMEM] * 5,
        courant,
        first,
        second,
        got_second,
        once,
        us=0,
    )
    return call(
        outer_kernel,
        f32(LOCAL, TROWS, NY),
        [
            pltpu.VMEM((4, LINES, 128), jnp.float32),
            pltpu.VMEM((4 * LINES, 128), jnp.float32),
            pltpu.VMEM((4, 2, 8, 128), jnp.float32),
            pltpu.VMEM((2, MAIN, TROWS, 128), jnp.float32),
            pltpu.VMEM((PACKS, 32 * TROWS, 128), jnp.float32),
            pltpu.VMEM((32, TROWS, NY), jnp.float32),
            pltpu.SemaphoreType.DMA((3,)),
        ],
        [VMEM] * 7,
        courant,
        first,
        second,
        got_first,
        once,
        done,
        near,
        outs=hbm,
    )


def solution(mesh):
    in_specs = (P("grp", "comp"), P("comp"), P("comp"), P("comp"))
    out_specs = P("grp", "comp", None)
    return jax.shard_map(local, mesh=mesh, in_specs=in_specs, out_specs=out_specs, check_vma=False)
```

```python
import functools
import math

import jax
import jax.numpy as jnp
import numpy as np
from jax import lax
from jax.experimental import pallas as pl
from jax.experimental.pallas import tpu as pltpu
from jax.sharding import PartitionSpec as P

DIRS = 24
FREQ = 25
TROWS = 8
NY = 256
SEA = 1536
SEND = 12
GROUPS = 4
TILES = 128
LOCAL = DIRS * FREQ // GROUPS
ROWS = 152
DEPTH = 160
MAIN = 128
EXTRA = ROWS - MAIN
PER_TILE = 5
SLOTS = 15
GRAV = 9.81
LOW_FREQ = 0.0418
FREQ_STEP = 1.1

VMEM = pl.BlockSpec(memory_space=pltpu.VMEM)

W_E, W_I, C_COS, C_SIN, C_OUT = range(5)
PHASES = 32
PACKS = 4
SHORT = PHASES // PACKS
LINES = (PHASES + SHORT) * 8
CHUNK = 16
PAD = 8
PARTS = 4
HALF = TROWS * NY // 2


def coefficient_tables():
    table = np.zeros((GROUPS, ROWS, 128), np.float64)
    courant = np.zeros((GROUPS, 8, 256), np.float64)
    for group in range(GROUPS):
        for row in range(LOCAL):
            d, j = row // FREQ + group * (DIRS // GROUPS), row % FREQ
            angle = 2.0 * math.pi * (d + 0.5) / DIRS
            freq = LOW_FREQ * FREQ_STEP**j
            s = 2.0 * math.pi * freq
            w = 2.0 * math.pi / DIRS * 0.1 * freq
            reach = 0.45 * (2.0 * math.pi * LOW_FREQ) / s
            ux, uy = abs(reach * math.cos(angle)), abs(reach * math.sin(angle))
            push = 0.1 * 28.0 * 0.035 * s / GRAV
            table[group, row, :5] = (
                w, w / s, push * math.cos(angle), push * math.sin(angle), 0.4 * s * s
            )
            if row < MAIN:
                lanes = [row]
            else:
                lanes = [128 + pack * 32 + row - MAIN for pack in range(PACKS)]
            for lane in lanes:
                courant[group, :4, lane] = (ux, ux * (1.0 - ux), uy, uy * (1.0 - uy))
    return table.astype(np.float32), courant.astype(np.float32)


def pack_kernel(x_hbm, speed_hbm, heading_hbm, out_hbm, x_ref, wind_ref, z_ref, b_ref, m_ref,
                sem_in, sem_wind, sem_out):
    width = SEA // PARTS
    tiles = TILES // PARTS
    ins = [
        pltpu.make_async_copy(x_hbm.at[:, pl.ds(c * width, width)], x_ref.at[c], sem_in.at[c])
        for c in range(PARTS)
    ]
    winds = [
        pltpu.make_async_copy(ref, wind_ref.at[i], sem_wind.at[i])
        for i, ref in enumerate((speed_hbm, heading_hbm))
    ]
    outs = [
        pltpu.make_async_copy(
            m_ref.at[pl.ds(c * tiles * SLOTS, tiles * SLOTS)],
            out_hbm.at[pl.ds(c * tiles * SLOTS, tiles * SLOTS)],
            sem_out.at[c],
        )
        for c in range(PARTS)
    ]
    ins[0].start()
    winds[0].start()
    winds[1].start()
    for c in range(1, PARTS):
        ins[c].start()
    b_ref[PER_TILE * EXTRA : 128, :] = jnp.zeros((128 - PER_TILE * EXTRA, width), jnp.float32)
    lane = lax.broadcasted_iota(jnp.int32, (tiles, 128), 1)
    for c in range(PARTS):
        if c == 0:
            winds[0].wait()
            winds[1].wait()
            speed, heading = wind_ref[0], wind_ref[1]
            wind_ref[0] = speed * jnp.cos(heading)
            wind_ref[1] = speed * jnp.sin(heading)
        ins[c].wait()
        for copy in range(PER_TILE):
            b_ref[copy * EXTRA : copy * EXTRA + LOCAL - MAIN, :] = x_ref[c, MAIN:LOCAL, :]
        for block in range(width // 128):
            cols = slice(block * 128, block * 128 + 128)
            at = c * (width // 128) + block
            for copy in range(PER_TILE):
                for i in range(2):
                    row = copy * EXTRA + LOCAL - MAIN + i
                    b_ref[row : row + 1, cols] = wind_ref[i, at : at + 1, :]
            z_ref[0, cols, :] = x_ref[c, 0:MAIN, cols].T
            z_ref[1, cols, :] = b_ref[:, cols].T
        first = c * tiles * SLOTS
        for k in range(SEND):
            m_ref[pl.ds(first + k, tiles, stride=SLOTS), :] = z_ref[
                0, pl.ds(k, tiles, stride=SEND), :
            ]
        for tile in range(SLOTS - SEND):
            total = None
            for k in range(tile * PER_TILE, min(SEND, (tile + 1) * PER_TILE)):
                piece = z_ref[1, pl.ds(k, tiles, stride=SEND), :]
                start = (k % PER_TILE) * EXTRA
                total = piece if total is None else jnp.where(lane < start, total, piece)
            m_ref[pl.ds(first + SEND + tile, tiles, stride=SLOTS), :] = total
        outs[c].start()
    for c in range(PARTS):
        outs[c].wait()


def moments_kernel(r_ref, tab_ref, y_ref, wind_ref, e_ref):
    extra = None
    we = jnp.broadcast_to(tab_ref[:, W_E : W_E + 1], (ROWS, 128))
    wi = jnp.broadcast_to(tab_ref[:, W_I : W_I + 1], (ROWS, 128))
    for k in range(SEND):
        if k % PER_TILE == 0:
            extra = r_ref[pl.ds(SEND + k // PER_TILE, TILES, stride=SLOTS), :].T
        part = extra[(k % PER_TILE) * EXTRA : (k % PER_TILE + 1) * EXTRA, :]
        main = r_ref[pl.ds(k, TILES, stride=SLOTS), :].T
        y_ref[k, 0:MAIN, :] = main
        y_ref[k, MAIN:ROWS, :] = part
        wind_ref[k : k + 1, :] = part[LOCAL - MAIN : LOCAL - MAIN + 1, :]
        wind_ref[SEND + k : SEND + k + 1, :] = part[LOCAL - MAIN + 1 : EXTRA, :]
        y = y_ref[k]
        energy = jnp.sum(y * we, axis=0, keepdims=True)
        inverse = jnp.sum(y * wi, axis=0, keepdims=True)
        for g in range(GROUPS):
            e_ref[g, k : k + 1, :] = energy
            e_ref[g, SEND + k : SEND + k + 1, :] = inverse


def onehot_kernel(cell_ref, out_ref):
    row = lax.broadcasted_iota(jnp.int32, (16, 128), 0)
    base = row % 8 * 32 + row // 8
    spots = [cell_ref[k : k + 1, :] - base for k in range(SEND)]

    def body(e, carry):
        for phase in range(0, PHASES, 2):
            pack, short = phase // SHORT, phase % SHORT
            line = ((e // 4 * PACKS + pack) * 4 + e % 4) * SHORT * 8 + short * 8
            for k in range(SEND):
                hit = spots[k] == e * NY + phase
                out_ref[pl.ds(pl.multiple_of(line, 16), 16), k * 128 : (k + 1) * 128] = jnp.where(
                    hit, 1.0, 0.0
                ).astype(jnp.bfloat16)
        return carry

    lax.fori_loop(0, TROWS, body, 0)


def spread(held_ref, main, side, ref, packs):
    turned = (((1,), (1,)), ((), ()))
    block = SHORT * 8
    hot = held_ref[packs[0] * 4 * block : (packs[-1] + 1) * 4 * block, :]
    out = lax.dot_general(hot, main, turned, preferred_element_type=jnp.float32)
    out = out[:, 0:128] + out[:, 128:256]
    rest = lax.dot_general(hot, side, turned, preferred_element_type=jnp.float32)
    rest = rest[:, 0:128] + rest[:, 128:256]
    lane = lax.broadcasted_iota(jnp.int32, (block, 128), 1)
    for i in range(4):
        total = ref[i, PHASES * 8 : LINES, :] if packs[0] else None
        for pack in packs:
            line = ((pack - packs[0]) * 4 + i) * block
            ref[i, pack * block : (pack + 1) * block, :] = out[line : line + block]
            part = rest[line : line + block]
            total = part if total is None else jnp.where(lane < pack * 32, total, part)
        ref[i, PHASES * 8 : LINES, :] = total


def place_kernel(y_ref, wind_ref, e_ref, tab_ref, hot_ref, first_ref, main_ref, side_ref,
                 kept_ref, s_ref, held_ref, sem):
    quarter = HALF // 2
    copies = [
        pltpu.make_async_copy(
            hot_ref.at[pl.ds(h * quarter, quarter)],
            held_ref.at[pl.ds(h * quarter, quarter)],
            sem.at[h],
        )
        for h in range(2)
    ]
    copies.append(pltpu.make_async_copy(hot_ref.at[pl.ds(HALF, HALF)], kept_ref, sem.at[2]))
    copies[0].start()
    copies[1].start()
    moments = e_ref[0] + e_ref[1] + e_ref[2] + e_ref[3]
    energy, inverse = moments[0:SEND], moments[SEND : 2 * SEND]
    mean = energy / inverse
    wavenumber = mean * mean / GRAV
    steepness = energy * wavenumber * wavenumber
    ratio = steepness / (steepness + 0.02)
    decay = ratio / (mean * mean)
    along, across = wind_ref[0:SEND, :], wind_ref[SEND : 2 * SEND, :]
    ccos = jnp.broadcast_to(tab_ref[:, C_COS : C_COS + 1], (ROWS, 128))
    csin = jnp.broadcast_to(tab_ref[:, C_SIN : C_SIN + 1], (ROWS, 128))
    cout = jnp.broadcast_to(tab_ref[:, C_OUT : C_OUT + 1], (ROWS, 128))
    row = lax.broadcasted_iota(jnp.int32, (ROWS, 128), 0)
    s_ref[ROWS:DEPTH, :] = jnp.zeros((DEPTH - ROWS, SEA), jnp.float32)
    for k in range(SEND):
        grow = ccos * along[k : k + 1] + csin * across[k : k + 1]
        rate = jnp.maximum(grow - 0.1, 0.0) - cout * decay[k : k + 1]
        value = y_ref[k] * jnp.exp(rate)
        value = jnp.where(row < LOCAL, value, 0.0)
        s_ref[0:ROWS, k * 128 : (k + 1) * 128] = value
    value = s_ref[...]
    high = value.astype(jnp.bfloat16)
    rest = (value - high.astype(jnp.float32)).astype(jnp.bfloat16)
    main_ref[0:MAIN, :] = high[0:MAIN]
    main_ref[MAIN:256, :] = rest[0:MAIN]
    for pack in range(PACKS):
        side_ref[pack * 32 : pack * 32 + 32, :] = high[MAIN:DEPTH]
        side_ref[128 + pack * 32 : 128 + pack * 32 + 32, :] = rest[MAIN:DEPTH]
    first_ref[:, LINES : LINES + PAD, :] = jnp.zeros((4, PAD, 128), jnp.float32)
    copies[0].wait()
    copies[2].start()
    spread(held_ref, main_ref[...], side_ref[...], first_ref, (0, 1))
    copies[1].wait()
    spread(held_ref, main_ref[...], side_ref[...], first_ref, (2, 3))
    copies[2].wait()


def place_rest_kernel(main_ref, side_ref, kept_ref, second_ref):
    spread(kept_ref, main_ref[...], side_ref[...], second_ref, (0, 1, 2, 3))


def limited(a, b):
    m = (a + (b + b)) * (1.0 / 6.0)
    least = jnp.minimum(jnp.maximum(a, b), 0.0)
    most = jnp.maximum(jnp.minimum(a, b), 0.0)
    return jnp.minimum(jnp.maximum(m, least), most)


def next_main(x):
    return pltpu.roll(x, 7, 0)


def last_main(x):
    return pltpu.roll(x, 1, 0)


def next_side(x):
    lane = lax.broadcasted_iota(jnp.int32, (8, 128), 1)
    x = pltpu.roll(x, 96, 1)
    return jnp.where(lane >= 96, pltpu.roll(x, 7, 0), x)


def last_side(x):
    lane = lax.broadcasted_iota(jnp.int32, (8, 128), 1)
    x = pltpu.roll(x, 32, 1)
    return jnp.where(lane < 32, pltpu.roll(x, 1, 0), x)


def substep(rows, seas, put, keep_ref, coef, base, phases, after, before):
    ux, kx, uy, ky = coef
    count = len(rows) - 3
    width = min(CHUNK, phases)

    def load(spot, phase):
        ref, at = spot
        return ref[at, pl.ds(pl.multiple_of(base + phase * 8, 8), 8), :]

    for i in range(count):
        spot = rows[i + 2]
        end = load(spot, phases - 1)
        ahead = load(spot, 0) - before(end)
        prior = before(end - load(spot, phases - 2))
        keep_ref[i, 0] = ahead
        keep_ref[i, 1] = uy * before(end) + ky * limited(prior, ahead)

    def body(chunk, carry):
        first = chunk * width
        following = jnp.where(first + width == phases, 0, first + width)
        wraps = first + width == phases
        q = [load(rows[1], first + j) for j in range(width)]
        diff = [q[j] - load(rows[0], first + j) for j in range(width)]
        flux = None
        for i in range(-1, count):
            up = [load(rows[i + 3], first + j) for j in range(width)]
            slope = [up[j] - q[j] for j in range(width)]
            gone = [ux * q[j] + kx * limited(diff[j], slope[j]) for j in range(width)]
            if i >= 0:
                behind, past = keep_ref[i, 0], keep_ref[i, 1]
                edge = load(rows[i + 2], following)
                edge = jnp.where(wraps, after(edge), edge)
                for j in range(width):
                    ahead = (q[j + 1] if j + 1 < width else edge) - q[j]
                    side = uy * q[j] + ky * limited(behind, ahead)
                    new = q[j] - ((gone[j] - flux[j]) + (side - past))
                    sea = q[j] if seas is None else load(seas[i], first + j)
                    put(i, first + j, jnp.where(sea > 0.0, new, 0.0))
                    behind, past = ahead, side
                keep_ref[i, 0] = behind
                keep_ref[i, 1] = past
            q, diff, flux = up, slope, gone
        return carry

    lax.fori_loop(0, phases // width, body, 0)


def flags():
    group = lax.axis_index("grp")
    mirror_x = ((group == 1) | (group == 2)).astype(jnp.int32)
    mirror_y = (group >= 2).astype(jnp.int32)
    odd = lax.axis_index("comp").astype(jnp.int32) % 2
    return mirror_x, mirror_y, odd ^ mirror_x


def halves(tab_ref):
    for base, phases, lanes, after, before in (
        (0, PHASES, 0, next_main, last_main),
        (PHASES * 8, SHORT, 128, next_side, last_side),
    ):
        coef = [
            jnp.broadcast_to(tab_ref[n : n + 1, lanes : lanes + 128], (8, 128)) for n in range(4)
        ]
        yield coef, base, phases, after, before


def writer(ref, base, offset):
    def put(i, phase, value):
        ref[i + offset, pl.ds(pl.multiple_of(base + phase * 8, 8), 8), :] = value

    return put


def last_writer(ref, base, offset, cols_back):
    def put(i, phase, value):
        if base == 0:
            phase = phase + (PHASES - 1 - 2 * phase) * cols_back
        line = (i + offset) * LINES + base + phase * 8
        ref[pl.ds(pl.multiple_of(line, 8), 8), :] = value

    return put


def field(flip, first_ref, second_ref):
    parts = (second_ref, first_ref) if flip else (first_ref, second_ref)
    return [(ref, i) for ref in parts for i in range(4)]


def turned_main(ref, at, half, cols_back):
    parts = []
    for s in range(half * 4, half * 4 + 4):
        start = at * LINES + s + (7 - 2 * s) * cols_back
        parts.append(ref[pl.ds(start, PHASES, stride=8), :])
    return jnp.concatenate(parts, axis=0).T


def turned_side(ref, at):
    line = at * LINES + PHASES * 8
    empty = jnp.zeros((128 - SHORT * 8, 128), jnp.float32)
    return jnp.concatenate([ref[line : line + SHORT * 8, :], empty], axis=0).T


def inner_kernel(tab_ref, first_ref, second_ref, once_ref, done_ref, twice_ref, keep_ref):
    once = [(once_ref, i) for i in range(5)]
    _, cols_back, side_up = flags()
    for flip in range(2):

        @pl.when(side_up == flip)
        def _():
            cells = field(flip, first_ref, second_ref)
            for half in halves(tab_ref):
                base = half[1]
                substep(cells, None, writer(once_ref, base, 0), keep_ref, *half)
                put = last_writer(twice_ref, base, 0, cols_back)
                substep(once, cells[4:6], put, keep_ref, *half)

    for i in range(2):
        done_ref[i, 0] = turned_main(twice_ref, i, 0, cols_back)
        done_ref[i, 1] = turned_main(twice_ref, i, 1, cols_back)
        done_ref[i, 2] = turned_side(twice_ref, i)


def edge(lower, cells, got_ref, inner_ref, once_ref, twice_ref, keep_ref, cols_back, half):
    base = half[1]
    once = [(inner_ref, i) for i in range(5)]
    if lower:
        near = [(got_ref, i) for i in range(4)] + cells[0:3]
        seas, fresh = cells[0:4], [(once_ref, i) for i in range(4)]
        once = fresh + once[0:3]
    else:
        near = cells[5:8] + [(got_ref, i) for i in range(2)]
        seas, fresh = cells[6:8], [(once_ref, i) for i in range(2)]
        once = once[2:5] + fresh
    substep(near, None, writer(once_ref, base, 0), keep_ref, *half)
    substep(once, seas, last_writer(twice_ref, base, 0, cols_back), keep_ref, *half)
    return len(seas)


def near_kernel(tab_ref, first_ref, second_ref, got_ref, inner_ref, done_ref, once_ref,
                twice_ref, keep_ref):
    _, cols_back, side_up = flags()
    for flip in range(2):

        @pl.when(side_up == flip)
        def _():
            cells = field(flip, first_ref, second_ref)
            for half in halves(tab_ref):
                count = edge(flip == 1, cells, got_ref, inner_ref, once_ref, twice_ref, keep_ref,
                             cols_back, half)
            for i in range(count):
                done_ref[i, 0] = turned_main(twice_ref, i, 0, cols_back)
                done_ref[i, 1] = turned_main(twice_ref, i, 1, cols_back)
                done_ref[i, 2] = turned_side(twice_ref, i)


def outer_kernel(tab_ref, first_ref, second_ref, got_ref, inner_ref, done_ref, near_ref,
                 out_hbm, once_ref, twice_ref, keep_ref, turn_ref, rest_ref, last_ref, sem):
    rows_back, cols_back, side_up = flags()

    def blocks(flip, part):
        for e in range(TROWS):
            r = e + (TROWS - 1 - 2 * e) * rows_back
            if e in (4, 5):
                yield r, done_ref[e - 4, part]
                continue
            lower, at = e < 4, e if e < 4 else e - 6
            if lower == (flip == 1):
                yield r, near_ref[at, part]
            elif part == 2:
                yield r, turned_side(twice_ref, at)
            else:
                yield r, turned_main(twice_ref, at, part, cols_back)

    def compute(flip, half):
        cells = field(flip, first_ref, second_ref)
        edge(flip == 0, cells, got_ref, inner_ref, once_ref, twice_ref, keep_ref, cols_back, half)

    main, side = halves(tab_ref)
    copies = [
        pltpu.make_async_copy(
            turn_ref.at[half],
            out_hbm.at[pl.ds(0, MAIN), :, pl.ds(half * 128, 128)],
            sem.at[half],
        )
        for half in range(2)
    ]
    count = LOCAL - MAIN
    copies.append(
        pltpu.make_async_copy(
            last_ref.at[pl.ds(0, count)], out_hbm.at[pl.ds(MAIN, count)], sem.at[2]
        )
    )
    for flip in range(2):

        @pl.when(side_up == flip)
        def _():
            compute(flip, side)
            for r, block in blocks(flip, 2):
                for pack in range(PACKS):
                    rest_ref[pack, pl.ds(r, 32, stride=TROWS), :] = block[
                        pack * 32 : pack * 32 + 32
                    ]

    spot = lax.broadcasted_iota(jnp.int32, (PACKS * 128, NY), 0)
    col = lax.broadcasted_iota(jnp.int32, (PACKS * 128, NY), 1)
    col = col + (NY - 1 - 2 * col) * cols_back
    pack, inner = spot // 128, spot % 128
    wanted = inner % 8 * 32 + pack * SHORT + inner // 8
    order = jnp.where((wanted == col) & (inner < SHORT * 8), 1.0, 0.0).astype(jnp.bfloat16)
    value = jnp.concatenate([rest_ref[pack] for pack in range(PACKS)], axis=1)
    high = value.astype(jnp.bfloat16)
    rest = (value - high.astype(jnp.float32)).astype(jnp.bfloat16)
    value = jnp.dot(high, order, preferred_element_type=jnp.float32)
    value = value + jnp.dot(rest, order, preferred_element_type=jnp.float32)
    for i in range(count):
        last_ref[i] = value[i * TROWS : (i + 1) * TROWS, :]
    copies[2].start()
    for flip in range(2):

        @pl.when(side_up == flip)
        def _():
            compute(flip, main)

    for half in range(2):
        lines = turn_ref.at[half].reshape(MAIN * TROWS, 128)
        for flip in range(2):

            @pl.when(side_up == flip)
            def _():
                for r, block in blocks(flip, half):
                    lines[pl.ds(r, MAIN, stride=TROWS), :] = block

        copies[half].start()
    for copy in copies:
        copy.wait()


def call(kernel, shapes, scratch, ins, *args, limit=20, us=0, outs=None):
    cost = pl.CostEstimate(flops=us * 10**9, bytes_accessed=us * 3 * 10**6, transcendentals=0)
    return pl.pallas_call(
        kernel,
        out_shape=shapes,
        in_specs=ins,
        out_specs=outs or jax.tree.map(lambda _: VMEM, shapes),
        scratch_shapes=scratch,
        cost_estimate=cost if us else None,
        compiler_params=pltpu.CompilerParams(vmem_limit_bytes=limit * 1024 * 1024),
    )(*args)


def f32(*shape):
    return jax.ShapeDtypeStruct(shape, jnp.float32)


def local(spectra, wind_speed, wind_dir, sea_cell):
    group = lax.axis_index("grp")
    table, courant = (
        lax.dynamic_index_in_dim(jnp.asarray(t), group, 0, keepdims=False)
        for t in coefficient_tables()
    )
    mirror_x, mirror_y, flip = flags()
    hbm = pl.BlockSpec(memory_space=pltpu.HBM)
    packed = call(
        pack_kernel,
        f32(TILES * SLOTS, 128),
        [
            pltpu.VMEM((PARTS, LOCAL, SEA // PARTS), jnp.float32),
            pltpu.VMEM((2, SEA // 128, 128), jnp.float32),
            pltpu.VMEM((2, SEA // PARTS, 128), jnp.float32),
            pltpu.VMEM((128, SEA // PARTS), jnp.float32),
            pltpu.VMEM((TILES * SLOTS, 128), jnp.float32),
            pltpu.SemaphoreType.DMA((PARTS,)),
            pltpu.SemaphoreType.DMA((2,)),
            pltpu.SemaphoreType.DMA((PARTS,)),
        ],
        [hbm] * 3,
        spectra,
        wind_speed.reshape(SEA // 128, 128),
        wind_dir.reshape(SEA // 128, 128),
        limit=57,
        outs=hbm,
    )
    received = lax.all_to_all(
        packed.reshape(TILES, 1, SLOTS * 128), "comp", split_axis=0, concat_axis=0, tiled=True
    ).reshape(TILES * SLOTS, 128)
    cells = sea_cell.reshape(TILES, SEND).T
    cells = cells ^ (mirror_x * (NY * (TROWS - 1)) + mirror_y * (NY - 1)) ^ (flip * (NY * TROWS // 2))
    hot = call(
        onehot_kernel,
        jax.ShapeDtypeStruct((TROWS * NY, SEA), jnp.bfloat16),
        [],
        [VMEM],
        cells,
    )
    received, hot = lax.optimization_barrier((received, hot))
    points, wind_here, partial = call(
        moments_kernel,
        (f32(SEND, ROWS, 128), f32(2 * SEND, 128), f32(GROUPS, 2 * SEND, 128)),
        [],
        [VMEM] * 2,
        received,
        table,
    )
    partial = lax.all_to_all(partial, "grp", split_axis=0, concat_axis=0, tiled=True)
    bf16 = functools.partial(jax.ShapeDtypeStruct, dtype=jnp.bfloat16)
    first, main, side, kept = call(
        place_kernel,
        (f32(4, LINES + PAD, 128), bf16((256, SEA)), bf16((256, SEA)), bf16((HALF, SEA))),
        [
            pltpu.VMEM((DEPTH, SEA), jnp.float32),
            pltpu.VMEM((HALF, SEA), jnp.bfloat16),
            pltpu.SemaphoreType.DMA((3,)),
        ],
        [VMEM] * 4 + [hbm],
        points,
        wind_here,
        partial,
        table,
        hot,
        limit=44,
    )
    second = call(
        place_rest_kernel,
        f32(4, LINES, 128),
        [],
        [VMEM] * 3,
        main,
        side,
        kept,
        us=2,
    )
    across, within = [], []
    for g in range(GROUPS):
        for i in range(TILES - 1):
            low, high = g * TILES + i, g * TILES + i + 1
            (across if i % 2 else within).extend([(low, high), (high, low)])
    got_first = lax.ppermute(first, ("grp", "comp"), across)
    got_second = lax.ppermute(second, ("grp", "comp"), within)
    once, done = call(
        inner_kernel,
        (f32(5, LINES, 128), f32(2, 3, 128, 128)),
        [pltpu.VMEM((2 * LINES, 128), jnp.float32), pltpu.VMEM((5, 2, 8, 128), jnp.float32)],
        [VMEM] * 3,
        courant,
        first,
        second,
        us=3,
    )
    near = call(
        near_kernel,
        f32(4, 3, 128, 128),
        [
            pltpu.VMEM((4, LINES, 128), jnp.float32),
            pltpu.VMEM((4 * LINES, 128), jnp.float32),
            pltpu.VMEM((4, 2, 8, 128), jnp.float32),
        ],
        [VMEM] * 5,
        courant,
        first,
        second,
        got_second,
        once,
        us=0,
    )
    return call(
        outer_kernel,
        f32(LOCAL, TROWS, NY),
        [
            pltpu.VMEM((4, LINES, 128), jnp.float32),
            pltpu.VMEM((4 * LINES, 128), jnp.float32),
            pltpu.VMEM((4, 2, 8, 128), jnp.float32),
            pltpu.VMEM((2, MAIN, TROWS, 128), jnp.float32),
            pltpu.VMEM((PACKS, 32 * TROWS, 128), jnp.float32),
            pltpu.VMEM((32, TROWS, NY), jnp.float32),
            pltpu.SemaphoreType.DMA((3,)),
        ],
        [VMEM] * 7,
        courant,
        first,
        second,
        got_first,
        once,
        done,
        near,
        outs=hbm,
    )


def solution(mesh):
    in_specs = (P("grp", "comp"), P("comp"), P("comp"), P("comp"))
    out_specs = P("grp", "comp", None)
    return jax.shard_map(local, mesh=mesh, in_specs=in_specs, out_specs=out_specs, check_vma=False)
```
